32 devices in a mesh: dp: 8 (over z, x), tensor: 4 (over y, core).
Axes of the slice: x: 2, y: 2, z: 4, core: 2. Of those that a mesh axis runs over, the one named last changes fastest.
Arguments:
- tokens: bfloat16 [32768, 256], P('dp'), may hold values from -6 to 6
- positions: bfloat16 [32768, 256], P('dp'), may hold values from -1 to 1
- segment_ids: int32 [8, 4096], P('dp'), may hold values from 0 to 4, as said below
- pad_flags: int32 [8, 4096], P('dp'), may hold values from 0 to 1, as said below
- cotangent: bfloat16 [32768, 256], P('dp'), may hold values from -6 to 6
- inward: float32 [3, 256, 256], P(None, 'dp', 'tensor'), may hold values from -0.375 to 0.375
- outward: float32 [256, 256], P('tensor', 'dp'), may hold values from -1 to 1
- upward: float32 [256, 2048], P('dp', 'tensor'), may hold values from -0.375 to 0.375
- downward: float32 [2048, 256], P('tensor', 'dp'), may hold values from -0.1875 to 0.1875
- vectors: float32 [6, 256], P(None, 'dp')
- offsets: float32 [2, 256], P(None, ('tensor', 'dp')), may hold values from -4 to 4
- shifts: float32 [2048], P(('tensor', 'dp')), may hold values from -4 to 4
- first_inward: float32 [3, 256, 256], P(None, 'dp', 'tensor'), may hold values from -1536 to 1536
- first_outward: float32 [256, 256], P('tensor', 'dp'), may hold values from -224 to 224
- first_upward: float32 [256, 2048], P('dp', 'tensor'), may hold values from -224 to 224
- first_downward: float32 [2048, 256], P('tensor', 'dp'), may hold values from -512 to 512
- first_vectors: float32 [6, 256], P(None, 'dp'), may hold values from -768 to 768
- first_offsets: float32 [2, 256], P(None, ('tensor', 'dp')), may hold values from -1536 to 1536
- first_shifts: float32 [2048], P(('tensor', 'dp')), may hold values from -224 to 224
- second_inward: float32 [3, 256, 256], P(None, 'dp', 'tensor'), may hold values from 73728 to 294912
- second_outward: float32 [256, 256], P('tensor', 'dp'), may hold values from 1310.72 to 5242.88
- second_upward: float32 [256, 2048], P('dp', 'tensor'), may hold values from 1310.72 to 5242.88
- second_downward: float32 [2048, 256], P('tensor', 'dp'), may hold values from 6553.6 to 26214.4
- second_vectors: float32 [6, 256], P(None, 'dp'), may hold values from 16384 to 65536
- second_offsets: float32 [2, 256], P(None, ('tensor', 'dp')), may hold values from 73728 to 294912
- second_shifts: float32 [2048], P(('tensor', 'dp')), may hold values from 1310.72 to 5242.88
Outputs:
- encoded: bfloat16 [32768, 256], P('dp')
- token_grad: float32 [32768, 256], P('dp')
- grad_inward: float32 [3, 256, 256], P(None, 'dp', 'tensor')
- grad_outward: float32 [256, 256], P('tensor', 'dp')
- grad_upward: float32 [256, 2048], P('dp', 'tensor')
- grad_downward: float32 [2048, 256], P('tensor', 'dp')
- grad_vectors: float32 [6, 256], P(None, 'dp')
- grad_offsets: float32 [2, 256], P(None, ('tensor', 'dp'))
- grad_shifts: float32 [2048], P(('tensor', 'dp'))
- updated_inward: float32 [3, 256, 256], P(None, 'dp', 'tensor')
- updated_outward: float32 [256, 256], P('tensor', 'dp')
- updated_upward: float32 [256, 2048], P('dp', 'tensor')
- updated_downward: float32 [2048, 256], P('tensor', 'dp')
- updated_vectors: float32 [6, 256], P(None, 'dp')
- updated_offsets: float32 [2, 256], P(None, ('tensor', 'dp'))
- updated_shifts: float32 [2048], P(('tensor', 'dp'))
- lowered_inward: bfloat16 [3, 256, 256], P(None, 'dp', 'tensor')
- lowered_outward: bfloat16 [256, 256], P('tensor', 'dp')
- lowered_upward: bfloat16 [256, 2048], P('dp', 'tensor')
- lowered_downward: bfloat16 [2048, 256], P('tensor', 'dp')
- momentum_inward: float32 [3, 256, 256], P(None, 'dp', 'tensor')
- momentum_outward: float32 [256, 256], P('tensor', 'dp')
- momentum_upward: float32 [256, 2048], P('dp', 'tensor')
- momentum_downward: float32 [2048, 256], P('tensor', 'dp')
- momentum_vectors: float32 [6, 256], P(None, 'dp')
- momentum_offsets: float32 [2, 256], P(None, ('tensor', 'dp'))
- momentum_shifts: float32 [2048], P(('tensor', 'dp'))
- variance_inward: float32 [3, 256, 256], P(None, 'dp', 'tensor')
- variance_outward: float32 [256, 256], P('tensor', 'dp')
- variance_upward: float32 [256, 2048], P('dp', 'tensor')
- variance_downward: float32 [2048, 256], P('tensor', 'dp')
- variance_vectors: float32 [6, 256], P(None, 'dp')
- variance_offsets: float32 [2, 256], P(None, ('tensor', 'dp'))
- variance_shifts: float32 [2048], P(('tensor', 'dp'))
The draws below stay inside these ranges and needn't reach their ends.
Inputs may be any that keep to these rules, and one draw needn't show every extreme that they name: `segment_ids`: in every pack the ids never fall and every id from 0 to 4 occurs. `pad_flags`: the first token of every image is never padding.
All inputs are finite; a program needn't handle non-finite values.
Results may differ from the reference program's by a relative error of at most 0.008.
The reference program's roundings to bfloat16 on the way count: a program that leaves them out, or rounds other values in their place, can miss the bound.
Values may be sent and summed in bfloat16 or wider, within the bound.
A program may use at most 128 MiB of HBM per device.

```python
import math
import jax
import jax.numpy as jnp
from jax import lax

D = 256
HEADS = 8
HEAD_DIM = 32
FF = 2048
PACK = 4096
IMAGES = 5
STEP = 10
PACKS = 8
TOKENS = 32768


def layout_draw(key):
    cut_key = jax.random.fold_in(key, 21)
    pad_key = jax.random.fold_in(key, 22)
    pack_keys = jax.random.split(cut_key, PACKS)

    def pack_cuts(pack_key):
        return jax.random.permutation(pack_key, PACK - 1)[:IMAGES - 1] + 1
    cut_points = jax.vmap(pack_cuts)(pack_keys)
    position = jnp.arange(PACK, dtype=jnp.int32)
    segment = jnp.sum((cut_points[:, :, None] <= position[None, None, :]).astype(jnp.int32), axis=1)
    starts = jnp.concatenate([jnp.ones((PACKS, 1), dtype=jnp.bool_), segment[:, 1:] != segment[:, :-1]], axis=1)
    coin_toss = jax.random.randint(pad_key, (PACKS, PACK), 0, 4)
    padding = ((coin_toss == 0) & jnp.logical_not(starts)).astype(jnp.int32)
    return (segment.astype(jnp.int32), padding)


def draw_segment_ids(key, part):
    return layout_draw(key)[0]


def draw_pad_flags(key, part):
    return layout_draw(key)[1]


def draw_vectors(key, part):
    gain_key = jax.random.fold_in(key, 11)
    shift_key = jax.random.fold_in(key, 12)
    gain_part = 1.0 + 0.2 * jax.random.uniform(gain_key, (6, D), jnp.float32, -1.0, 1.0)
    shift_part = 0.3 * jax.random.normal(shift_key, (6, D), jnp.float32)
    row_index = jnp.arange(6)[:, None]
    is_gain = (row_index == 0) | (row_index == 2)
    return jnp.where(is_gain, gain_part, shift_part).astype(jnp.float32)


def with_spikes(drawn, stream_key, source, target, parts, factor):
    owner, partner = [(jnp.arange(drawn.shape[dim]) // (drawn.shape[dim] // parts)).reshape([-1 if axis == dim else 1 for axis in range(drawn.ndim)]) for dim in (source, target)]
    chosen = jax.random.permutation(stream_key, parts)[partner]
    strong = (owner == chosen) | (owner == (partner + parts // 2) % parts)
    return jnp.where(strong, factor * drawn, drawn)


def block_levels(stream_key, dims, cuts, smallest, high):
    def one(dim, shards_of):
        draws = jax.random.uniform(jax.random.fold_in(jax.random.fold_in(stream_key, 6), dim), (shards_of,), jnp.float32, smallest / len(cuts), high / len(cuts))
        return jnp.repeat(jnp.exp(draws), dims[dim] // shards_of).reshape((-1,) + (1,) * (len(dims) - dim - 1))

    level = one(*cuts[0])
    for cut in cuts[1:]:
        level = level * one(*cut)
    return level


def scatter_about(own_key, extent, width, limit, cuts=(), kind=jnp.bfloat16):
    level = block_levels(own_key, extent, cuts, -0.22, 0.18) if cuts else 1.0
    values = jax.random.normal(own_key, extent, jnp.float32) * width * level
    return jnp.minimum(jnp.maximum(values, -limit), limit).astype(kind)


def noise_with(rng, shape, width, most, cuts, heavy, kind=jnp.bfloat16):
    values = width * jax.random.normal(rng, shape, jnp.float32)
    if cuts:
        values = values * block_levels(rng, shape, cuts, -0.22, 0.18)
    return jnp.clip(with_spikes(values, jax.random.fold_in(rng, 3), *heavy), -most, most).astype(kind)


def setup_inputs(seed: int = 0) -> dict:
    seeds = jax.random.split(jax.random.key(seed), 27)
    tokens = scatter_about(seeds[0], (TOKENS, D), 1.0, 6.0, ((0, 8),))
    positions = jnp.clip(jax.random.uniform(seeds[1], (TOKENS, D), jnp.float32, -1.0, 1.0) * block_levels(seeds[1], (TOKENS, D), ((0, 8),), -0.4, 0.0), -1.0, 1.0).astype(jnp.bfloat16)
    segment_ids = draw_segment_ids(jax.random.fold_in(seeds[26], 71), 0)
    pad_flags = draw_pad_flags(jax.random.fold_in(seeds[26], 71), 0)
    cotangent = noise_with(seeds[4], (TOKENS, D), 1.0, 6.0, ((0, 8),), (0, 1, 8, 2.0))
    inward = scatter_about(seeds[5], (3, D, D), D ** -0.5, 0.375, ((1, 8), (2, 4)), jnp.float32)
    outward = scatter_about(seeds[6], (D, D), (D // 8) ** -0.5, 1.0, ((0, 4), (1, 8)), jnp.float32)
    upward = scatter_about(seeds[7], (D, FF), D ** -0.5, 0.375, ((0, 8), (1, 4)), jnp.float32)
    downward = scatter_about(seeds[8], (FF, D), (FF // 2) ** -0.5, 0.1875, ((0, 4), (1, 8)), jnp.float32)
    vectors = draw_vectors(jax.random.fold_in(seeds[26], 71), 0)
    offsets = scatter_about(seeds[10], (2, D), 0.3, 4.0, ((1, 32),), jnp.float32)
    shifts = scatter_about(seeds[11], (FF,), 0.3, 4.0, ((0, 32),), jnp.float32)
    first_inward = scatter_about(seeds[12], (3, D, D), (1.5 * TOKENS ** 0.5), 1536.0, ((1, 8), (2, 4)), jnp.float32)
    first_outward = scatter_about(seeds[13], (D, D), (0.2 * TOKENS ** 0.5), 224.0, ((0, 4), (1, 8)), jnp.float32)
    first_upward = scatter_about(seeds[14], (D, FF), (0.2 * TOKENS ** 0.5), 224.0, ((0, 8), (1, 4)), jnp.float32)
    first_downward = scatter_about(seeds[15], (FF, D), (0.45 * TOKENS ** 0.5), 512.0, ((0, 4), (1, 8)), jnp.float32)
    first_vectors = scatter_about(seeds[16], (6, D), (0.7 * TOKENS ** 0.5), 768.0, ((1, 8),), jnp.float32)
    first_offsets = scatter_about(seeds[17], (2, D), (1.5 * TOKENS ** 0.5), 1536.0, ((1, 32),), jnp.float32)
    first_shifts = scatter_about(seeds[18], (FF,), (0.2 * TOKENS ** 0.5), 224.0, ((0, 32),), jnp.float32)
    second_inward = jnp.clip(jnp.exp(math.log(294912.0) - 1.3862944 * jax.random.uniform(seeds[19], (3, D, D), jnp.float32) ** block_levels(seeds[19], (3, D, D), ((1, 8), (2, 4)), -0.2, 0.2)), 73728.0, 294912.0)
    second_outward = jnp.clip(jnp.exp(math.log(5242.88) - 1.3862944 * jax.random.uniform(seeds[20], (D, D), jnp.float32) ** block_levels(seeds[20], (D, D), ((0, 4), (1, 8)), -0.2, 0.2)), 1310.72, 5242.88)
    second_upward = jnp.clip(jnp.exp(math.log(5242.88) - 1.3862944 * jax.random.uniform(seeds[21], (D, FF), jnp.float32) ** block_levels(seeds[21], (D, FF), ((0, 8), (1, 4)), -0.2, 0.2)), 1310.72, 5242.88)
    second_downward = jnp.clip(jnp.exp(math.log(26214.4) - 1.3862944 * jax.random.uniform(seeds[22], (FF, D), jnp.float32) ** block_levels(seeds[22], (FF, D), ((0, 4), (1, 8)), -0.2, 0.2)), 6553.6, 26214.4)
    second_vectors = jnp.clip(jnp.exp(math.log(65536.0) - 1.3862944 * jax.random.uniform(seeds[23], (6, D), jnp.float32) ** block_levels(seeds[23], (6, D), ((1, 8),), -0.2, 0.2)), 16384.0, 65536.0)
    second_offsets = jnp.clip(jnp.exp(math.log(294912.0) - 1.3862944 * jax.random.uniform(seeds[24], (2, D), jnp.float32) ** block_levels(seeds[24], (2, D), ((1, 32),), -0.2, 0.2)), 73728.0, 294912.0)
    second_shifts = jnp.clip(jnp.exp(math.log(5242.88) - 1.3862944 * jax.random.uniform(seeds[25], (FF,), jnp.float32) ** block_levels(seeds[25], (FF,), ((0, 32),), -0.2, 0.2)), 1310.72, 5242.88)
    return dict(tokens=tokens, positions=positions, segment_ids=segment_ids, pad_flags=pad_flags, cotangent=cotangent, inward=inward, outward=outward, upward=upward, downward=downward, vectors=vectors, offsets=offsets, shifts=shifts, first_inward=first_inward, first_outward=first_outward, first_upward=first_upward, first_downward=first_downward, first_vectors=first_vectors, first_offsets=first_offsets, first_shifts=first_shifts, second_inward=second_inward, second_outward=second_outward, second_upward=second_upward, second_downward=second_downward, second_vectors=second_vectors, second_offsets=second_offsets, second_shifts=second_shifts)


@jax.custom_vjp
def low(v):
    return lax.optimization_barrier(v.astype(jnp.bfloat16)).astype(jnp.float32)

@jax.custom_vjp
def low_back(v):
    return v

def low_keep(v):
    return (low(v), None)

def low_pass(kept, grad):
    return (grad,)

def back_keep(v):
    return (v, None)

def back_low(kept, grad):
    return (low(grad),)
low.defvjp(low_keep, low_pass)
low_back.defvjp(back_keep, back_low)
neg_fill = -1e+30
norm_eps = 1e-05
beta_one = 0.5
beta_two = 0.5
adam_eps = 1e-08
decay_rate = 0.0001
step_rates = (0.06, 0.15, 0.06, 0.03, 0.1, 0.1, 0.1)
block_limit = 512

def product(left_side, right_side):
    return jnp.dot(left_side, right_side, precision=lax.Precision.HIGHEST, preferred_element_type=jnp.float32)

def smooth_unit(values):
    return jax.nn.gelu(values, approximate=False)

def layer_norm(values, gain_row, shift_row):
    center = values - lax.optimization_barrier(jnp.mean(values, axis=-1, keepdims=True))
    inverse = lax.rsqrt(lax.optimization_barrier(jnp.mean(center * center, axis=-1, keepdims=True)) + norm_eps)
    return center * inverse * gain_row + shift_row

def attend(queries, key_rows, values, segment, padding):
    row_count = queries.shape[0]
    block_rows = min(block_limit, row_count)
    block_count = row_count // block_rows
    query_heads = queries.reshape(block_count, block_rows, HEADS, HEAD_DIM)
    seg_blocks = segment.reshape(block_count, block_rows)
    key_heads = key_rows.reshape(row_count, HEADS, HEAD_DIM)
    value_heads = values.reshape(row_count, HEADS, HEAD_DIM)
    key_open = padding == 0

    def one_block(packed):
        query_block, seg_block = packed
        scores = jnp.einsum('qhd,khd->hqk', query_block, key_heads, precision=lax.Precision.HIGHEST) * HEAD_DIM ** (-0.5)
        scores = low_back(scores)
        allowed = (seg_block[:, None] == segment[None, :]) & key_open[None, :]
        scores = jnp.where(allowed[None], scores, neg_fill)
        maxima = lax.optimization_barrier(jnp.max(scores, axis=-1, keepdims=True))
        exponent = jnp.exp(scores - maxima)
        weights = low(exponent / lax.optimization_barrier(jnp.sum(exponent, axis=-1, keepdims=True)))
        context = jnp.einsum('hqk,khd->qhd', weights, value_heads, precision=lax.Precision.HIGHEST)
        return context.reshape(block_rows, HEADS * HEAD_DIM)
    contexts = lax.map(jax.checkpoint(one_block), (query_heads, seg_blocks))
    return contexts.reshape(row_count, HEADS * HEAD_DIM)

def pack_forward(params, rows_in, places, segment, padding):
    inward, outward, upward, downward, vectors, offsets, shifts = params
    query_in = low(rows_in + places)
    queries = low(low_back(product(query_in, inward[0]) + offsets[0]))
    key_rows = low(low_back(product(query_in, inward[1])))
    values = low(low_back(product(rows_in, inward[2]) + offsets[1]))
    context = low(low_back(attend(queries, key_rows, values, segment, padding)))
    first_sum = rows_in + low_back(product(context, outward)) + vectors[4]
    normed = layer_norm(first_sum, vectors[0], vectors[1])
    hidden = low_back(product(low(normed), upward) + shifts)
    active = low(smooth_unit(hidden))
    second_sum = normed + low_back(product(active, downward)) + vectors[5]
    return layer_norm(second_sum, vectors[2], vectors[3])

def adamw(master, gradient, old_first, old_second, step_rate):
    momentum = beta_one * old_first + (1.0 - beta_one) * gradient
    variance = beta_two * old_second + (1.0 - beta_two) * gradient * gradient
    normal_step = momentum / (1.0 - beta_one ** STEP) / (jnp.sqrt(variance / (1.0 - beta_two ** STEP)) + adam_eps)
    return (master - step_rate * (normal_step + decay_rate * master), momentum, variance)

def reference(tokens, positions, segment_ids, pad_flags, cotangent, inward, outward, upward, downward, vectors, offsets, shifts, first_inward, first_outward, first_upward, first_downward, first_vectors, first_offsets, first_shifts, second_inward, second_outward, second_upward, second_downward, second_vectors, second_offsets, second_shifts):
    masters = (inward, outward, upward, downward, vectors, offsets, shifts)
    firsts = (first_inward, first_outward, first_upward, first_downward, first_vectors, first_offsets, first_shifts)
    seconds = (second_inward, second_outward, second_upward, second_downward, second_vectors, second_offsets, second_shifts)
    working = tuple((lax.optimization_barrier(master.astype(jnp.bfloat16)).astype(jnp.float32) for master in masters))
    place_rows = positions.astype(jnp.float32).reshape(PACKS, PACK, D)
    input_rows = tokens.astype(jnp.float32).reshape(PACKS, PACK, D)

    def whole_forward(params, rows_all):

        def per_pack(packed):
            rows_in, places, segment, padding = packed
            return pack_forward(params, rows_in, places, segment, padding)
        return lax.map(per_pack, (rows_all, place_rows, segment_ids, pad_flags))
    encoded, pullback = jax.vjp(whole_forward, working, input_rows)
    grads, token_grad = pullback(cotangent.astype(jnp.float32).reshape(PACKS, PACK, D))
    updated = []
    momenta = []
    variances = []
    for master, gradient, old_first, old_second, step_rate in zip(masters, grads, firsts, seconds, step_rates):
        new_master, momentum, variance = adamw(master, gradient, old_first, old_second, step_rate)
        updated.append(new_master)
        momenta.append(momentum)
        variances.append(variance)
    return (encoded.reshape(TOKENS, D).astype(jnp.bfloat16), token_grad.reshape(TOKENS, D), grads[0], grads[1], grads[2], grads[3], grads[4], grads[5], grads[6], updated[0], updated[1], updated[2], updated[3], updated[4], updated[5], updated[6], updated[0].astype(jnp.bfloat16), updated[1].astype(jnp.bfloat16), updated[2].astype(jnp.bfloat16), updated[3].astype(jnp.bfloat16), momenta[0], momenta[1], momenta[2], momenta[3], momenta[4], momenta[5], momenta[6], variances[0], variances[1], variances[2], variances[3], variances[4], variances[5], variances[6])
```

```python
import functools
import jax
import jax.numpy as jnp
from jax import lax
from jax.experimental import pallas as pl
from jax.experimental.pallas import tpu as pltpu
from jax.sharding import PartitionSpec as P

HEAD_DIM = 32
PACK_ROWS = 4096
IMAGES = 5
QUERY_ROWS = 512
KEY_ROWS = 512
SPAN = PACK_ROWS + 512
LOG_SCALE = HEAD_DIM**-0.5 * 1.4426950408889634
FENCE = 2.0**100
LARGE = 2.0**100
SMALL = 2.0**-60
NN = (((1,), (0,)), ((), ()))
NT = (((1,), (1,)), ((), ()))
TN = (((0,), (0,)), ((), ()))
bf16 = jnp.bfloat16
f32 = jnp.float32


def mm(left, right, dims=NN):
    return lax.dot_general(left, right, dims, preferred_element_type=f32)


def iota(shape, dim):
    return lax.broadcasted_iota(jnp.int32, shape, dim)


def pieces_of(value):
    one = value.astype(bf16).astype(f32)
    rest = value - one
    two = rest.astype(bf16).astype(f32)
    return one, two, rest - two


def attend_forward_kernel(
    tok, pos, w3, off, seg, pad,
    packed, ctx, qa, qw, ka, va, rank, bounds,
    wqd, wkd, compact, dst,
):
    lane = iota((256, 128), 1)
    for which, spread in ((0, wqd), (1, wkd)):
        base = w3[which].astype(f32)
        left = pltpu.roll(base, 32, 1)
        right = pltpu.roll(base, 96, 1)
        spread[:, :128] = jnp.where(lane < 32, base, jnp.where(lane < 64, left, 0.0)).astype(bf16)
        spread[:, 128:] = jnp.where(lane < 32, right, jnp.where(lane < 64, base, 0.0)).astype(bf16)
    lane8 = iota((8, 128), 1)
    off_rows = off[...]
    off_left = pltpu.roll(off_rows, 32, 1)
    off_right = pltpu.roll(off_rows, 96, 1)
    q_bias = jnp.concatenate(
        [
            jnp.where(lane8 < 32, off_rows, jnp.where(lane8 < 64, off_left, 0.0))[0:1],
            jnp.where(lane8 < 32, off_right, jnp.where(lane8 < 64, off_rows, 0.0))[0:1],
        ],
        axis=1,
    )
    v_bias = jnp.where(lane8 < 64, off_rows, 0.0)[1:2]

    segment = seg[...]
    open_key = jnp.where(pad[...] == 0, 1.0, 0.0)
    grid_row = iota((32, 128), 0)
    before = (iota((128, 128), 0) < iota((128, 128), 1)).astype(bf16)
    in_row = mm(open_key.astype(bf16), before)
    row_total = jnp.broadcast_to(jnp.sum(open_key, axis=1, keepdims=True), (32, 128))
    above = (iota((32, 32), 1) < iota((32, 32), 0)).astype(bf16)
    place = (in_row + mm(above, row_total.astype(bf16))).astype(jnp.int32)
    place = jnp.where(open_key > 0.5, place, -1)
    for r in range(32):
        rank[r, :, :] = place[r : r + 1, :]
    for s in range(IMAGES + 1):
        if s == 0:
            bounds[0] = 0
            bounds[8] = 0
        else:
            low = (segment < s).astype(f32)
            bounds[s] = jnp.sum(low).astype(jnp.int32)
            bounds[8 + s] = jnp.sum(low * open_key).astype(jnp.int32)
    for i in range(16):
        dst[i] = jnp.sum(jnp.where(grid_row < 2 * i, open_key, 0.0)).astype(jnp.int32)
    for i in range(16):
        bounds[16 + i] = dst[i]
    total = bounds[8 + IMAGES]

    lane_row = iota((1, 128), 1)
    q_from = jnp.full((1, 128), SPAN, jnp.int32)
    q_to = jnp.full((1, 128), SPAN, jnp.int32)
    k_from = jnp.full((1, 128), SPAN, jnp.int32)
    k_to = jnp.full((1, 128), SPAN, jnp.int32)
    for s in range(IMAGES):
        at = lane_row == 64 + s
        q_from = jnp.where(at, bounds[s], q_from)
        q_to = jnp.where(at, bounds[s + 1], q_to)
        k_from = jnp.where(at, bounds[8 + s], k_from)
        k_to = jnp.where(at, bounds[9 + s], k_to)

    compact[pl.ds(0, 16), :] = jnp.zeros((16, 512), bf16)
    qa[:, pl.ds(PACK_ROWS, SPAN - PACK_ROWS), :] = jnp.zeros((2, SPAN - PACK_ROWS, 128), bf16)
    qw[pl.ds(PACK_ROWS, SPAN - PACK_ROWS), :] = jnp.zeros((SPAN - PACK_ROWS, 128), bf16)

    lane_q = iota((256, 128), 1)
    row_q = iota((256, 128), 0)

    def project(i, _):
        first = pl.multiple_of(i * 256, 256)
        rows = pl.ds(first, 256)
        token = tok[rows, :]
        query_in = (token.astype(f32) + pos[rows, :].astype(f32)).astype(bf16)
        both = (mm(query_in, wqd[...]) + q_bias).astype(bf16).astype(f32)
        here = row_q + first
        outside = (here < q_from) | (here >= q_to)
        feature = jnp.where(
            lane_q < 64 + IMAGES, jnp.where(outside, 1.0, 0.0), jnp.where(lane_q == 69, 1.0, 0.0)
        )
        for h in range(2):
            exact = both[:, 128 * h : 128 * h + 128] * LOG_SCALE
            high = exact.astype(bf16).astype(f32)
            qa[h, rows, :] = jnp.where(
                lane_q < 32, high, jnp.where(lane_q < 64, exact - high, feature)
            ).astype(bf16)
        qw[rows, :] = jnp.where(
            lane_q < 32, both[:, :128], jnp.where(lane_q < 64, both[:, 128:], 0.0)
        ).astype(bf16)
        start = dst[i]
        aligned = pl.multiple_of((start // 16) * 16, 16)
        places = jnp.concatenate([rank[2 * i], rank[2 * i + 1]], axis=1)
        hot = jnp.where(iota((272, 256), 0) + aligned == places, 1.0, 0.0).astype(bf16)
        moved = mm(hot, jnp.concatenate([query_in, token], axis=1)).astype(bf16)
        head = pl.ds(aligned, 16)
        compact[head, :] = compact[head, :] + moved[:16]
        compact[pl.ds(pl.multiple_of(aligned + 16, 16), 256), :] = moved[16:]
        return 0

    lax.fori_loop(0, 16, project, 0)

    lane_k = iota((512, 128), 1)
    row_k = iota((512, 128), 0)

    def project_keys(i, _):
        first = pl.multiple_of(i * 512, 512)
        rows = pl.ds(first, 512)
        here = row_k + first
        real = here < total
        both = mm(compact[rows, 0:256], wkd[...])
        value = mm(compact[rows, 256:512], w3[2]) + v_bias
        value = jnp.where(real, value, 0.0)
        inside = (here >= k_from) & (here < k_to)
        feature = jnp.where(inside, -FENCE, 0.0)
        feature = jnp.where(lane_k == 69, jnp.where(real, 0.0, -FENCE), feature)
        feature = jnp.where((lane_k >= 70) & (lane_k < 73), 1.0, feature)
        for h in range(2):
            key = jnp.where(real, both[:, 128 * h : 128 * h + 128], 0.0)
            ka[h, rows, :] = jnp.where(lane_k < 64, key, feature).astype(bf16)
        va[0, rows, :] = jnp.where(
            lane_k < 32, value, jnp.where(lane_k < 35, 1.0, 0.0)
        ).astype(bf16)
        va[1, rows, :] = jnp.where(
            lane_k < 3, 1.0, jnp.where((lane_k >= 32) & (lane_k < 64), value, 0.0)
        ).astype(bf16)
        return 0

    lax.fori_loop(0, SPAN // 512, project_keys, 0)

    lane_b = iota((QUERY_ROWS, 128), 1)
    row_b = iota((QUERY_ROWS, 128), 0)

    def finish(q_rows, q_row, q_start, q_end, sums, shift):
        at = row_b + q_row
        mine = (at >= q_start) & (at < q_end)
        l_zero = jnp.broadcast_to(sums[0][:, 32:33], (QUERY_ROWS, 128))
        l_one = jnp.broadcast_to(sums[1][:, 0:1], (QUERY_ROWS, 128))
        joined = jnp.where(
            lane_b < 32, sums[0] / l_zero, jnp.where(lane_b < 64, sums[1] / l_one, 0.0)
        )
        ctx[q_rows, :] = jnp.where(mine, joined, ctx[q_rows, :])
        for h, total_row in ((0, l_zero), (1, l_one)):
            one, two, three = pieces_of(-(shift[h] + jnp.log2(total_row)))
            new = jnp.where(lane_b == 70, one, jnp.where(lane_b == 71, two, three))
            spot = mine & (lane_b >= 70) & (lane_b < 73)
            old = qa[h, q_rows, :].astype(f32)
            qa[h, q_rows, :] = jnp.where(spot, new, old).astype(bf16)

    def per_segment(s, _):
        q_start, q_end = bounds[s], bounds[s + 1]
        k_start, k_end = bounds[8 + s], bounds[9 + s]
        q_first = (q_start // 16) * 16
        k_first = (k_start // 16) * 16
        q_steps = (q_end - q_first + QUERY_ROWS - 1) // QUERY_ROWS
        k_steps = (k_end - k_first + KEY_ROWS - 1) // KEY_ROWS

        def per_query(i, _):
            q_row = pl.multiple_of(q_first + i * QUERY_ROWS, 16)
            q_rows = pl.ds(q_row, QUERY_ROWS)
            zero = jnp.zeros((QUERY_ROWS, 128), f32)

            def per_key(j, sums):
                k_rows = pl.ds(pl.multiple_of(k_first + j * KEY_ROWS, 16), KEY_ROWS)
                out = []
                for h in range(2):
                    score = mm(qa[h, q_rows, :], ka[h, k_rows, :], NT)
                    weight = jnp.exp2(score).astype(bf16)
                    out.append(sums[h] + mm(weight, va[h, k_rows, :]))
                return tuple(out)

            sums = lax.fori_loop(0, k_steps, per_key, (zero, zero))
            at = row_b + q_row
            mine = (at >= q_start) & (at < q_end)
            check = jnp.where(
                mine & (lane_b == 32), sums[0], jnp.where(mine & (lane_b == 0), sums[1], 1.0)
            )
            fine = (jnp.max(check) < LARGE) & (jnp.min(check) > SMALL)

            @pl.when(fine)
            def _():
                finish(q_rows, q_row, q_start, q_end, sums, (0.0, 0.0))

            @pl.when(jnp.logical_not(fine))
            def _():
                low = jnp.full((QUERY_ROWS, 128), -3.0e38, f32)

                def peak(j, tops):
                    k_rows = pl.ds(pl.multiple_of(k_first + j * KEY_ROWS, 16), KEY_ROWS)
                    out = []
                    for h in range(2):
                        score = mm(qa[h, q_rows, :], ka[h, k_rows, :], NT)
                        out.append(
                            jnp.maximum(tops[h], jnp.max(score, axis=1, keepdims=True))
                        )
                    return tuple(out)

                tops = lax.fori_loop(0, k_steps, peak, (low, low))

                def per_key_safe(j, sums):
                    k_rows = pl.ds(pl.multiple_of(k_first + j * KEY_ROWS, 16), KEY_ROWS)
                    out = []
                    for h in range(2):
                        score = mm(qa[h, q_rows, :], ka[h, k_rows, :], NT)
                        weight = jnp.exp2(score - tops[h][:, 0:1]).astype(bf16)
                        out.append(sums[h] + mm(weight, va[h, k_rows, :]))
                    return tuple(out)

                safe = lax.fori_loop(0, k_steps, per_key_safe, (zero, zero))
                finish(q_rows, q_row, q_start, q_end, safe, tops)

            return 0

        lax.fori_loop(0, q_steps, per_query, 0)
        return 0

    lax.fori_loop(0, IMAGES, per_segment, 0)

    lane_p = iota((512, 128), 1)
    for t in range(4):
        upper = ctx[pl.ds(1024 * t, 512), :]
        lower = pltpu.roll(ctx[pl.ds(1024 * t + 512, 512), :], 64, 1)
        packed[pl.ds(512 * t, 512), :] = jnp.where(lane_p < 64, upper, lower).astype(bf16)


VMEM_SPEC = pl.BlockSpec(memory_space=pltpu.VMEM)
SMEM_SPEC = pl.BlockSpec(memory_space=pltpu.SMEM)


def attend_forward(tokens, positions, w3, off, segment, padding):
    return pl.pallas_call(
        attend_forward_kernel,
        out_shape=(
            jax.ShapeDtypeStruct((2048, 128), bf16),
            jax.ShapeDtypeStruct((SPAN, 128), f32),
            jax.ShapeDtypeStruct((2, SPAN, 128), bf16),
            jax.ShapeDtypeStruct((SPAN, 128), bf16),
            jax.ShapeDtypeStruct((2, SPAN, 128), bf16),
            jax.ShapeDtypeStruct((2, SPAN, 128), bf16),
            jax.ShapeDtypeStruct((32, 1, 128), jnp.int32),
            jax.ShapeDtypeStruct((32,), jnp.int32),
        ),
        in_specs=[VMEM_SPEC] * 6,
        out_specs=[VMEM_SPEC] * 7 + [SMEM_SPEC],
        scratch_shapes=[
            pltpu.VMEM((256, 256), bf16),
            pltpu.VMEM((256, 256), bf16),
            pltpu.VMEM((SPAN, 512), bf16),
            pltpu.SMEM((16,), jnp.int32),
        ],
        compiler_params=pltpu.CompilerParams(vmem_limit_bytes=56 * 2**20),
        cost_estimate=pl.CostEstimate(
            flops=20 * 10**9, bytes_accessed=20 * 10**6, transcendentals=10**7
        ),
    )(tokens, positions, w3, off, segment.reshape(32, 128), padding.reshape(32, 128))


def attend_backward_kernel(
    packed, ctx, qa, qw, ka, va, rank, bounds, gq, gkv, do, kw, dq, dkv
):
    lane = iota((512, 128), 1)
    for t in range(4):
        pair = packed[pl.ds(512 * t, 512), :].astype(f32)
        for half in range(2):
            rows = pl.ds(1024 * t + 512 * half, 512)
            grad = pair if half == 0 else pltpu.roll(pair, 64, 1)
            product = grad * ctx[rows, :]
            delta_zero = jnp.sum(jnp.where(lane < 32, product, 0.0), axis=1, keepdims=True)
            delta_one = jnp.sum(
                jnp.where((lane >= 32) & (lane < 64), product, 0.0), axis=1, keepdims=True
            )
            one, two, three = pieces_of(-jnp.broadcast_to(delta_zero, (512, 128)))
            tail = jnp.where(lane == 32, one, jnp.where(lane == 33, two, three))
            do[0, rows, :] = jnp.where(
                lane < 32, grad, jnp.where(lane < 35, tail, 0.0)
            ).astype(bf16)
            one, two, three = pieces_of(-jnp.broadcast_to(delta_one, (512, 128)))
            tail = jnp.where(lane == 0, one, jnp.where(lane == 1, two, three))
            do[1, rows, :] = jnp.where(
                lane < 3, tail, jnp.where((lane >= 32) & (lane < 64), grad, 0.0)
            ).astype(bf16)
    do[:, pl.ds(PACK_ROWS, SPAN - PACK_ROWS), :] = jnp.zeros((2, SPAN - PACK_ROWS, 128), bf16)
    for i in range(SPAN // 512):
        rows = pl.ds(512 * i, 512)
        dq[rows, :] = jnp.zeros((512, 128), f32)
        dkv[rows, :] = jnp.zeros((512, 128), f32)

    def per_segment(s, _):
        q_start, q_end = bounds[s], bounds[s + 1]
        k_start, k_end = bounds[8 + s], bounds[9 + s]
        q_first = (q_start // 16) * 16
        k_first = (k_start // 16) * 16
        q_steps = (q_end - q_first + QUERY_ROWS - 1) // QUERY_ROWS
        k_steps = (k_end - k_first + KEY_ROWS - 1) // KEY_ROWS

        def per_key(j, _):
            k_row = pl.multiple_of(k_first + j * KEY_ROWS, 16)
            k_rows = pl.ds(k_row, KEY_ROWS)
            at = iota((KEY_ROWS, 128), 0) + k_row
            mine = (at >= k_start) & (at < k_end)
            for h in range(2):
                mask = mine & (lane >= 32 * h) & (lane < 32 * h + 32)
                kw[h] = jnp.where(mask, ka[h, k_rows, :].astype(f32), 0.0).astype(bf16)

            def per_query(i, carry):
                q_rows = pl.ds(pl.multiple_of(q_first + i * QUERY_ROWS, 16), QUERY_ROWS)
                total = dq[q_rows, :]
                out = list(carry)
                for h in range(2):
                    score = mm(qa[h, q_rows, :], ka[h, k_rows, :], NT)
                    prob = jnp.exp2(score)
                    prob_grad = mm(do[h, q_rows, :], va[h, k_rows, :], NT)
                    score_grad = (prob * prob_grad).astype(bf16)
                    total = total + mm(score_grad, kw[h])
                    span = slice(32 * h, 32 * h + 32)
                    out[h] = out[h] + mm(qw[q_rows, span], score_grad, TN)
                    out[2 + h] = out[2 + h] + mm(do[h, q_rows, span], prob.astype(bf16), TN)
                dq[q_rows, :] = total
                return tuple(out)

            zero = jnp.zeros((32, KEY_ROWS), f32)
            done = lax.fori_loop(0, q_steps, per_query, (zero,) * 4)
            fresh = jnp.concatenate(done, axis=0).T
            dkv[k_rows, :] = dkv[k_rows, :] + jnp.where(mine, fresh, 0.0)
            return 0

        lax.fori_loop(0, k_steps, per_key, 0)
        return 0

    lax.fori_loop(0, IMAGES, per_segment, 0)

    lane_t = iota((256, 128), 1)

    def emit(i, _):
        rows = pl.ds(pl.multiple_of(i * 256, 256), 256)
        gq[rows, :] = (dq[rows, :] * HEAD_DIM**-0.5).astype(bf16)
        start = bounds[16 + i]
        aligned = pl.multiple_of((start // 16) * 16, 16)
        places = jnp.concatenate([rank[2 * i], rank[2 * i + 1]], axis=1)
        hot = jnp.where(iota((272, 256), 0) + aligned == places, 1.0, 0.0).astype(bf16)
        piece = dkv[pl.ds(aligned, 272), :]
        scale = jnp.where(iota((272, 128), 1) < 64, HEAD_DIM**-0.5, 1.0)
        gkv[rows, :] = mm(hot, (piece * scale).astype(bf16), TN).astype(bf16)
        return 0

    lax.fori_loop(0, 16, emit, 0)


def attend_backward(packed, ctx, qa, qw, ka, va, rank, bounds):
    return pl.pallas_call(
        attend_backward_kernel,
        out_shape=(
            jax.ShapeDtypeStruct((PACK_ROWS, 128), bf16),
            jax.ShapeDtypeStruct((PACK_ROWS, 128), bf16),
        ),
        in_specs=[VMEM_SPEC] * 7 + [SMEM_SPEC],
        out_specs=[VMEM_SPEC] * 2,
        scratch_shapes=[
            pltpu.VMEM((2, SPAN, 128), bf16),
            pltpu.VMEM((2, KEY_ROWS, 128), bf16),
            pltpu.VMEM((SPAN, 128), f32),
            pltpu.VMEM((SPAN, 128), f32),
        ],
        compiler_params=pltpu.CompilerParams(vmem_limit_bytes=56 * 2**20),
        cost_estimate=pl.CostEstimate(
            flops=50 * 10**9, bytes_accessed=20 * 10**6, transcendentals=10**7
        ),
    )(packed, ctx, qa, qw, ka, va, rank, bounds)


STEP = 10


neg_fill = -1e30
norm_eps = 1e-05
beta_one = 0.5
beta_two = 0.5
adam_eps = 1e-08
decay_rate = 0.0001
step_rates = (0.06, 0.15, 0.06, 0.03, 0.1, 0.1, 0.1)


def product(left_side, right_side):
    return jnp.dot(left_side, right_side, preferred_element_type=jnp.float32)


def product_left(left_side, right_side):
    return lax.dot_general(
        left_side, right_side, (((0,), (0,)), ((), ())), preferred_element_type=jnp.float32
    )


def product_right(left_side, right_side):
    return lax.dot_general(
        left_side, right_side, (((1,), (1,)), ((), ())), preferred_element_type=jnp.float32
    )


def smooth_unit(values):
    return jax.nn.gelu(values, approximate=False)


def norm_forward(values, gain_row, shift_row):
    center = values - jnp.mean(values, axis=-1, keepdims=True)
    inverse = lax.rsqrt(jnp.mean(center * center, axis=-1, keepdims=True) + norm_eps)
    scaled = center * inverse
    return (scaled * gain_row + shift_row, scaled, inverse)


def norm_backward(upstream, scaled, inverse, gain_row):
    spread = upstream * gain_row
    centred = (
        spread
        - jnp.mean(spread, axis=-1, keepdims=True)
        - scaled * jnp.mean(spread * scaled, axis=-1, keepdims=True)
    )
    return (inverse * centred, jnp.sum(upstream * scaled, axis=0), jnp.sum(upstream, axis=0))


def summed(partial_value):
    return lax.psum(partial_value, "tensor")


def adamw(master, gradient, old_first, old_second, step_rate):
    momentum = beta_one * old_first + (1.0 - beta_one) * gradient
    variance = beta_two * old_second + (1.0 - beta_two) * gradient * gradient
    normal_step = (
        momentum / (1.0 - beta_one**STEP) / (jnp.sqrt(variance / (1.0 - beta_two**STEP)) + adam_eps)
    )
    return (master - step_rate * (normal_step + decay_rate * master), momentum, variance)


def body(
    tokens,
    positions,
    segment_ids,
    pad_flags,
    cotangent,
    inward,
    outward,
    upward,
    downward,
    vectors,
    offsets,
    shifts,
    first_inward,
    first_outward,
    first_upward,
    first_downward,
    first_vectors,
    first_offsets,
    first_shifts,
    second_inward,
    second_outward,
    second_upward,
    second_downward,
    second_vectors,
    second_offsets,
    second_shifts,
):
    w_inward, w_outward, w_upward, w_downward, vector_low, offset_low, shift_low = (
        lax.all_gather(inward.astype(jnp.bfloat16), "dp", axis=1, tiled=True),
        lax.all_gather(outward.astype(jnp.bfloat16), "dp", axis=1, tiled=True),
        lax.all_gather(upward.astype(jnp.bfloat16), "dp", axis=0, tiled=True),
        lax.all_gather(downward.astype(jnp.bfloat16), "dp", axis=1, tiled=True),
        lax.all_gather(vectors.astype(jnp.bfloat16), "dp", axis=1, tiled=True),
        lax.all_gather(offsets.astype(jnp.bfloat16), "dp", axis=1, tiled=True),
        lax.all_gather(shifts.astype(jnp.bfloat16), "dp", axis=0, tiled=True),
    )
    vector_wide = vector_low.astype(jnp.float32)
    offset_wide = offset_low.astype(jnp.float32)
    shift_wide = shift_low.astype(jnp.float32)
    input_wide = tokens.astype(jnp.float32)
    query_in = (input_wide + positions.astype(jnp.float32)).astype(jnp.bfloat16)
    w_lanes = jnp.pad(w_inward, ((0, 0), (0, 0), (0, 64)))
    off_lanes = jnp.pad(offset_wide, ((0, 6), (0, 64)))
    packed, *saved = attend_forward(
        tokens, positions, w_lanes, off_lanes, segment_ids, pad_flags
    )
    pairs = packed.reshape(4, 512, 2, 64)
    context_low = pairs.transpose(0, 2, 1, 3).reshape(PACK_ROWS, 64)
    first_sum = input_wide + summed(product(context_low, w_outward)) + vector_wide[4]
    normed, scaled_one, inverse_one = norm_forward(first_sum, vector_wide[0], vector_wide[1])
    normed_low = normed.astype(jnp.bfloat16)
    hidden = product(normed_low, w_upward) + shift_wide
    unit_value, unit_back = jax.vjp(smooth_unit, hidden)
    active = unit_value.astype(jnp.bfloat16)
    second_sum = normed + summed(product(active, w_downward)) + vector_wide[5]
    result, scaled_two, inverse_two = norm_forward(second_sum, vector_wide[2], vector_wide[3])
    encoded = result.astype(jnp.bfloat16)
    upstream = cotangent.astype(jnp.float32)
    second_grad, gain_two, shift_two = norm_backward(
        upstream, scaled_two, inverse_two, vector_wide[2]
    )
    down_low = second_grad.astype(jnp.bfloat16)
    grad_downward = product_left(active, down_low)
    hidden_low = unit_back(product_right(down_low, w_downward))[0].astype(jnp.bfloat16)
    grad_upward = product_left(normed_low, hidden_low)
    grad_shifts = jnp.sum(hidden_low.astype(jnp.float32), axis=0)
    normed_grad = second_grad + summed(product_right(hidden_low, w_upward))
    first_grad, gain_one, shift_one = norm_backward(
        normed_grad, scaled_one, inverse_one, vector_wide[0]
    )
    first_low = first_grad.astype(jnp.bfloat16)
    grad_outward = product_left(context_low, first_low)
    context_grad = product_right(first_low, w_outward).astype(jnp.bfloat16)
    halves = context_grad.reshape(4, 2, 512, 64)
    gq, gkv = attend_backward(
        halves.transpose(0, 2, 1, 3).reshape(2048, 128), *saved
    )
    query_grad, key_grad, value_grad = gq[:, :64], gkv[:, :64], gkv[:, 64:]
    grad_inward = jnp.stack(
        [
            product_left(query_in, query_grad),
            product_left(query_in, key_grad),
            product_left(tokens, value_grad),
        ]
    )
    grad_offsets = jnp.stack(
        [
            jnp.sum(query_grad.astype(jnp.float32), axis=0),
            jnp.sum(value_grad.astype(jnp.float32), axis=0),
        ]
    )
    input_part = (
        product_right(query_grad, w_inward[0])
        + product_right(key_grad, w_inward[1])
        + product_right(value_grad, w_inward[2])
    )
    input_grad = first_grad + summed(input_part)
    grad_vectors = jnp.stack(
        [
            gain_one,
            shift_one,
            gain_two,
            shift_two,
            jnp.sum(first_grad, axis=0),
            jnp.sum(second_grad, axis=0),
        ]
    )
    reduced = (
        lax.psum_scatter(grad_inward, "dp", scatter_dimension=1, tiled=True),
        lax.psum_scatter(grad_outward, "dp", scatter_dimension=1, tiled=True),
        lax.psum_scatter(grad_upward, "dp", scatter_dimension=0, tiled=True),
        lax.psum_scatter(grad_downward, "dp", scatter_dimension=1, tiled=True),
        lax.psum_scatter(grad_vectors, "dp", scatter_dimension=1, tiled=True),
        lax.psum_scatter(grad_offsets, "dp", scatter_dimension=1, tiled=True),
        lax.psum_scatter(grad_shifts, "dp", scatter_dimension=0, tiled=True),
    )
    masters = (inward, outward, upward, downward, vectors, offsets, shifts)
    firsts = (
        first_inward,
        first_outward,
        first_upward,
        first_downward,
        first_vectors,
        first_offsets,
        first_shifts,
    )
    seconds = (
        second_inward,
        second_outward,
        second_upward,
        second_downward,
        second_vectors,
        second_offsets,
        second_shifts,
    )
    updated = []
    momenta = []
    variances = []
    for master, gradient, old_first, old_second, step_rate in zip(
        masters, reduced, firsts, seconds, step_rates
    ):
        new_master, momentum, variance = adamw(master, gradient, old_first, old_second, step_rate)
        updated.append(new_master)
        momenta.append(momentum)
        variances.append(variance)
    return (
        encoded,
        input_grad,
        reduced[0],
        reduced[1],
        reduced[2],
        reduced[3],
        reduced[4],
        reduced[5],
        reduced[6],
        updated[0],
        updated[1],
        updated[2],
        updated[3],
        updated[4],
        updated[5],
        updated[6],
        updated[0].astype(jnp.bfloat16),
        updated[1].astype(jnp.bfloat16),
        updated[2].astype(jnp.bfloat16),
        updated[3].astype(jnp.bfloat16),
        momenta[0],
        momenta[1],
        momenta[2],
        momenta[3],
        momenta[4],
        momenta[5],
        momenta[6],
        variances[0],
        variances[1],
        variances[2],
        variances[3],
        variances[4],
        variances[5],
        variances[6],
    )


def solution(mesh):
    in_specs = (
        P("dp", None),
        P("dp", None),
        P("dp", None),
        P("dp", None),
        P("dp", None),
        P(None, "dp", "tensor"),
        P("tensor", "dp"),
        P("dp", "tensor"),
        P("tensor", "dp"),
        P(None, "dp"),
        P(None, ("tensor", "dp")),
        P(("tensor", "dp")),
        P(None, "dp", "tensor"),
        P("tensor", "dp"),
        P("dp", "tensor"),
        P("tensor", "dp"),
        P(None, "dp"),
        P(None, ("tensor", "dp")),
        P(("tensor", "dp")),
        P(None, "dp", "tensor"),
        P("tensor", "dp"),
        P("dp", "tensor"),
        P("tensor", "dp"),
        P(None, "dp"),
        P(None, ("tensor", "dp")),
        P(("tensor", "dp")),
    )
    out_specs = (
        P("dp", None),
        P("dp", None),
        P(None, "dp", "tensor"),
        P("tensor", "dp"),
        P("dp", "tensor"),
        P("tensor", "dp"),
        P(None, "dp"),
        P(None, ("tensor", "dp")),
        P(("tensor", "dp")),
        P(None, "dp", "tensor"),
        P("tensor", "dp"),
        P("dp", "tensor"),
        P("tensor", "dp"),
        P(None, "dp"),
        P(None, ("tensor", "dp")),
        P(("tensor", "dp")),
        P(None, "dp", "tensor"),
        P("tensor", "dp"),
        P("dp", "tensor"),
        P("tensor", "dp"),
        P(None, "dp", "tensor"),
        P("tensor", "dp"),
        P("dp", "tensor"),
        P("tensor", "dp"),
        P(None, "dp"),
        P(None, ("tensor", "dp")),
        P(("tensor", "dp")),
        P(None, "dp", "tensor"),
        P("tensor", "dp"),
        P("dp", "tensor"),
        P("tensor", "dp"),
        P(None, "dp"),
        P(None, ("tensor", "dp")),
        P(("tensor", "dp")),
    )
    return jax.shard_map(body, mesh=mesh, in_specs=in_specs, out_specs=out_specs, check_vma=False)
```

```python
import functools
import jax
import jax.numpy as jnp
from jax import lax
from jax.experimental import pallas as pl
from jax.experimental.pallas import tpu as pltpu
from jax.sharding import PartitionSpec as P

HEAD_DIM = 32
PACK_ROWS = 4096
IMAGES = 5
QUERY_ROWS = 512
KEY_ROWS = 512
SPAN = PACK_ROWS + 512
LOG_SCALE = HEAD_DIM**-0.5 * 1.4426950408889634
FENCE = 2.0**100
LARGE = 2.0**100
SMALL = 2.0**-60
NN = (((1,), (0,)), ((), ()))
NT = (((1,), (1,)), ((), ()))
TN = (((0,), (0,)), ((), ()))
bf16 = jnp.bfloat16
f32 = jnp.float32


def mm(left, right, dims=NN):
    return lax.dot_general(left, right, dims, preferred_element_type=f32)


def iota(shape, dim):
    return lax.broadcasted_iota(jnp.int32, shape, dim)


def pieces_of(value):
    one = value.astype(bf16).astype(f32)
    rest = value - one
    two = rest.astype(bf16).astype(f32)
    return one, two, rest - two


def attend_forward_kernel(
    tok, pos, w3, off, seg, pad,
    packed, ctx, qa, qw, ka, va, rank, bounds,
    wqd, wkd, compact, dst,
):
    lane = iota((256, 128), 1)
    for which, spread in ((0, wqd), (1, wkd)):
        base = w3[which].astype(f32)
        left = pltpu.roll(base, 32, 1)
        right = pltpu.roll(base, 96, 1)
        spread[:, :128] = jnp.where(lane < 32, base, jnp.where(lane < 64, left, 0.0)).astype(bf16)
        spread[:, 128:] = jnp.where(lane < 32, right, jnp.where(lane < 64, base, 0.0)).astype(bf16)
    lane8 = iota((8, 128), 1)
    off_rows = off[...]
    off_left = pltpu.roll(off_rows, 32, 1)
    off_right = pltpu.roll(off_rows, 96, 1)
    q_bias = jnp.concatenate(
        [
            jnp.where(lane8 < 32, off_rows, jnp.where(lane8 < 64, off_left, 0.0))[0:1],
            jnp.where(lane8 < 32, off_right, jnp.where(lane8 < 64, off_rows, 0.0))[0:1],
        ],
        axis=1,
    )
    v_bias = jnp.where(lane8 < 64, off_rows, 0.0)[1:2]

    segment = seg[...]
    open_key = jnp.where(pad[...] == 0, 1.0, 0.0)
    grid_row = iota((32, 128), 0)
    before = (iota((128, 128), 0) < iota((128, 128), 1)).astype(bf16)
    in_row = mm(open_key.astype(bf16), before)
    row_total = jnp.broadcast_to(jnp.sum(open_key, axis=1, keepdims=True), (32, 128))
    above = (iota((32, 32), 1) < iota((32, 32), 0)).astype(bf16)
    place = (in_row + mm(above, row_total.astype(bf16))).astype(jnp.int32)
    place = jnp.where(open_key > 0.5, place, -1)
    for r in range(32):
        rank[r, :, :] = place[r : r + 1, :]
    for s in range(IMAGES + 1):
        if s == 0:
            bounds[0] = 0
            bounds[8] = 0
        else:
            low = (segment < s).astype(f32)
            bounds[s] = jnp.sum(low).astype(jnp.int32)
            bounds[8 + s] = jnp.sum(low * open_key).astype(jnp.int32)
    for i in range(16):
        dst[i] = jnp.sum(jnp.where(grid_row < 2 * i, open_key, 0.0)).astype(jnp.int32)
    for i in range(16):
        bounds[16 + i] = dst[i]
    total = bounds[8 + IMAGES]

    lane_row = iota((1, 128), 1)
    q_from = jnp.full((1, 128), SPAN, jnp.int32)
    q_to = jnp.full((1, 128), SPAN, jnp.int32)
    k_from = jnp.full((1, 128), SPAN, jnp.int32)
    k_to = jnp.full((1, 128), SPAN, jnp.int32)
    for s in range(IMAGES):
        at = lane_row == 64 + s
        q_from = jnp.where(at, bounds[s], q_from)
        q_to = jnp.where(at, bounds[s + 1], q_to)
        k_from = jnp.where(at, bounds[8 + s], k_from)
        k_to = jnp.where(at, bounds[9 + s], k_to)

    compact[pl.ds(0, 16), :] = jnp.zeros((16, 512), bf16)
    qa[:, pl.ds(PACK_ROWS, SPAN - PACK_ROWS), :] = jnp.zeros((2, SPAN - PACK_ROWS, 128), bf16)
    qw[pl.ds(PACK_ROWS, SPAN - PACK_ROWS), :] = jnp.zeros((SPAN - PACK_ROWS, 128), bf16)

    lane_q = iota((256, 128), 1)
    row_q = iota((256, 128), 0)

    def project(i, _):
        first = pl.multiple_of(i * 256, 256)
        rows = pl.ds(first, 256)
        token = tok[rows, :]
        query_in = (token.astype(f32) + pos[rows, :].astype(f32)).astype(bf16)
        both = (mm(query_in, wqd[...]) + q_bias).astype(bf16).astype(f32)
        here = row_q + first
        outside = (here < q_from) | (here >= q_to)
        feature = jnp.where(
            lane_q < 64 + IMAGES, jnp.where(outside, 1.0, 0.0), jnp.where(lane_q == 69, 1.0, 0.0)
        )
        for h in range(2):
            exact = both[:, 128 * h : 128 * h + 128] * LOG_SCALE
            high = exact.astype(bf16).astype(f32)
            qa[h, rows, :] = jnp.where(
                lane_q < 32, high, jnp.where(lane_q < 64, exact - high, feature)
            ).astype(bf16)
        qw[rows, :] = jnp.where(
            lane_q < 32, both[:, :128], jnp.where(lane_q < 64, both[:, 128:], 0.0)
        ).astype(bf16)
        start = dst[i]
        aligned = pl.multiple_of((start // 16) * 16, 16)
        places = jnp.concatenate([rank[2 * i], rank[2 * i + 1]], axis=1)
        hot = jnp.where(iota((272, 256), 0) + aligned == places, 1.0, 0.0).astype(bf16)
        moved = mm(hot, jnp.concatenate([query_in, token], axis=1)).astype(bf16)
        head = pl.ds(aligned, 16)
        compact[head, :] = compact[head, :] + moved[:16]
        compact[pl.ds(pl.multiple_of(aligned + 16, 16), 256), :] = moved[16:]
        return 0

    lax.fori_loop(0, 16, project, 0)

    lane_k = iota((512, 128), 1)
    row_k = iota((512, 128), 0)

    def project_keys(i, _):
        first = pl.multiple_of(i * 512, 512)
        rows = pl.ds(first, 512)
        here = row_k + first
        real = here < total
        both = mm(compact[rows, 0:256], wkd[...])
        value = mm(compact[rows, 256:512], w3[2]) + v_bias
        value = jnp.where(real, value, 0.0)
        inside = (here >= k_from) & (here < k_to)
        feature = jnp.where(inside, -FENCE, 0.0)
        feature = jnp.where(lane_k == 69, jnp.where(real, 0.0, -FENCE), feature)
        feature = jnp.where((lane_k >= 70) & (lane_k < 73), 1.0, feature)
        for h in range(2):
            key = jnp.where(real, both[:, 128 * h : 128 * h + 128], 0.0)
            ka[h, rows, :] = jnp.where(lane_k < 64, key, feature).astype(bf16)
        va[0, rows, :] = jnp.where(
            lane_k < 32, value, jnp.where(lane_k < 35, 1.0, 0.0)
        ).astype(bf16)
        va[1, rows, :] = jnp.where(
            lane_k < 3, 1.0, jnp.where((lane_k >= 32) & (lane_k < 64), value, 0.0)
        ).astype(bf16)
        return 0

    lax.fori_loop(0, SPAN // 512, project_keys, 0)

    lane_b = iota((QUERY_ROWS, 128), 1)
    row_b = iota((QUERY_ROWS, 128), 0)

    def finish(q_rows, q_row, q_start, q_end, sums, shift):
        at = row_b + q_row
        mine = (at >= q_start) & (at < q_end)
        l_zero = jnp.broadcast_to(sums[0][:, 32:33], (QUERY_ROWS, 128))
        l_one = jnp.broadcast_to(sums[1][:, 0:1], (QUERY_ROWS, 128))
        joined = jnp.where(
            lane_b < 32, sums[0] / l_zero, jnp.where(lane_b < 64, sums[1] / l_one, 0.0)
        )
        ctx[q_rows, :] = jnp.where(mine, joined, ctx[q_rows, :])
        for h, total_row in ((0, l_zero), (1, l_one)):
            one, two, three = pieces_of(-(shift[h] + jnp.log2(total_row)))
            new = jnp.where(lane_b == 70, one, jnp.where(lane_b == 71, two, three))
            spot = mine & (lane_b >= 70) & (lane_b < 73)
            old = qa[h, q_rows, :].astype(f32)
            qa[h, q_rows, :] = jnp.where(spot, new, old).astype(bf16)

    def per_segment(s, _):
        q_start, q_end = bounds[s], bounds[s + 1]
        k_start, k_end = bounds[8 + s], bounds[9 + s]
        q_first = (q_start // 16) * 16
        k_first = (k_start // 16) * 16
        q_steps = (q_end - q_first + QUERY_ROWS - 1) // QUERY_ROWS
        k_steps = (k_end - k_first + KEY_ROWS - 1) // KEY_ROWS

        def per_query(i, _):
            q_row = pl.multiple_of(q_first + i * QUERY_ROWS, 16)
            q_rows = pl.ds(q_row, QUERY_ROWS)
            zero = jnp.zeros((QUERY_ROWS, 128), f32)

            def per_key(j, sums):
                k_rows = pl.ds(pl.multiple_of(k_first + j * KEY_ROWS, 16), KEY_ROWS)
                out = []
                for h in range(2):
                    score = mm(qa[h, q_rows, :], ka[h, k_rows, :], NT)
                    weight = jnp.exp2(score).astype(bf16)
                    out.append(sums[h] + mm(weight, va[h, k_rows, :]))
                return tuple(out)

            sums = lax.fori_loop(0, k_steps, per_key, (zero, zero))
            at = row_b + q_row
            mine = (at >= q_start) & (at < q_end)
            check = jnp.where(
                mine & (lane_b == 32), sums[0], jnp.where(mine & (lane_b == 0), sums[1], 1.0)
            )
            fine = (jnp.max(check) < LARGE) & (jnp.min(check) > SMALL)

            @pl.when(fine)
            def _():
                finish(q_rows, q_row, q_start, q_end, sums, (0.0, 0.0))

            @pl.when(jnp.logical_not(fine))
            def _():
                low = jnp.full((QUERY_ROWS, 128), -3.0e38, f32)

                def peak(j, tops):
                    k_rows = pl.ds(pl.multiple_of(k_first + j * KEY_ROWS, 16), KEY_ROWS)
                    out = []
                    for h in range(2):
                        score = mm(qa[h, q_rows, :], ka[h, k_rows, :], NT)
                        out.append(
                            jnp.maximum(tops[h], jnp.max(score, axis=1, keepdims=True))
                        )
                    return tuple(out)

                tops = lax.fori_loop(0, k_steps, peak, (low, low))

                def per_key_safe(j, sums):
                    k_rows = pl.ds(pl.multiple_of(k_first + j * KEY_ROWS, 16), KEY_ROWS)
                    out = []
                    for h in range(2):
                        score = mm(qa[h, q_rows, :], ka[h, k_rows, :], NT)
                        weight = jnp.exp2(score - tops[h][:, 0:1]).astype(bf16)
                        out.append(sums[h] + mm(weight, va[h, k_rows, :]))
                    return tuple(out)

                safe = lax.fori_loop(0, k_steps, per_key_safe, (zero, zero))
                finish(q_rows, q_row, q_start, q_end, safe, tops)

            return 0

        lax.fori_loop(0, q_steps, per_query, 0)
        return 0

    lax.fori_loop(0, IMAGES, per_segment, 0)

    lane_p = iota((128, 128), 1)
    for b in range(16):
        upper = ctx[pl.ds(256 * b, 128), :]
        lower = pltpu.roll(ctx[pl.ds(256 * b + 128, 128), :], 64, 1)
        packed[pl.ds(128 * b, 128), :] = jnp.where(lane_p < 64, upper, lower).astype(bf16)


VMEM_SPEC = pl.BlockSpec(memory_space=pltpu.VMEM)
SMEM_SPEC = pl.BlockSpec(memory_space=pltpu.SMEM)


def attend_forward(tokens, positions, w3, off, segment, padding):
    return pl.pallas_call(
        attend_forward_kernel,
        out_shape=(
            jax.ShapeDtypeStruct((2048, 128), bf16),
            jax.ShapeDtypeStruct((SPAN, 128), f32),
            jax.ShapeDtypeStruct((2, SPAN, 128), bf16),
            jax.ShapeDtypeStruct((SPAN, 128), bf16),
            jax.ShapeDtypeStruct((2, SPAN, 128), bf16),
            jax.ShapeDtypeStruct((2, SPAN, 128), bf16),
            jax.ShapeDtypeStruct((32, 1, 128), jnp.int32),
            jax.ShapeDtypeStruct((32,), jnp.int32),
        ),
        in_specs=[VMEM_SPEC] * 6,
        out_specs=[VMEM_SPEC] * 7 + [SMEM_SPEC],
        scratch_shapes=[
            pltpu.VMEM((256, 256), bf16),
            pltpu.VMEM((256, 256), bf16),
            pltpu.VMEM((SPAN, 512), bf16),
            pltpu.SMEM((16,), jnp.int32),
        ],
        compiler_params=pltpu.CompilerParams(vmem_limit_bytes=56 * 2**20),
        cost_estimate=pl.CostEstimate(
            flops=20 * 10**9, bytes_accessed=20 * 10**6, transcendentals=10**7
        ),
    )(tokens, positions, w3, off, segment.reshape(32, 128), padding.reshape(32, 128))


def attend_backward_kernel(
    packed, ctx, qa, qw, ka, va, rank, bounds, gq, gkv, do, kw, dq, dkv
):
    lane = iota((128, 128), 1)
    for b in range(16):
        pair = packed[pl.ds(128 * b, 128), :].astype(f32)
        for half in range(2):
            rows = pl.ds(256 * b + 128 * half, 128)
            grad = pair if half == 0 else pltpu.roll(pair, 64, 1)
            product = grad * ctx[rows, :]
            delta_zero = jnp.sum(jnp.where(lane < 32, product, 0.0), axis=1, keepdims=True)
            delta_one = jnp.sum(
                jnp.where((lane >= 32) & (lane < 64), product, 0.0), axis=1, keepdims=True
            )
            one, two, three = pieces_of(-jnp.broadcast_to(delta_zero, (128, 128)))
            tail = jnp.where(lane == 32, one, jnp.where(lane == 33, two, three))
            do[0, rows, :] = jnp.where(
                lane < 32, grad, jnp.where(lane < 35, tail, 0.0)
            ).astype(bf16)
            one, two, three = pieces_of(-jnp.broadcast_to(delta_one, (128, 128)))
            tail = jnp.where(lane == 0, one, jnp.where(lane == 1, two, three))
            do[1, rows, :] = jnp.where(
                lane < 3, tail, jnp.where((lane >= 32) & (lane < 64), grad, 0.0)
            ).astype(bf16)
    do[:, pl.ds(PACK_ROWS, SPAN - PACK_ROWS), :] = jnp.zeros((2, SPAN - PACK_ROWS, 128), bf16)
    lane = iota((512, 128), 1)
    for i in range(SPAN // 512):
        rows = pl.ds(512 * i, 512)
        dq[rows, :] = jnp.zeros((512, 128), f32)
        dkv[rows, :] = jnp.zeros((512, 128), f32)

    def per_segment(s, _):
        q_start, q_end = bounds[s], bounds[s + 1]
        k_start, k_end = bounds[8 + s], bounds[9 + s]
        q_first = (q_start // 16) * 16
        k_first = (k_start // 16) * 16
        q_steps = (q_end - q_first + QUERY_ROWS - 1) // QUERY_ROWS
        k_steps = (k_end - k_first + KEY_ROWS - 1) // KEY_ROWS

        def per_key(j, _):
            k_row = pl.multiple_of(k_first + j * KEY_ROWS, 16)
            k_rows = pl.ds(k_row, KEY_ROWS)
            at = iota((KEY_ROWS, 128), 0) + k_row
            mine = (at >= k_start) & (at < k_end)
            for h in range(2):
                mask = mine & (lane >= 32 * h) & (lane < 32 * h + 32)
                kw[h] = jnp.where(mask, ka[h, k_rows, :].astype(f32), 0.0).astype(bf16)

            def per_query(i, carry):
                q_rows = pl.ds(pl.multiple_of(q_first + i * QUERY_ROWS, 16), QUERY_ROWS)
                total = dq[q_rows, :]
                out = list(carry)
                for h in range(2):
                    score = mm(qa[h, q_rows, :], ka[h, k_rows, :], NT)
                    prob = jnp.exp2(score)
                    prob_grad = mm(do[h, q_rows, :], va[h, k_rows, :], NT)
                    score_grad = (prob * prob_grad).astype(bf16)
                    total = total + mm(score_grad, kw[h])
                    span = slice(32 * h, 32 * h + 32)
                    out[h] = out[h] + mm(qw[q_rows, span], score_grad, TN)
                    out[2 + h] = out[2 + h] + mm(do[h, q_rows, span], prob.astype(bf16), TN)
                dq[q_rows, :] = total
                return tuple(out)

            zero = jnp.zeros((32, KEY_ROWS), f32)
            done = lax.fori_loop(0, q_steps, per_query, (zero,) * 4)
            fresh = jnp.concatenate(done, axis=0).T
            dkv[k_rows, :] = dkv[k_rows, :] + jnp.where(mine, fresh, 0.0)
            return 0

        lax.fori_loop(0, k_steps, per_key, 0)
        return 0

    lax.fori_loop(0, IMAGES, per_segment, 0)

    lane_t = iota((256, 128), 1)

    def emit(i, _):
        rows = pl.ds(pl.multiple_of(i * 256, 256), 256)
        gq[rows, :] = (dq[rows, :] * HEAD_DIM**-0.5).astype(bf16)
        start = bounds[16 + i]
        aligned = pl.multiple_of((start // 16) * 16, 16)
        places = jnp.concatenate([rank[2 * i], rank[2 * i + 1]], axis=1)
        hot = jnp.where(iota((272, 256), 0) + aligned == places, 1.0, 0.0).astype(bf16)
        piece = dkv[pl.ds(aligned, 272), :]
        scale = jnp.where(iota((272, 128), 1) < 64, HEAD_DIM**-0.5, 1.0)
        gkv[rows, :] = mm(hot, (piece * scale).astype(bf16), TN).astype(bf16)
        return 0

    lax.fori_loop(0, 16, emit, 0)


def attend_backward(packed, ctx, qa, qw, ka, va, rank, bounds):
    return pl.pallas_call(
        attend_backward_kernel,
        out_shape=(
            jax.ShapeDtypeStruct((PACK_ROWS, 128), bf16),
            jax.ShapeDtypeStruct((PACK_ROWS, 128), bf16),
        ),
        in_specs=[VMEM_SPEC] * 7 + [SMEM_SPEC],
        out_specs=[VMEM_SPEC] * 2,
        scratch_shapes=[
            pltpu.VMEM((2, SPAN, 128), bf16),
            pltpu.VMEM((2, KEY_ROWS, 128), bf16),
            pltpu.VMEM((SPAN, 128), f32),
            pltpu.VMEM((SPAN, 128), f32),
        ],
        compiler_params=pltpu.CompilerParams(vmem_limit_bytes=56 * 2**20),
        cost_estimate=pl.CostEstimate(
            flops=50 * 10**9, bytes_accessed=20 * 10**6, transcendentals=10**7
        ),
    )(packed, ctx, qa, qw, ka, va, rank, bounds)


STEP = 10


neg_fill = -1e30
norm_eps = 1e-05
beta_one = 0.5
beta_two = 0.5
adam_eps = 1e-08
decay_rate = 0.0001
step_rates = (0.06, 0.15, 0.06, 0.03, 0.1, 0.1, 0.1)


def product(left_side, right_side):
    return jnp.dot(left_side, right_side, preferred_element_type=jnp.float32)


def product_left(left_side, right_side):
    return lax.dot_general(
        left_side, right_side, (((0,), (0,)), ((), ())), preferred_element_type=jnp.float32
    )


def product_right(left_side, right_side):
    return lax.dot_general(
        left_side, right_side, (((1,), (1,)), ((), ())), preferred_element_type=jnp.float32
    )


def smooth_unit(values):
    return jax.nn.gelu(values, approximate=False)


def norm_forward(values, gain_row, shift_row):
    center = values - jnp.mean(values, axis=-1, keepdims=True)
    inverse = lax.rsqrt(jnp.mean(center * center, axis=-1, keepdims=True) + norm_eps)
    scaled = center * inverse
    return (scaled * gain_row + shift_row, scaled, inverse)


def norm_backward(upstream, scaled, inverse, gain_row):
    spread = upstream * gain_row
    centred = (
        spread
        - jnp.mean(spread, axis=-1, keepdims=True)
        - scaled * jnp.mean(spread * scaled, axis=-1, keepdims=True)
    )
    return (inverse * centred, jnp.sum(upstream * scaled, axis=0), jnp.sum(upstream, axis=0))


def summed(partial_value):
    return lax.psum(partial_value, "tensor")


def adamw(master, gradient, old_first, old_second, step_rate):
    momentum = beta_one * old_first + (1.0 - beta_one) * gradient
    variance = beta_two * old_second + (1.0 - beta_two) * gradient * gradient
    normal_step = (
        momentum / (1.0 - beta_one**STEP) / (jnp.sqrt(variance / (1.0 - beta_two**STEP)) + adam_eps)
    )
    return (master - step_rate * (normal_step + decay_rate * master), momentum, variance)


MESH = pl.DeviceIdType.MESH
ANY_SPEC = pl.BlockSpec(memory_space=pl.ANY)
SHARD_ROWS = 304
GROUPS = 16
CHUNK = 256
CHUNKS = 4
OWN_ROWS = CHUNK * CHUNKS


def greet(peers):
    barrier = pltpu.get_barrier_semaphore()
    for peer in peers:
        pl.semaphore_signal(barrier, inc=1, device_id=peer, device_id_type=MESH)
    return lambda: pl.semaphore_wait(barrier, len(peers))


def remote(source, target, send_sem, recv_sem, peer):
    return pltpu.make_async_remote_copy(
        src_ref=source,
        dst_ref=target,
        send_sem=send_sem,
        recv_sem=recv_sem,
        device_id=peer,
        device_id_type=MESH,
    )


def gather_kernel(
    up, down, outer, vec, shift, inward, off,
    pack, w3, offs,
    small, one, send_buf, recv_buf, send_sem, recv_sem,
):
    me = lax.axis_index("dp")
    peers = [lax.rem(me + k, 8) for k in range(1, 8)]
    ready = greet([{"dp": p} for p in peers])
    send_buf[...] = jnp.zeros((112, 128), bf16)
    for which in range(3):
        send_buf[32 * which : 32 * which + 32, 0:64] = inward[which].astype(bf16)
    small[...] = jnp.zeros((3, 16, 128), f32)
    small[0, 0:2, 0:8] = off[...]
    small[1, 0:6, 0:32] = vec[...]
    small[2, 6:7, 0:64] = shift[...]
    send_buf[96:112, :] = pltpu.roll(small[0], me * 8, 1).astype(bf16)
    recv_buf[me] = send_buf[...]
    ready()
    copies = []
    for k, peer in enumerate(peers):
        copy = remote(
            send_buf, recv_buf.at[me], send_sem.at[k], recv_sem.at[me], {"dp": peer}
        )
        copy.start()
        copies.append(copy)
    for b in range(4):
        one[32 * b : 32 * b + 32, :] = up[:, 128 * b : 128 * b + 128].astype(bf16)
        one[128 + 32 * b : 160 + 32 * b, :] = down[:, 128 * b : 128 * b + 128].astype(bf16)
    one[256:304, :] = jnp.zeros((48, 128), bf16)
    one[256:288, 0:64] = outer[...].astype(bf16)
    placed = pltpu.roll(small[1], lax.rem(me, 4) * 32, 1)
    placed = placed + pltpu.roll(small[2], lax.rem(me, 2) * 64, 1)
    one[288:304, :] = placed.astype(bf16)

    def spread(j, _):
        pack[j] = one[...]
        return 0

    lax.fori_loop(0, GROUPS, spread, 0)
    for peer in peers:
        remote(
            send_buf, recv_buf.at[peer], send_sem.at[0], recv_sem.at[peer], {"dp": peer}
        ).wait_recv()
    total = jnp.zeros((16, 128), f32)
    for d in range(8):
        for which in range(3):
            w3[which, 32 * d : 32 * d + 32, :] = recv_buf[d, 32 * which : 32 * which + 32, :]
        total = total + recv_buf[d, 96:112, :].astype(f32)
    offs[...] = total[0:8]
    for copy in copies:
        copy.wait_send()


def gather_weights(upward, down_t, out_t, vectors, shifts, inward, offsets):
    return pl.pallas_call(
        gather_kernel,
        out_shape=(
            jax.ShapeDtypeStruct((GROUPS, SHARD_ROWS, 128), bf16),
            jax.ShapeDtypeStruct((3, 256, 128), bf16),
            jax.ShapeDtypeStruct((8, 128), f32),
        ),
        in_specs=[VMEM_SPEC] * 7,
        out_specs=[VMEM_SPEC] * 3,
        scratch_shapes=[
            pltpu.VMEM((3, 16, 128), f32),
            pltpu.VMEM((SHARD_ROWS, 128), bf16),
            pltpu.VMEM((112, 128), bf16),
            pltpu.VMEM((8, 112, 128), bf16),
            pltpu.SemaphoreType.DMA((7,)),
            pltpu.SemaphoreType.DMA((8,)),
        ],
        compiler_params=pltpu.CompilerParams(
            collective_id=0, has_side_effects=True, vmem_limit_bytes=16 * 2**20
        ),
    )(upward, down_t, out_t, vectors, shifts, inward, offsets)


def norm_rows(values):
    center = values - jnp.mean(values, axis=1, keepdims=True)
    inverse = lax.rsqrt(jnp.mean(center * center, axis=1, keepdims=True) + norm_eps)
    return center * inverse, inverse


def norm_rows_back(spread, scaled, inverse):
    return inverse * (
        spread
        - jnp.mean(spread, axis=1, keepdims=True)
        - scaled * jnp.mean(spread * scaled, axis=1, keepdims=True)
    )


def dense_kernel(
    ctxp, half, tok_hbm, cot_hbm,
    encoded, dctx, first, gout,
    other, ctxs, up, down, out_a, out_b, vec, shift,
    tok, cot, enc, grads_ctx, normed_low, second_low, first_a, first_b,
    active, hgrad, slope, sums, give, take, keep,
    w_sem, load_sem, ctx_send, ctx_recv, dctx_send, dctx_recv,
    enc_send, enc_recv, local_sem, g_sem,
):
    me = lax.axis_index("tensor")
    core = lax.rem(me, 2)
    sibling = me + 1 - 2 * core
    across = lax.rem(me + 2, 4)
    diagonal = lax.rem(sibling + 2, 4)
    order = (sibling, across, diagonal)
    ready = greet([{"tensor": p} for p in order])
    own = pl.multiple_of(me * OWN_ROWS, OWN_ROWS)
    load_tok = pltpu.make_async_copy(tok_hbm.at[pl.ds(own, OWN_ROWS)], tok, load_sem.at[0])
    load_cot = pltpu.make_async_copy(cot_hbm.at[pl.ds(own, OWN_ROWS)], cot, load_sem.at[1])
    load_tok.start()
    load_cot.start()
    ctxs[me] = ctxp[pl.ds(pl.multiple_of(me * 512, 512), 512), :]
    sums[...] = jnp.zeros((8, 256), f32)
    ready()
    weights = [
        remote(
            half.at[:, pl.ds(256, 48)], other.at[:, pl.ds(256, 48)],
            w_sem.at[0], w_sem.at[1], {"tensor": sibling},
        ),
        remote(
            half.at[:, pl.ds(0, 256)], other.at[:, pl.ds(0, 256)],
            w_sem.at[2], w_sem.at[3], {"tensor": sibling},
        ),
    ]
    weights[0].start()

    def ctx_copy(peer, c):
        rows = pl.ds(pl.multiple_of(peer * 512 + c * 128, 128), 128)
        return remote(
            ctxp.at[rows], ctxs.at[me, pl.ds(pl.multiple_of(c * 128, 128), 128)],
            ctx_send.at[peer, c], ctx_recv.at[me, c], {"tensor": peer},
        )

    def ctx_arrival(peer, c):
        rows = pl.ds(pl.multiple_of(c * 128, 128), 128)
        return remote(
            ctxp.at[rows], ctxs.at[peer, rows],
            ctx_send.at[peer, c], ctx_recv.at[peer, c], {"tensor": peer},
        )

    for peer in (across, diagonal, sibling):
        ctx_copy(peer, 0).start()
    weights[1].start()
    for c in range(1, CHUNKS):
        for peer in (across, diagonal, sibling):
            ctx_copy(peer, c).start()

    out_a[...] = jnp.zeros((256, 512), bf16)
    out_b[...] = jnp.zeros((256, 512), bf16)

    def unpack_small(source, t_of):
        for ty in range(2):
            t = t_of(ty)
            lanes = pl.ds(pl.multiple_of(t * 128, 128), 128)
            for d in range(8):
                piece = source[2 * d + ty, 256:288, :].astype(f32)
                out_a[32 * d : 32 * d + 32, lanes] = piece.astype(bf16)
                out_b[32 * d : 32 * d + 32, lanes] = pltpu.roll(piece, 64, 1).astype(bf16)
            for b in range(4):
                both = source[4 * b + ty, 288:304, :] + source[4 * b + 2 + ty, 288:304, :]
                shift[:, pl.ds(pl.multiple_of(t * 512 + 128 * b, 128), 128)] = (
                    both.astype(f32)[6:7]
                )

    def unpack_large(source, t_of):
        for ty in range(2):
            t = t_of(ty)

            def one_row(d, _):
                rows = pl.ds(pl.multiple_of(d * 32, 32), 32)
                for b in range(4):
                    lanes = pl.ds(pl.multiple_of(t * 512 + 128 * b, 128), 128)
                    up[rows, lanes] = source[2 * d + ty, 32 * b : 32 * b + 32, :]
                    down[rows, lanes] = source[2 * d + ty, 128 + 32 * b : 160 + 32 * b, :]
                return 0

            lax.fori_loop(0, 8, one_row, 0)

    mine_t = lambda ty: 2 * ty + core
    other_t = lambda ty: 2 * ty + 1 - core
    for b in range(2):
        total = jnp.zeros((16, 128), f32)
        for d in range(4 * b, 4 * b + 4):
            total = total + half[2 * d, 288:304, :].astype(f32)
        vec[:, 128 * b : 128 * b + 128] = total[0:8]
    unpack_small(half, mine_t)
    unpack_large(half, mine_t)
    weights[0].wait_recv()
    unpack_small(other, other_t)
    weights[1].wait_recv()
    unpack_large(other, other_t)
    load_tok.wait()
    load_cot.wait()

    def enc_copies(c):
        rows = pl.ds(pl.multiple_of(own + c * CHUNK, CHUNK), CHUNK)
        source = enc.at[pl.ds(pl.multiple_of(c * CHUNK, CHUNK), CHUNK)]
        return (
            remote(source, encoded.at[rows], enc_send.at[0, c], enc_recv.at[0, c],
                   {"tensor": across}),
            remote(source, encoded.at[rows], enc_send.at[1, c], enc_recv.at[1, c],
                   {"tensor": sibling}),
            pltpu.make_async_copy(source, encoded.at[rows], local_sem.at[0, c]),
        )

    def enc_arrival(owner, kind, c):
        rows = pl.ds(pl.multiple_of(owner * OWN_ROWS + c * CHUNK, CHUNK), CHUNK)
        return remote(encoded.at[rows], encoded.at[rows], enc_send.at[2, c],
                      enc_recv.at[kind, c], {"tensor": sibling})

    def dctx_copy(peer, c):
        rows = pl.ds(pl.multiple_of(c * 128, 128), 128)
        return remote(
            grads_ctx.at[peer, rows],
            dctx.at[pl.ds(pl.multiple_of(me * 512 + c * 128, 128), 128)],
            dctx_send.at[peer, c], dctx_recv.at[me, c], {"tensor": peer},
        )

    def dctx_arrival(peer, c):
        rows = pl.ds(pl.multiple_of(c * 128, 128), 128)
        return remote(
            grads_ctx.at[peer, rows],
            dctx.at[pl.ds(pl.multiple_of(peer * 512 + c * 128, 128), 128)],
            dctx_send.at[peer, c], dctx_recv.at[peer, c], {"tensor": peer},
        )

    def dctx_local(c):
        rows = pl.ds(pl.multiple_of(c * 128, 128), 128)
        return pltpu.make_async_copy(
            grads_ctx.at[me, rows],
            dctx.at[pl.ds(pl.multiple_of(me * 512 + c * 128, 128), 128)],
            local_sem.at[1, c],
        )

    def chunk_step(c, _):
        for peer in order:
            ctx_arrival(peer, c).wait_recv()
        rows = pl.ds(pl.multiple_of(c * CHUNK, CHUNK), CHUNK)
        pair_rows = pl.ds(pl.multiple_of(c * 128, 128), 128)
        context = jnp.concatenate([ctxs[t, pair_rows, :] for t in range(4)], axis=1)
        attended = jnp.concatenate(
            [mm(context, out_a[...], NT), mm(context, out_b[...], NT)], axis=0
        )
        first_sum = tok[rows, :].astype(f32) + attended + vec[4:5]
        scaled_one, inverse_one = norm_rows(first_sum)
        normed = scaled_one * vec[0:1] + vec[1:2]
        low = normed.astype(bf16)
        normed_low[rows, :] = low
        for n in range(4):
            span = slice(512 * n, 512 * n + 512)
            hidden = mm(low, up[:, span]) + shift[:, span]
            cumulative = 0.5 * (1.0 + lax.erf(hidden * 0.7071067811865476))
            active[rows, span] = (hidden * cumulative).astype(bf16)
            slope[:, span] = cumulative + hidden * (
                0.3989422804014327 * jnp.exp(-0.5 * hidden * hidden)
            )
        second_sum = normed + mm(active[rows, :], down[...], NT) + vec[5:6]
        scaled_two, inverse_two = norm_rows(second_sum)
        enc[rows, :] = (scaled_two * vec[2:3] + vec[3:4]).astype(bf16)
        for copy in enc_copies(c):
            copy.start()
        upstream = cot[rows, :].astype(f32)
        second_grad = norm_rows_back(upstream * vec[2:3], scaled_two, inverse_two)
        low_two = second_grad.astype(bf16)
        second_low[rows, :] = low_two
        for n in range(4):
            span = slice(512 * n, 512 * n + 512)
            hgrad[rows, span] = (mm(low_two, down[:, span]) * slope[:, span]).astype(bf16)
        normed_grad = second_grad + mm(hgrad[rows, :], up[...], NT)
        first_grad = norm_rows_back(normed_grad * vec[0:1], scaled_one, inverse_one)
        first[rows, :] = first_grad
        low_one = first_grad.astype(bf16)
        first_a[pair_rows, :] = low_one[0:128]
        first_b[pair_rows, :] = low_one[128:256]
        back = (mm(low_one[0:128], out_a[...]) + mm(low_one[128:256], out_b[...])).astype(bf16)
        for t in range(4):
            grads_ctx[t, pair_rows, :] = back[:, 128 * t : 128 * t + 128]
        for peer in (across, diagonal, sibling):
            dctx_copy(peer, c).start()
        dctx_local(c).start()
        fold = lambda value: jnp.sum(value, axis=0, keepdims=True)
        sums[0:1] += fold(normed_grad * scaled_one)
        sums[1:2] += fold(normed_grad)
        sums[2:3] += fold(upstream * scaled_two)
        sums[3:4] += fold(upstream)
        sums[4:5] += fold(first_grad)
        sums[5:6] += fold(second_grad)
        return 0

    lax.fori_loop(0, CHUNKS, chunk_step, 0)

    ones = jnp.ones((8, OWN_ROWS), bf16)

    def weight_grads(t_of, target, kind):
        for ty in range(2):
            t = t_of(ty)
            lanes = pl.ds(pl.multiple_of(t * 512, 512), 512)
            grad_up = mm(normed_low[...], hgrad[:, lanes], TN).astype(kind)
            grad_down = mm(second_low[...], active[:, lanes], TN).astype(kind)
            part_a = mm(first_a[...], ctxs[t], TN)
            part_b = pltpu.roll(mm(first_b[...], ctxs[t], TN), 64, 1)
            grad_out = jnp.where(
                iota((256, 128), 1) < 64, part_a + part_b, 0.0
            ).astype(kind)
            shift_sum = mm(ones, hgrad[:, lanes])
            for d in range(8):
                j = 2 * d + ty
                block = slice(32 * d, 32 * d + 32)
                for b in range(4):
                    cols = slice(128 * b, 128 * b + 128)
                    target[j, 32 * b : 32 * b + 32, :] = grad_up[block, cols]
                    target[j, 128 + 32 * b : 160 + 32 * b, :] = grad_down[block, cols]
                target[j, 256:288, :] = grad_out[block]
                vector = sums[:, 128 * (d // 4) : 128 * (d // 4) + 128]
                cols = slice(128 * (d // 2), 128 * (d // 2) + 128)
                tail = jnp.where(iota((8, 128), 0) == 6, shift_sum[:, cols], vector)
                target[j, 288:304, :] = jnp.concatenate(
                    [tail, jnp.zeros((8, 128), f32)], axis=0
                ).astype(kind)

    weight_grads(other_t, give, bf16)
    trade = remote(give, take, g_sem.at[0], g_sem.at[1], {"tensor": sibling})
    trade.start()
    for c in range(CHUNKS):
        enc_arrival(across, 0, c).wait_recv()
        enc_arrival(across, 2, c).start()
    weight_grads(mine_t, keep, f32)
    trade.wait_recv()

    def merge(j, _):
        gout[j] = (keep[j] + take[j].astype(f32)).astype(bf16)
        return 0

    lax.fori_loop(0, GROUPS, merge, 0)
    trade.wait_send()
    for copy in weights:
        copy.wait_send()
    for c in range(CHUNKS):
        for peer in order:
            ctx_copy(peer, c).wait_send()
            dctx_copy(peer, c).wait_send()
            dctx_arrival(peer, c).wait_recv()
        dctx_local(c).wait()
        far, near, local = enc_copies(c)
        far.wait_send()
        near.wait_send()
        local.wait()
        enc_arrival(sibling, 1, c).wait_recv()
        enc_arrival(across, 2, c).wait_send()
        enc_arrival(diagonal, 2, c).wait_recv()


def dense(ctxp, half, tokens, cotangent):
    dma = pltpu.SemaphoreType.DMA
    return pl.pallas_call(
        dense_kernel,
        out_shape=(
            jax.ShapeDtypeStruct((PACK_ROWS, 256), bf16),
            jax.ShapeDtypeStruct((PACK_ROWS // 2, 128), bf16),
            jax.ShapeDtypeStruct((OWN_ROWS, 256), f32),
            jax.ShapeDtypeStruct((GROUPS, SHARD_ROWS, 128), bf16),
        ),
        in_specs=[VMEM_SPEC, VMEM_SPEC, ANY_SPEC, ANY_SPEC],
        out_specs=[ANY_SPEC, ANY_SPEC, VMEM_SPEC, VMEM_SPEC],
        scratch_shapes=[
            pltpu.VMEM((GROUPS, SHARD_ROWS, 128), bf16),
            pltpu.VMEM((4, 512, 128), bf16),
            pltpu.VMEM((256, 2048), bf16),
            pltpu.VMEM((256, 2048), bf16),
            pltpu.VMEM((256, 512), bf16),
            pltpu.VMEM((256, 512), bf16),
            pltpu.VMEM((8, 256), f32),
            pltpu.VMEM((1, 2048), f32),
            pltpu.VMEM((OWN_ROWS, 256), bf16),
            pltpu.VMEM((OWN_ROWS, 256), bf16),
            pltpu.VMEM((OWN_ROWS, 256), bf16),
            pltpu.VMEM((4, 512, 128), bf16),
            pltpu.VMEM((OWN_ROWS, 256), bf16),
            pltpu.VMEM((OWN_ROWS, 256), bf16),
            pltpu.VMEM((512, 256), bf16),
            pltpu.VMEM((512, 256), bf16),
            pltpu.VMEM((OWN_ROWS, 2048), bf16),
            pltpu.VMEM((OWN_ROWS, 2048), bf16),
            pltpu.VMEM((CHUNK, 2048), f32),
            pltpu.VMEM((8, 256), f32),
            pltpu.VMEM((GROUPS, SHARD_ROWS, 128), bf16),
            pltpu.VMEM((GROUPS, SHARD_ROWS, 128), bf16),
            pltpu.VMEM((GROUPS, SHARD_ROWS, 128), f32),
            dma((4,)),
            dma((2,)),
            dma((4, CHUNKS)),
            dma((4, CHUNKS)),
            dma((4, CHUNKS)),
            dma((4, CHUNKS)),
            dma((3, CHUNKS)),
            dma((3, CHUNKS)),
            dma((2, CHUNKS)),
            dma((2,)),
        ],
        compiler_params=pltpu.CompilerParams(
            collective_id=1, has_side_effects=True, vmem_limit_bytes=56 * 2**20
        ),
        cost_estimate=pl.CostEstimate(
            flops=7 * 10**9, bytes_accessed=8 * 10**6, transcendentals=4 * 10**6
        ),
    )(ctxp, half, tokens, cotangent)


def tail_kernel(
    gq, gkv, tok, pos, w3, first,
    tg, gin,
    wall, s1_send, s1_recv, s2_send, s2_recv, s3_send, s3_recv, mine,
    in_send, in_recv,
    s_send, s_recv, t_send, t_recv, local_sem, i_send, i_recv,
):
    me = lax.axis_index("tensor")
    rank = lax.axis_index("dp")
    core = lax.rem(me, 2)
    sibling = me + 1 - 2 * core
    across = lax.rem(me + 2, 4)
    diagonal = lax.rem(sibling + 2, 4)
    peers = [lax.rem(rank + k, 8) for k in range(1, 8)]
    ready = greet(
        [{"tensor": sibling}, {"tensor": across}] + [{"dp": peer} for peer in peers]
    )
    lane = iota((256, 128), 1)
    wall[:, 0:128] = w3[0]
    wall[:, 128:256] = jnp.where(
        lane < 64, w3[1].astype(f32), pltpu.roll(w3[2].astype(f32), 64, 1)
    ).astype(bf16)

    def chunk_at(c):
        return pl.ds(pl.multiple_of(c * CHUNK, CHUNK), CHUNK)

    def rows_of(owner, c):
        return pl.ds(pl.multiple_of(owner * OWN_ROWS + c * CHUNK, CHUNK), CHUNK)

    def partial(owner, c):
        rows = rows_of(owner, c)
        return mm(jnp.concatenate([gq[rows, :], gkv[rows, :]], axis=1), wall[...], NT)

    def step(kind, source, target, c, peer):
        return remote(
            source.at[chunk_at(c)], target.at[chunk_at(c)],
            s_send.at[kind, c], s_recv.at[kind, c], {"tensor": peer},
        )

    one_copy = lambda c: step(0, s1_send, s1_recv, c, sibling)
    two_copy = lambda c: step(1, s2_send, s2_recv, c, across)
    three_copy = lambda c: step(2, s3_send, s3_recv, c, sibling)

    def first_stage(c, _):
        s1_send[chunk_at(c), :] = partial(diagonal, c).astype(bf16)
        one_copy(c).start()
        return 0

    def second_stage(c, _):
        value = partial(across, c)
        one_copy(c).wait_recv()
        s2_send[chunk_at(c), :] = (value + s1_recv[chunk_at(c), :].astype(f32)).astype(bf16)
        two_copy(c).start()
        return 0

    def third_stage(c, _):
        s3_send[chunk_at(c), :] = partial(sibling, c).astype(bf16)
        three_copy(c).start()
        return 0

    ready()
    lax.fori_loop(0, CHUNKS, first_stage, 0)
    lax.fori_loop(0, CHUNKS, second_stage, 0)
    lax.fori_loop(0, CHUNKS, third_stage, 0)

    def inward_step(i, carry):
        left, right, total = carry
        rows = pl.ds(pl.multiple_of(i * 1024, 1024), 1024)
        token = tok[rows, :]
        query_in = (token.astype(f32) + pos[rows, :].astype(f32)).astype(bf16)
        both = jnp.concatenate([gq[rows, :], gkv[rows, :]], axis=1)
        left = left + mm(query_in, both, TN)
        right = right + mm(token, gkv[rows, :], TN)
        total = total + mm(jnp.ones((8, 1024), bf16), both)
        return left, right, total

    left, right, total = lax.fori_loop(
        0, 4, inward_step,
        (jnp.zeros((256, 256), f32), jnp.zeros((256, 128), f32), jnp.zeros((8, 256), f32)),
    )
    joined = jnp.concatenate([jnp.where(lane < 64, left[:, 0:128], right), left[:, 128:256]], 1)
    for d in range(8):
        in_send[d, 0:32, :] = joined[32 * d : 32 * d + 32]
        in_send[d, 32:40, :] = total
    in_copies = []
    for k, peer in enumerate(peers):
        copy = remote(
            in_send.at[peer], in_recv.at[rank], i_send.at[k], i_recv.at[rank], {"dp": peer}
        )
        copy.start()
        in_copies.append(copy)

    def out_copies(c):
        source = mine.at[chunk_at(c)]
        rows = rows_of(me, c)
        return (
            remote(source, tg.at[rows], t_send.at[0, c], t_recv.at[0, c], {"tensor": across}),
            remote(source, tg.at[rows], t_send.at[1, c], t_recv.at[1, c], {"tensor": sibling}),
            pltpu.make_async_copy(source, tg.at[rows], local_sem.at[c]),
        )

    def arrival(owner, kind, c):
        rows = rows_of(owner, c)
        return remote(
            tg.at[rows], tg.at[rows], t_send.at[2, c], t_recv.at[kind, c], {"tensor": sibling}
        )

    def fourth_stage(c, _):
        value = partial(me, c) + first[chunk_at(c), :]
        three_copy(c).wait_recv()
        value = value + s3_recv[chunk_at(c), :].astype(f32)
        two_copy(c).wait_recv()
        value = value + s2_recv[chunk_at(c), :].astype(f32)
        mine[chunk_at(c), :] = value.astype(bf16)
        for copy in out_copies(c):
            copy.start()
        return 0

    lax.fori_loop(0, CHUNKS, fourth_stage, 0)

    gathered = in_send[rank]
    for peer in peers:
        remote(
            in_send.at[peer], in_recv.at[peer], i_send.at[0], i_recv.at[peer], {"dp": peer}
        ).wait_recv()
        gathered = gathered + in_recv[peer]
    gin[...] = gathered

    for c in range(CHUNKS):
        arrival(across, 0, c).wait_recv()
        arrival(across, 2, c).start()
    for copy in in_copies:
        copy.wait_send()
    for c in range(CHUNKS):
        one_copy(c).wait_send()
        two_copy(c).wait_send()
        three_copy(c).wait_send()
        far, near, local = out_copies(c)
        far.wait_send()
        near.wait_send()
        local.wait()
        arrival(sibling, 1, c).wait_recv()
        arrival(across, 2, c).wait_send()
        arrival(diagonal, 2, c).wait_recv()


def tail(gq, gkv, tokens, positions, w3, first):
    dma = pltpu.SemaphoreType.DMA
    return pl.pallas_call(
        tail_kernel,
        out_shape=(
            jax.ShapeDtypeStruct((PACK_ROWS, 256), bf16),
            jax.ShapeDtypeStruct((40, 256), f32),
        ),
        in_specs=[VMEM_SPEC] * 6,
        out_specs=[ANY_SPEC, VMEM_SPEC],
        scratch_shapes=[pltpu.VMEM((256, 256), bf16)]
        + [pltpu.VMEM((OWN_ROWS, 256), bf16)] * 7
        + [
            pltpu.VMEM((8, 40, 256), f32),
            pltpu.VMEM((8, 40, 256), f32),
            dma((3, CHUNKS)),
            dma((3, CHUNKS)),
            dma((3, CHUNKS)),
            dma((3, CHUNKS)),
            dma((CHUNKS,)),
            dma((7,)),
            dma((8,)),
        ],
        compiler_params=pltpu.CompilerParams(
            collective_id=2, has_side_effects=True, vmem_limit_bytes=48 * 2**20
        ),
        cost_estimate=pl.CostEstimate(
            flops=3 * 10**9, bytes_accessed=16 * 10**6, transcendentals=0
        ),
    )(gq, gkv, tokens, positions, w3, first)


def update_kernel(pieces, gin, *refs):
    masters, firsts, seconds = refs[0:7], refs[7:14], refs[14:21]
    grads, news, lows, moms, varis = (
        refs[21:28], refs[28:35], refs[35:39], refs[39:46], refs[46:53],
    )
    me = lax.axis_index("dp")

    def add(j, total):
        return total + pieces[j].astype(f32)

    total = lax.fori_loop(0, GROUPS, add, jnp.zeros((SHARD_ROWS, 128), f32))
    wide = gin[...]
    small = total[288:296]
    vec_grad = pltpu.roll(small, lax.rem(128 - lax.rem(me, 4) * 32, 128), 1)[0:6, 0:32]
    shift_grad = pltpu.roll(small, lax.rem(128 - lax.rem(me, 2) * 64, 128), 1)[6:7, 0:64]
    off_q = pltpu.roll(wide[32:40, 0:128], lax.rem(128 - me * 8, 128), 1)
    off_v = pltpu.roll(wide[32:40, 128:256], 64 - me * 8, 1)
    off_grad = jnp.where(iota((8, 128), 0) == 0, off_q, off_v)[0:2, 0:8]
    left, right = wide[0:32, 0:128], wide[0:32, 128:256]
    inward_grads = (left[:, 0:64], right[:, 0:64], pltpu.roll(left, 64, 1)[:, 0:64])
    joined = lambda base: jnp.concatenate(
        [total[base + 32 * b : base + 32 * b + 32] for b in range(4)], axis=1
    )
    plain = (None, total[256:288, 0:64], joined(0), joined(128), vec_grad, off_grad, shift_grad)

    def apply(index, at, gradient):
        new, momentum, variance = adamw(
            masters[index][at], gradient, firsts[index][at], seconds[index][at],
            step_rates[index],
        )
        grads[index][at] = gradient
        news[index][at] = new
        moms[index][at] = momentum
        varis[index][at] = variance
        if index < 4:
            lows[index][at] = new.astype(bf16)

    for which in range(3):
        apply(0, which, inward_grads[which])
    for index in range(1, 7):
        apply(index, Ellipsis, plain[index])


def update(pieces, gin, masters, firsts, seconds):
    shapes = [m.shape for m in masters]
    of = lambda kind, count: [jax.ShapeDtypeStruct(s, kind) for s in shapes[:count]]
    out = of(f32, 7) + of(f32, 7) + of(bf16, 4) + of(f32, 7) + of(f32, 7)
    return pl.pallas_call(
        update_kernel,
        out_shape=out,
        in_specs=[VMEM_SPEC] * 23,
        out_specs=[VMEM_SPEC] * len(out),
        compiler_params=pltpu.CompilerParams(vmem_limit_bytes=32 * 2**20),
    )(pieces, gin, *masters, *firsts, *seconds)


def exchange(pieces):
    groups = [[4 * d + 2 * y + c for d in range(8) for y in range(2)] for c in range(2)]
    return lax.all_to_all(
        pieces, ("dp", "tensor"), 0, 0, axis_index_groups=groups, tiled=True
    )


def turned(group):
    inward, outward, upward, downward, vectors, offsets, shifts = group
    return [inward, outward.T, upward, downward.T, vectors, offsets, shifts.reshape(1, -1)]


def returned(group):
    if len(group) == 4:
        return [group[0], group[1].T, group[2], group[3].T]
    inward, outward, upward, downward, vectors, offsets, shifts = group
    return [inward, outward.T, upward, downward.T, vectors, offsets, shifts.reshape(-1)]


def body_pods(tokens, positions, segment_ids, pad_flags, cotangent, *state):
    masters, firsts, seconds = (turned(state[7 * i : 7 * i + 7]) for i in range(3))
    inward, out_t, upward, down_t, vectors, offsets, shifts = masters
    pack, w3, off = gather_weights(upward, down_t, out_t, vectors, shifts, inward, offsets)
    half = exchange(pack)
    ctxp, *saved = attend_forward(tokens, positions, w3, off, segment_ids, pad_flags)
    encoded, dctx, first, gout = dense(ctxp, half, tokens, cotangent)
    pieces = exchange(gout)
    gq, gkv = attend_backward(dctx, *saved)
    tg, gin = tail(gq, gkv, tokens, positions, w3, first)
    outs = update(pieces, gin, masters, firsts, seconds)
    grads, news, lows, moms, varis = outs[:7], outs[7:14], outs[14:18], outs[18:25], outs[25:]
    return (
        encoded,
        tg.astype(f32),
        *returned(grads),
        *returned(news),
        *returned(lows),
        *returned(moms),
        *returned(varis),
    )


def body(
    tokens,
    positions,
    segment_ids,
    pad_flags,
    cotangent,
    inward,
    outward,
    upward,
    downward,
    vectors,
    offsets,
    shifts,
    first_inward,
    first_outward,
    first_upward,
    first_downward,
    first_vectors,
    first_offsets,
    first_shifts,
    second_inward,
    second_outward,
    second_upward,
    second_downward,
    second_vectors,
    second_offsets,
    second_shifts,
):
    w_inward, w_outward, w_upward, w_downward, vector_low, offset_low, shift_low = (
        lax.all_gather(inward.astype(jnp.bfloat16), "dp", axis=1, tiled=True),
        lax.all_gather(outward.astype(jnp.bfloat16), "dp", axis=1, tiled=True),
        lax.all_gather(upward.astype(jnp.bfloat16), "dp", axis=0, tiled=True),
        lax.all_gather(downward.astype(jnp.bfloat16), "dp", axis=1, tiled=True),
        lax.all_gather(vectors.astype(jnp.bfloat16), "dp", axis=1, tiled=True),
        lax.all_gather(offsets.astype(jnp.bfloat16), "dp", axis=1, tiled=True),
        lax.all_gather(shifts.astype(jnp.bfloat16), "dp", axis=0, tiled=True),
    )
    vector_wide = vector_low.astype(jnp.float32)
    offset_wide = offset_low.astype(jnp.float32)
    shift_wide = shift_low.astype(jnp.float32)
    input_wide = tokens.astype(jnp.float32)
    query_in = (input_wide + positions.astype(jnp.float32)).astype(jnp.bfloat16)
    w_lanes = jnp.pad(w_inward, ((0, 0), (0, 0), (0, 64)))
    off_lanes = jnp.pad(offset_wide, ((0, 6), (0, 64)))
    packed, *saved = attend_forward(
        tokens, positions, w_lanes, off_lanes, segment_ids, pad_flags
    )
    pairs = packed.reshape(16, 128, 2, 64)
    context_low = pairs.transpose(0, 2, 1, 3).reshape(PACK_ROWS, 64)
    first_sum = input_wide + summed(product(context_low, w_outward)) + vector_wide[4]
    normed, scaled_one, inverse_one = norm_forward(first_sum, vector_wide[0], vector_wide[1])
    normed_low = normed.astype(jnp.bfloat16)
    hidden = product(normed_low, w_upward) + shift_wide
    unit_value, unit_back = jax.vjp(smooth_unit, hidden)
    active = unit_value.astype(jnp.bfloat16)
    second_sum = normed + summed(product(active, w_downward)) + vector_wide[5]
    result, scaled_two, inverse_two = norm_forward(second_sum, vector_wide[2], vector_wide[3])
    encoded = result.astype(jnp.bfloat16)
    upstream = cotangent.astype(jnp.float32)
    second_grad, gain_two, shift_two = norm_backward(
        upstream, scaled_two, inverse_two, vector_wide[2]
    )
    down_low = second_grad.astype(jnp.bfloat16)
    grad_downward = product_left(active, down_low)
    hidden_low = unit_back(product_right(down_low, w_downward))[0].astype(jnp.bfloat16)
    grad_upward = product_left(normed_low, hidden_low)
    grad_shifts = jnp.sum(hidden_low.astype(jnp.float32), axis=0)
    normed_grad = second_grad + summed(product_right(hidden_low, w_upward))
    first_grad, gain_one, shift_one = norm_backward(
        normed_grad, scaled_one, inverse_one, vector_wide[0]
    )
    first_low = first_grad.astype(jnp.bfloat16)
    grad_outward = product_left(context_low, first_low)
    context_grad = product_right(first_low, w_outward).astype(jnp.bfloat16)
    halves = context_grad.reshape(16, 2, 128, 64)
    gq, gkv = attend_backward(
        halves.transpose(0, 2, 1, 3).reshape(2048, 128), *saved
    )
    query_grad, key_grad, value_grad = gq[:, :64], gkv[:, :64], gkv[:, 64:]
    grad_inward = jnp.stack(
        [
            product_left(query_in, query_grad),
            product_left(query_in, key_grad),
            product_left(tokens, value_grad),
        ]
    )
    grad_offsets = jnp.stack(
        [
            jnp.sum(query_grad.astype(jnp.float32), axis=0),
            jnp.sum(value_grad.astype(jnp.float32), axis=0),
        ]
    )
    input_part = (
        product_right(query_grad, w_inward[0])
        + product_right(key_grad, w_inward[1])
        + product_right(value_grad, w_inward[2])
    )
    input_grad = first_grad + summed(input_part)
    grad_vectors = jnp.stack(
        [
            gain_one,
            shift_one,
            gain_two,
            shift_two,
            jnp.sum(first_grad, axis=0),
            jnp.sum(second_grad, axis=0),
        ]
    )
    reduced = (
        lax.psum_scatter(grad_inward, "dp", scatter_dimension=1, tiled=True),
        lax.psum_scatter(grad_outward, "dp", scatter_dimension=1, tiled=True),
        lax.psum_scatter(grad_upward, "dp", scatter_dimension=0, tiled=True),
        lax.psum_scatter(grad_downward, "dp", scatter_dimension=1, tiled=True),
        lax.psum_scatter(grad_vectors, "dp", scatter_dimension=1, tiled=True),
        lax.psum_scatter(grad_offsets, "dp", scatter_dimension=1, tiled=True),
        lax.psum_scatter(grad_shifts, "dp", scatter_dimension=0, tiled=True),
    )
    masters = (inward, outward, upward, downward, vectors, offsets, shifts)
    firsts = (
        first_inward,
        first_outward,
        first_upward,
        first_downward,
        first_vectors,
        first_offsets,
        first_shifts,
    )
    seconds = (
        second_inward,
        second_outward,
        second_upward,
        second_downward,
        second_vectors,
        second_offsets,
        second_shifts,
    )
    updated = []
    momenta = []
    variances = []
    for master, gradient, old_first, old_second, step_rate in zip(
        masters, reduced, firsts, seconds, step_rates
    ):
        new_master, momentum, variance = adamw(master, gradient, old_first, old_second, step_rate)
        updated.append(new_master)
        momenta.append(momentum)
        variances.append(variance)
    return (
        encoded,
        input_grad,
        reduced[0],
        reduced[1],
        reduced[2],
        reduced[3],
        reduced[4],
        reduced[5],
        reduced[6],
        updated[0],
        updated[1],
        updated[2],
        updated[3],
        updated[4],
        updated[5],
        updated[6],
        updated[0].astype(jnp.bfloat16),
        updated[1].astype(jnp.bfloat16),
        updated[2].astype(jnp.bfloat16),
        updated[3].astype(jnp.bfloat16),
        momenta[0],
        momenta[1],
        momenta[2],
        momenta[3],
        momenta[4],
        momenta[5],
        momenta[6],
        variances[0],
        variances[1],
        variances[2],
        variances[3],
        variances[4],
        variances[5],
        variances[6],
    )


def solution(mesh):
    in_specs = (
        P("dp", None),
        P("dp", None),
        P("dp", None),
        P("dp", None),
        P("dp", None),
        P(None, "dp", "tensor"),
        P("tensor", "dp"),
        P("dp", "tensor"),
        P("tensor", "dp"),
        P(None, "dp"),
        P(None, ("tensor", "dp")),
        P(("tensor", "dp")),
        P(None, "dp", "tensor"),
        P("tensor", "dp"),
        P("dp", "tensor"),
        P("tensor", "dp"),
        P(None, "dp"),
        P(None, ("tensor", "dp")),
        P(("tensor", "dp")),
        P(None, "dp", "tensor"),
        P("tensor", "dp"),
        P("dp", "tensor"),
        P("tensor", "dp"),
        P(None, "dp"),
        P(None, ("tensor", "dp")),
        P(("tensor", "dp")),
    )
    out_specs = (
        P("dp", None),
        P("dp", None),
        P(None, "dp", "tensor"),
        P("tensor", "dp"),
        P("dp", "tensor"),
        P("tensor", "dp"),
        P(None, "dp"),
        P(None, ("tensor", "dp")),
        P(("tensor", "dp")),
        P(None, "dp", "tensor"),
        P("tensor", "dp"),
        P("dp", "tensor"),
        P("tensor", "dp"),
        P(None, "dp"),
        P(None, ("tensor", "dp")),
        P(("tensor", "dp")),
        P(None, "dp", "tensor"),
        P("tensor", "dp"),
        P("dp", "tensor"),
        P("tensor", "dp"),
        P(None, "dp", "tensor"),
        P("tensor", "dp"),
        P("dp", "tensor"),
        P("tensor", "dp"),
        P(None, "dp"),
        P(None, ("tensor", "dp")),
        P(("tensor", "dp")),
        P(None, "dp", "tensor"),
        P("tensor", "dp"),
        P("dp", "tensor"),
        P("tensor", "dp"),
        P(None, "dp"),
        P(None, ("tensor", "dp")),
        P(("tensor", "dp")),
    )
    pods = mesh.shape["dp"] == 8 and mesh.shape["tensor"] == 4
    chosen = body_pods if pods else body
    return jax.shard_map(chosen, mesh=mesh, in_specs=in_specs, out_specs=out_specs, check_vma=False)
```

```python
import functools
import jax
import jax.numpy as jnp
from jax import lax
from jax.experimental import pallas as pl
from jax.experimental.pallas import tpu as pltpu
from jax.sharding import PartitionSpec as P

HEAD_DIM = 32
MIB = 2**20
LIMIT_GATHER = 58 * MIB
LIMIT_FORWARD = 58 * MIB
LIMIT_DENSE = 58 * MIB
LIMIT_BACKWARD = 58 * MIB
LIMIT_TAIL = 58 * MIB
LIMIT_UPDATE = 58 * MIB
PACK_ROWS = 4096
IMAGES = 5
SPAN = PACK_ROWS + 512
BACK_QUERY = (1024, 512, 256)
BACK_KEY = (1024, 512, 256)
FORWARD_QUERY = (1024, 512, 256)
FORWARD_KEY = (1024, 512, 256)
LOG_SCALE = HEAD_DIM**-0.5 * 1.4426950408889634
FENCE = 2.0**100
LARGE = 2.0**100
SMALL = 2.0**-60
NN = (((1,), (0,)), ((), ()))
NT = (((1,), (1,)), ((), ()))
TN = (((0,), (0,)), ((), ()))
bf16 = jnp.bfloat16
f32 = jnp.float32


def mm(left, right, dims=NN):
    return lax.dot_general(left, right, dims, preferred_element_type=f32)


def iota(shape, dim):
    return lax.broadcasted_iota(jnp.int32, shape, dim)


def plan(length, sizes):
    out = []
    offset = 0
    least = sizes[-1]
    for size in sizes:
        left = jnp.maximum(length - offset, 0)
        count = (left + least - 1) // size
        out.append((size, offset, count))
        offset = offset + count * size
    return out


def twice(step):
    def both(i, carry):
        return step(2 * i + 1, step(2 * i, carry))

    return both


def pieces_of(value):
    one = value.astype(bf16).astype(f32)
    rest = value - one
    two = rest.astype(bf16).astype(f32)
    return one, two, rest - two


def attend_forward_kernel(
    tok_hbm, pos_hbm, w3, off, seg, pad,
    packed, ctx_hbm, qa_hbm, qw_hbm, ka_hbm, va_hbm, rank, bounds,
    tok, pos, raw, ctx_pair, qa, qw, ka, va, wqd, wkd, compact, dst, load_sem, save_sem,
):
    loads = []
    for part in range(4):
        rows = pl.ds(1024 * part, 1024)
        for which, (source, target) in enumerate(((tok_hbm, tok), (pos_hbm, pos))):
            copy = pltpu.make_async_copy(
                source.at[rows], target.at[rows], load_sem.at[2 * part + which]
            )
            copy.start()
            loads.append(copy)
    lane = iota((256, 128), 1)
    for which, spread in ((0, wqd), (1, wkd)):
        base = w3[which].astype(f32)
        left = pltpu.roll(base, 32, 1)
        right = pltpu.roll(base, 96, 1)
        spread[:, :128] = jnp.where(lane < 32, base, jnp.where(lane < 64, left, 0.0)).astype(bf16)
        spread[:, 128:] = jnp.where(lane < 32, right, jnp.where(lane < 64, base, 0.0)).astype(bf16)
    lane8 = iota((8, 128), 1)
    off_rows = off[...]
    off_left = pltpu.roll(off_rows, 32, 1)
    off_right = pltpu.roll(off_rows, 96, 1)
    q_bias = jnp.concatenate(
        [
            jnp.where(lane8 < 32, off_rows, jnp.where(lane8 < 64, off_left, 0.0))[0:1],
            jnp.where(lane8 < 32, off_right, jnp.where(lane8 < 64, off_rows, 0.0))[0:1],
        ],
        axis=1,
    )
    v_bias = jnp.where(lane8 < 64, off_rows, 0.0)[1:2]

    segment = seg[...]
    open_key = jnp.where(pad[...] == 0, 1.0, 0.0)
    grid_row = iota((32, 128), 0)
    before = (iota((128, 128), 0) < iota((128, 128), 1)).astype(bf16)
    in_row = mm(open_key.astype(bf16), before)
    row_total = jnp.broadcast_to(jnp.sum(open_key, axis=1, keepdims=True), (32, 128))
    above = (iota((32, 32), 1) < iota((32, 32), 0)).astype(bf16)
    place = (in_row + mm(above, row_total.astype(bf16))).astype(jnp.int32)
    place = jnp.where(open_key > 0.5, place, -1)
    for r in range(32):
        rank[r, :, :] = place[r : r + 1, :]
    for s in range(IMAGES + 1):
        if s == 0:
            bounds[0] = 0
            bounds[8] = 0
        else:
            low = (segment < s).astype(f32)
            bounds[s] = jnp.sum(low).astype(jnp.int32)
            bounds[8 + s] = jnp.sum(low * open_key).astype(jnp.int32)
    for i in range(16):
        dst[i] = jnp.sum(jnp.where(grid_row < 2 * i, open_key, 0.0)).astype(jnp.int32)
    for i in range(16):
        bounds[16 + i] = dst[i]
    total = bounds[8 + IMAGES]

    lane_row = iota((1, 128), 1)
    q_from = jnp.full((1, 128), SPAN, jnp.int32)
    q_to = jnp.full((1, 128), SPAN, jnp.int32)
    k_from = jnp.full((1, 128), SPAN, jnp.int32)
    k_to = jnp.full((1, 128), SPAN, jnp.int32)
    for s in range(IMAGES):
        at = lane_row == 64 + s
        q_from = jnp.where(at, bounds[s], q_from)
        q_to = jnp.where(at, bounds[s + 1], q_to)
        k_from = jnp.where(at, bounds[8 + s], k_from)
        k_to = jnp.where(at, bounds[9 + s], k_to)

    compact[pl.ds(0, 16), :] = jnp.zeros((16, 512), bf16)
    qa[:, pl.ds(PACK_ROWS, SPAN - PACK_ROWS), :] = jnp.zeros((2, SPAN - PACK_ROWS, 128), bf16)
    qw[pl.ds(PACK_ROWS, SPAN - PACK_ROWS), :] = jnp.zeros((SPAN - PACK_ROWS, 128), bf16)

    lane_q = iota((256, 128), 1)
    row_q = iota((256, 128), 0)

    def project(i, _):
        first = pl.multiple_of(i * 256, 256)
        rows = pl.ds(first, 256)
        token = tok[rows, :]
        query_in = (token.astype(f32) + pos[rows, :].astype(f32)).astype(bf16)
        both = (mm(query_in, wqd[...]) + q_bias).astype(bf16).astype(f32)
        here = row_q + first
        outside = (here < q_from) | (here >= q_to)
        feature = jnp.where(
            lane_q < 64 + IMAGES, jnp.where(outside, 1.0, 0.0), jnp.where(lane_q == 69, 1.0, 0.0)
        )
        for h in range(2):
            exact = both[:, 128 * h : 128 * h + 128] * LOG_SCALE
            high = exact.astype(bf16).astype(f32)
            qa[h, rows, :] = jnp.where(
                lane_q < 32, high, jnp.where(lane_q < 64, exact - high, feature)
            ).astype(bf16)
        qw[rows, :] = jnp.where(
            lane_q < 32, both[:, :128], jnp.where(lane_q < 64, both[:, 128:], 0.0)
        ).astype(bf16)
        start = dst[i]
        aligned = pl.multiple_of((start // 16) * 16, 16)
        places = jnp.concatenate([rank[2 * i], rank[2 * i + 1]], axis=1)
        hot = jnp.where(iota((272, 256), 0) + aligned == places, 1.0, 0.0).astype(bf16)
        moved = mm(hot, jnp.concatenate([query_in, token], axis=1)).astype(bf16)
        head = pl.ds(aligned, 16)
        compact[head, :] = compact[head, :] + moved[:16]
        compact[pl.ds(pl.multiple_of(aligned + 16, 16), 256), :] = moved[16:]
        return 0

    for part in range(4):
        loads[2 * part].wait()
        loads[2 * part + 1].wait()
        lax.fori_loop(2 * part, 2 * part + 2, twice(project), 0)

    lane_k = iota((512, 128), 1)
    row_k = iota((512, 128), 0)

    def project_keys(i, _):
        first = pl.multiple_of(i * 512, 512)
        rows = pl.ds(first, 512)
        here = row_k + first
        real = here < total
        both = mm(compact[rows, 0:256], wkd[...])
        value = mm(compact[rows, 256:512], w3[2]) + v_bias
        value = jnp.where(real, value, 0.0)
        inside = (here >= k_from) & (here < k_to)
        feature = jnp.where(inside, -FENCE, 0.0)
        feature = jnp.where(lane_k == 69, jnp.where(real, 0.0, -FENCE), feature)
        for h in range(2):
            spot = (lane_k >= 70 + 3 * h) & (lane_k < 73 + 3 * h)
            key = jnp.where(real, both[:, 128 * h : 128 * h + 128], 0.0)
            ka[h, rows, :] = jnp.where(
                lane_k < 64, key, jnp.where(spot, 1.0, feature)
            ).astype(bf16)
        va[0, rows, :] = jnp.where(
            lane_k < 32, value, jnp.where(lane_k < 35, 1.0, 0.0)
        ).astype(bf16)
        va[1, rows, :] = jnp.where(
            lane_k < 3, 1.0, jnp.where((lane_k >= 32) & (lane_k < 64), value, 0.0)
        ).astype(bf16)
        return 0

    lax.fori_loop(0, (total + 767) // 512, project_keys, 0)
    saves = [
        pltpu.make_async_copy(source, target, save_sem.at[n])
        for n, (source, target) in enumerate(
            ((qw, qw_hbm), (ka, ka_hbm), (va, va_hbm), (qa, qa_hbm), (ctx_pair, ctx_hbm))
        )
    ]
    for copy in saves[:3]:
        copy.start()

    def per_segment(safe, s, _):
        q_start, q_end = bounds[s], bounds[s + 1]
        k_start, k_end = bounds[8 + s], bounds[9 + s]
        q_first = (q_start // 16) * 16
        k_first = (k_start // 16) * 16

        def per_query(size, base, i, _):
            q_row = pl.multiple_of(base + i * size, 16)
            q_rows = pl.ds(q_row, size)
            head = pl.ds(q_row, 16)
            kept = iota((16, 128), 0) + q_row < q_start
            olds = [raw[h, head, :] for h in range(2)]
            for h in range(2):
                raw[h, q_rows, :] = jnp.zeros((size, 128), f32)

            def per_key(tops, span, first_key, j, _):
                k_rows = pl.ds(pl.multiple_of(first_key + j * span, 16), span)
                for h in range(2):
                    score = mm(qa[h, q_rows, :], ka[h, k_rows, :], NT)
                    if tops is not None:
                        score = score - tops[h]
                    weight = jnp.exp2(score).astype(bf16)
                    raw[h, q_rows, :] += mm(weight, va[h, k_rows, :])
                return 0

            def peak(j, tops):
                k_rows = pl.ds(pl.multiple_of(k_first + j * 256, 16), 256)
                out = []
                for h in range(2):
                    score = mm(qa[h, q_rows, :], ka[h, k_rows, :], NT)
                    out.append(jnp.maximum(tops[h], jnp.max(score, axis=1, keepdims=True)))
                return tuple(out)

            if safe:
                steps = (k_end - k_first + 255) // 256
                low = jnp.full((size, 1), -3.0e38, f32)
                tops = lax.fori_loop(0, steps, peak, (low, low))
                lane = iota((size, 128), 1)
                raw[0, q_rows, :] = jnp.where(
                    lane == 64, tops[0], jnp.where(lane == 65, tops[1], 0.0)
                )
                lax.fori_loop(0, steps, functools.partial(per_key, tops, 256, k_first), 0)
            else:
                for span, offset, count in plan(k_end - k_first, FORWARD_KEY):
                    lax.fori_loop(
                        0, count, functools.partial(per_key, None, span, k_first + offset), 0
                    )
            for h in range(2):
                raw[h, head, :] = jnp.where(kept, olds[h], raw[h, head, :])
            return 0

        for size, offset, count in plan(q_end - q_first, FORWARD_QUERY):
            lax.fori_loop(0, count, functools.partial(per_query, size, q_first + offset), 0)
        return 0

    lax.fori_loop(0, IMAGES, functools.partial(per_segment, False), 0)

    def extremes(i, carry):
        rows = pl.ds(pl.multiple_of(i * 512, 512), 512)
        lane = iota((512, 128), 1)
        both = jnp.where(lane == 32, raw[0, rows, :], jnp.where(lane == 0, raw[1, rows, :], 1.0))
        return (
            jnp.maximum(carry[0], jnp.max(both, axis=0, keepdims=True)),
            jnp.minimum(carry[1], jnp.min(both, axis=0, keepdims=True)),
        )

    one_row = jnp.ones((1, 128), f32)
    most, least = lax.fori_loop(0, 8, extremes, (one_row, one_row))
    fine = (jnp.max(most) < LARGE) & (jnp.min(least) > SMALL)

    @pl.when(jnp.logical_not(fine))
    def _():
        lax.fori_loop(0, IMAGES, functools.partial(per_segment, True), 0)

    def close(b, _):
        rows = pl.ds(pl.multiple_of(b * 256, 256), 256)
        pair_rows = pl.ds(pl.multiple_of(b * 128, 128), 128)
        lane = iota((256, 128), 1)
        zero, one = raw[0, rows, :], raw[1, rows, :]
        l_zero = jnp.broadcast_to(zero[:, 32:33], (256, 128))
        l_one = jnp.broadcast_to(one[:, 0:1], (256, 128))
        lower = lane < 32
        joined = jnp.where(lower, zero, one) / jnp.where(lower, l_zero, l_one)
        early = lane < 73
        shift = jnp.where(
            early,
            jnp.broadcast_to(zero[:, 64:65], (256, 128)),
            jnp.broadcast_to(zero[:, 65:66], (256, 128)),
        )
        parts = pieces_of(-(shift + jnp.log2(jnp.where(early, l_zero, l_one))))
        for h in range(2):
            at = 70 + 3 * h
            value = qa[h, rows, :].astype(f32)
            for n in range(3):
                value = jnp.where(lane == at + n, parts[n], value)
            qa[h, rows, :] = value.astype(bf16)
        pair = jnp.where(
            iota((128, 128), 1) < 64, joined[0:128], pltpu.roll(joined[128:256], 64, 1)
        )
        ctx_pair[pair_rows, :] = pair
        packed[pair_rows, :] = pair.astype(bf16)
        return 0

    lax.fori_loop(0, 8, twice(close), 0)
    for copy in saves[3:]:
        copy.start()
    for copy in saves:
        copy.wait()


VMEM_SPEC = pl.BlockSpec(memory_space=pltpu.VMEM)
SMEM_SPEC = pl.BlockSpec(memory_space=pltpu.SMEM)
ANY_SPEC = pl.BlockSpec(memory_space=pl.ANY)


def attend_forward(tokens, positions, w3, off, segment, padding):
    return pl.pallas_call(
        attend_forward_kernel,
        out_shape=(
            jax.ShapeDtypeStruct((2048, 128), bf16),
            jax.ShapeDtypeStruct((2048, 128), f32),
            jax.ShapeDtypeStruct((2, SPAN, 128), bf16),
            jax.ShapeDtypeStruct((SPAN, 128), bf16),
            jax.ShapeDtypeStruct((2, SPAN, 128), bf16),
            jax.ShapeDtypeStruct((2, SPAN, 128), bf16),
            jax.ShapeDtypeStruct((32, 1, 128), jnp.int32),
            jax.ShapeDtypeStruct((32,), jnp.int32),
        ),
        in_specs=[ANY_SPEC] * 2 + [VMEM_SPEC] * 4,
        out_specs=[VMEM_SPEC] + [ANY_SPEC] * 5 + [VMEM_SPEC, SMEM_SPEC],
        scratch_shapes=[
            pltpu.VMEM((PACK_ROWS, 256), bf16),
            pltpu.VMEM((PACK_ROWS, 256), bf16),
            pltpu.VMEM((2, SPAN, 128), f32),
            pltpu.VMEM((2048, 128), f32),
            pltpu.VMEM((2, SPAN, 128), bf16),
            pltpu.VMEM((SPAN, 128), bf16),
            pltpu.VMEM((2, SPAN, 128), bf16),
            pltpu.VMEM((2, SPAN, 128), bf16),
            pltpu.VMEM((256, 256), bf16),
            pltpu.VMEM((256, 256), bf16),
            pltpu.VMEM((SPAN, 512), bf16),
            pltpu.SMEM((16,), jnp.int32),
            pltpu.SemaphoreType.DMA((8,)),
            pltpu.SemaphoreType.DMA((5,)),
        ],
        compiler_params=pltpu.CompilerParams(vmem_limit_bytes=LIMIT_FORWARD),
        cost_estimate=pl.CostEstimate(
            flops=20 * 10**9, bytes_accessed=20 * 10**6, transcendentals=10**7
        ),
    )(tokens, positions, w3, off, segment.reshape(32, 128), padding.reshape(32, 128))


def attend_backward_kernel(
    packed, ctx_hbm, qa_hbm, qw_hbm, ka_hbm, va_hbm, rank, bounds, done_rows,
    gq, gkv, copied,
    ctx, qa, qw, ka, va, do, kw, dq, dkv, turned_sum, passing, sem, load_sem,
):
    handing = pltpu.make_async_copy(done_rows, passing, sem.at[0])
    handed = pltpu.make_async_copy(passing, copied, sem.at[1])
    loads = [
        pltpu.make_async_copy(source, target, load_sem.at[n])
        for n, (source, target) in enumerate(
            ((ctx_hbm, ctx), (qa_hbm, qa), (ka_hbm, ka), (va_hbm, va), (qw_hbm, qw))
        )
    ]
    for copy in loads:
        copy.start()
    handing.start()
    for i in range(SPAN // 512):
        rows = pl.ds(512 * i, 512)
        dq[rows, :] = jnp.zeros((512, 128), f32)
        dkv[rows, :] = jnp.zeros((512, 128), f32)
    do[:, pl.ds(PACK_ROWS, SPAN - PACK_ROWS), :] = jnp.zeros((2, SPAN - PACK_ROWS, 128), bf16)
    loads[0].wait()
    lane = iota((128, 128), 1)
    for b in range(16):
        pair = packed[pl.ds(128 * b, 128), :].astype(f32)
        product = pair * ctx[pl.ds(128 * b, 128), :]
        for half in range(2):
            rows = pl.ds(256 * b + 128 * half, 128)
            grad = pair if half == 0 else pltpu.roll(pair, 64, 1)
            at = 64 * half
            tails = []
            for h in range(2):
                inside = (lane >= at + 32 * h) & (lane < at + 32 * h + 32)
                delta = jnp.sum(jnp.where(inside, product, 0.0), axis=1, keepdims=True)
                one, two, three = pieces_of(-jnp.broadcast_to(delta, (128, 128)))
                spot = 32 - 32 * h
                tails.append(jnp.where(lane == spot, one, jnp.where(lane == spot + 1, two, three)))
            do[0, rows, :] = jnp.where(
                lane < 32, grad, jnp.where(lane < 35, tails[0], 0.0)
            ).astype(bf16)
            do[1, rows, :] = jnp.where(
                lane < 3, tails[1], jnp.where((lane >= 32) & (lane < 64), grad, 0.0)
            ).astype(bf16)
    for copy in loads[1:]:
        copy.wait()
    handing.wait()
    handed.start()

    def per_segment(s, _):
        q_start, q_end = bounds[s], bounds[s + 1]
        k_start, k_end = bounds[8 + s], bounds[9 + s]
        q_first = (q_start // 16) * 16
        k_first = (k_start // 16) * 16
        q_plan = plan(q_end - q_first, BACK_QUERY)

        def per_key(span, first_key, j, _):
            k_row = pl.multiple_of(first_key + j * span, 16)
            k_rows = pl.ds(k_row, span)
            lane = iota((span, 128), 1)
            at = iota((span, 128), 0) + k_row
            mine = (at >= k_start) & (at < k_end)
            here = pl.ds(0, span)
            for h in range(2):
                mask = mine & (lane >= 32 * h) & (lane < 32 * h + 32)
                kw[h, here, :] = jnp.where(mask, ka[h, k_rows, :].astype(f32), 0.0).astype(bf16)

            turned_sum[:, here] = jnp.zeros((128, span), f32)

            def per_query(size, first_row, i, _):
                q_rows = pl.ds(pl.multiple_of(first_row + i * size, 16), size)
                for h in range(2):
                    score = mm(qa[h, q_rows, :], ka[h, k_rows, :], NT)
                    prob = jnp.exp2(score)
                    prob_grad = mm(do[h, q_rows, :], va[h, k_rows, :], NT)
                    score_grad = (prob * prob_grad).astype(bf16)
                    dq[q_rows, :] += mm(score_grad, kw[h, here, :])
                    cols = slice(32 * h, 32 * h + 32)
                    turned_sum[32 * h : 32 * h + 32, here] += mm(qw[q_rows, cols], score_grad, TN)
                    turned_sum[64 + 32 * h : 96 + 32 * h, here] += mm(
                        do[h, q_rows, cols], prob.astype(bf16), TN
                    )
                return 0

            for size, offset, count in q_plan:
                lax.fori_loop(0, count, functools.partial(per_query, size, q_first + offset), 0)
            fresh = turned_sum[:, here].T
            dkv[k_rows, :] = dkv[k_rows, :] + jnp.where(mine, fresh, 0.0)
            return 0

        for span, offset, count in plan(k_end - k_first, BACK_KEY):
            lax.fori_loop(0, count, functools.partial(per_key, span, k_first + offset), 0)
        return 0

    lax.fori_loop(0, IMAGES, per_segment, 0)

    def emit(i, _):
        rows = pl.ds(pl.multiple_of(i * 256, 256), 256)
        gq[rows, :] = (dq[rows, :] * HEAD_DIM**-0.5).astype(bf16)
        start = bounds[16 + i]
        aligned = pl.multiple_of((start // 16) * 16, 16)
        places = jnp.concatenate([rank[2 * i], rank[2 * i + 1]], axis=1)
        hot = jnp.where(iota((272, 256), 0) + aligned == places, 1.0, 0.0).astype(bf16)
        piece = dkv[pl.ds(aligned, 272), :]
        scale = jnp.where(iota((272, 128), 1) < 64, HEAD_DIM**-0.5, 1.0)
        gkv[rows, :] = mm(hot, (piece * scale).astype(bf16), TN).astype(bf16)
        return 0

    lax.fori_loop(0, 8, twice(emit), 0)
    handed.wait()


def attend_backward(packed, ctx, qa, qw, ka, va, rank, bounds, done_rows):
    return pl.pallas_call(
        attend_backward_kernel,
        out_shape=(
            jax.ShapeDtypeStruct((PACK_ROWS, 128), bf16),
            jax.ShapeDtypeStruct((PACK_ROWS, 128), bf16),
            jax.ShapeDtypeStruct(done_rows.shape, done_rows.dtype),
        ),
        in_specs=[VMEM_SPEC] + [ANY_SPEC] * 5 + [VMEM_SPEC, SMEM_SPEC, ANY_SPEC],
        out_specs=[VMEM_SPEC] * 2 + [ANY_SPEC],
        scratch_shapes=[
            pltpu.VMEM((2048, 128), f32),
            pltpu.VMEM((2, SPAN, 128), bf16),
            pltpu.VMEM((SPAN, 128), bf16),
            pltpu.VMEM((2, SPAN, 128), bf16),
            pltpu.VMEM((2, SPAN, 128), bf16),
            pltpu.VMEM((2, SPAN, 128), bf16),
            pltpu.VMEM((2, BACK_KEY[0], 128), bf16),
            pltpu.VMEM((SPAN, 128), f32),
            pltpu.VMEM((SPAN, 128), f32),
            pltpu.VMEM((128, BACK_KEY[0]), f32),
            pltpu.VMEM(done_rows.shape, done_rows.dtype),
            pltpu.SemaphoreType.DMA((2,)),
            pltpu.SemaphoreType.DMA((5,)),
        ],
        compiler_params=pltpu.CompilerParams(vmem_limit_bytes=LIMIT_BACKWARD),
        cost_estimate=pl.CostEstimate(
            flops=50 * 10**9, bytes_accessed=20 * 10**6, transcendentals=10**7
        ),
    )(packed, ctx, qa, qw, ka, va, rank, bounds, done_rows)


STEP = 10


neg_fill = -1e30
norm_eps = 1e-05
beta_one = 0.5
beta_two = 0.5
adam_eps = 1e-08
decay_rate = 0.0001
step_rates = (0.06, 0.15, 0.06, 0.03, 0.1, 0.1, 0.1)


def product(left_side, right_side):
    return jnp.dot(left_side, right_side, preferred_element_type=jnp.float32)


def product_left(left_side, right_side):
    return lax.dot_general(
        left_side, right_side, (((0,), (0,)), ((), ())), preferred_element_type=jnp.float32
    )


def product_right(left_side, right_side):
    return lax.dot_general(
        left_side, right_side, (((1,), (1,)), ((), ())), preferred_element_type=jnp.float32
    )


def smooth_unit(values):
    return jax.nn.gelu(values, approximate=False)


def norm_forward(values, gain_row, shift_row):
    center = values - jnp.mean(values, axis=-1, keepdims=True)
    inverse = lax.rsqrt(jnp.mean(center * center, axis=-1, keepdims=True) + norm_eps)
    scaled = center * inverse
    return (scaled * gain_row + shift_row, scaled, inverse)


def norm_backward(upstream, scaled, inverse, gain_row):
    spread = upstream * gain_row
    centred = (
        spread
        - jnp.mean(spread, axis=-1, keepdims=True)
        - scaled * jnp.mean(spread * scaled, axis=-1, keepdims=True)
    )
    return (inverse * centred, jnp.sum(upstream * scaled, axis=0), jnp.sum(upstream, axis=0))


def summed(partial_value):
    return lax.psum(partial_value, "tensor")


def adamw(master, gradient, old_first, old_second, step_rate):
    momentum = beta_one * old_first + (1.0 - beta_one) * gradient
    variance = beta_two * old_second + (1.0 - beta_two) * gradient * gradient
    normal_step = (
        momentum / (1.0 - beta_one**STEP) / (jnp.sqrt(variance / (1.0 - beta_two**STEP)) + adam_eps)
    )
    return (master - step_rate * (normal_step + decay_rate * master), momentum, variance)


MESH = pl.DeviceIdType.MESH
SHARD_ROWS = 304
GROUPS = 16
CHUNK = 256
CHUNKS = 4
OWN_ROWS = CHUNK * CHUNKS


def greet(peers):
    barrier = pltpu.get_barrier_semaphore()
    for peer in peers:
        pl.semaphore_signal(barrier, inc=1, device_id=peer, device_id_type=MESH)
    return lambda: pl.semaphore_wait(barrier, len(peers))


def remote(source, target, send_sem, recv_sem, peer):
    return pltpu.make_async_remote_copy(
        src_ref=source,
        dst_ref=target,
        send_sem=send_sem,
        recv_sem=recv_sem,
        device_id=peer,
        device_id_type=MESH,
    )


def gather_kernel(
    up, down, outer, vec, shift, inward, off,
    pack, w3, offs,
    small, one, send_buf, recv_buf, send_sem, recv_sem,
):
    me = lax.axis_index("dp")
    peers = [lax.rem(me + k, 8) for k in range(1, 8)]
    ready = greet([{"dp": p} for p in peers])
    send_buf[...] = jnp.zeros((112, 128), bf16)
    for which in range(3):
        send_buf[32 * which : 32 * which + 32, 0:64] = inward[which].astype(bf16)
    small[...] = jnp.zeros((3, 16, 128), f32)
    small[0, 0:2, 0:8] = off[...]
    small[1, 0:6, 0:32] = vec[...]
    small[2, 6:7, 0:64] = shift[...]
    send_buf[96:112, :] = pltpu.roll(small[0], me * 8, 1).astype(bf16)
    recv_buf[me] = send_buf[...]
    ready()
    copies = []
    for k, peer in enumerate(peers):
        copy = remote(
            send_buf, recv_buf.at[me], send_sem.at[k], recv_sem.at[me], {"dp": peer}
        )
        copy.start()
        copies.append(copy)
    for b in range(4):
        one[32 * b : 32 * b + 32, :] = up[:, 128 * b : 128 * b + 128].astype(bf16)
        one[128 + 32 * b : 160 + 32 * b, :] = down[:, 128 * b : 128 * b + 128].astype(bf16)
    one[256:304, :] = jnp.zeros((48, 128), bf16)
    one[256:288, 0:64] = outer[...].astype(bf16)
    placed = pltpu.roll(small[1], lax.rem(me, 4) * 32, 1)
    placed = placed + pltpu.roll(small[2], lax.rem(me, 2) * 64, 1)
    one[288:304, :] = placed.astype(bf16)

    def spread(j, _):
        pack[j] = one[...]
        return 0

    lax.fori_loop(0, GROUPS, spread, 0)
    for peer in peers:
        remote(
            send_buf, recv_buf.at[peer], send_sem.at[0], recv_sem.at[peer], {"dp": peer}
        ).wait_recv()
    total = jnp.zeros((16, 128), f32)
    for d in range(8):
        for which in range(3):
            w3[which, 32 * d : 32 * d + 32, :] = recv_buf[d, 32 * which : 32 * which + 32, :]
        total = total + recv_buf[d, 96:112, :].astype(f32)
    offs[...] = total[0:8]
    for copy in copies:
        copy.wait_send()


def gather_weights(upward, down_t, out_t, vectors, shifts, inward, offsets):
    return pl.pallas_call(
        gather_kernel,
        out_shape=(
            jax.ShapeDtypeStruct((GROUPS, SHARD_ROWS, 128), bf16),
            jax.ShapeDtypeStruct((3, 256, 128), bf16),
            jax.ShapeDtypeStruct((8, 128), f32),
        ),
        in_specs=[VMEM_SPEC] * 7,
        out_specs=[VMEM_SPEC] * 3,
        scratch_shapes=[
            pltpu.VMEM((3, 16, 128), f32),
            pltpu.VMEM((SHARD_ROWS, 128), bf16),
            pltpu.VMEM((112, 128), bf16),
            pltpu.VMEM((8, 112, 128), bf16),
            pltpu.SemaphoreType.DMA((7,)),
            pltpu.SemaphoreType.DMA((8,)),
        ],
        compiler_params=pltpu.CompilerParams(
            collective_id=0, has_side_effects=True, vmem_limit_bytes=LIMIT_GATHER
        ),
    )(upward, down_t, out_t, vectors, shifts, inward, offsets)


def norm_rows(values):
    center = values - jnp.mean(values, axis=1, keepdims=True)
    inverse = lax.rsqrt(jnp.mean(center * center, axis=1, keepdims=True) + norm_eps)
    return center * inverse, inverse


def norm_rows_back(spread, scaled, inverse):
    return inverse * (
        spread
        - jnp.mean(spread, axis=1, keepdims=True)
        - scaled * jnp.mean(spread * scaled, axis=1, keepdims=True)
    )


def dense_kernel(
    ctxp, half, tok_hbm, cot_hbm,
    encoded, dctx, first, gout,
    other, ctxs, up, down, out_a, out_b, vec, shift,
    tok, cot, grads_ctx, normed_low, second_low, first_a, first_b,
    active, hgrad, slope, sums, give, take, keep,
    w_sem, load_sem, ctx_send, ctx_recv, dctx_send, dctx_recv,
    enc_send, enc_recv, local_sem, g_sem, enc_all,
):
    me = lax.axis_index("tensor")
    core = lax.rem(me, 2)
    sibling = me + 1 - 2 * core
    across = lax.rem(me + 2, 4)
    diagonal = lax.rem(sibling + 2, 4)
    order = (sibling, across, diagonal)
    ready = greet([{"tensor": p} for p in order])
    own = pl.multiple_of(me * OWN_ROWS, OWN_ROWS)
    load_tok = pltpu.make_async_copy(tok_hbm.at[pl.ds(own, OWN_ROWS)], tok, load_sem.at[0])
    load_cot = pltpu.make_async_copy(cot_hbm.at[pl.ds(own, OWN_ROWS)], cot, load_sem.at[1])
    load_tok.start()
    load_cot.start()
    ctxs[me] = ctxp[pl.ds(pl.multiple_of(me * 512, 512), 512), :]
    sums[...] = jnp.zeros((8, 256), f32)
    ready()
    weights = [
        remote(
            half.at[:, pl.ds(256, 48)], other.at[:, pl.ds(256, 48)],
            w_sem.at[0], w_sem.at[1], {"tensor": sibling},
        ),
        remote(
            half.at[:, pl.ds(0, 256)], other.at[:, pl.ds(0, 256)],
            w_sem.at[2], w_sem.at[3], {"tensor": sibling},
        ),
    ]
    weights[0].start()

    def ctx_copy(peer, c):
        rows = pl.ds(pl.multiple_of(peer * 512 + c * 128, 128), 128)
        return remote(
            ctxp.at[rows], ctxs.at[me, pl.ds(pl.multiple_of(c * 128, 128), 128)],
            ctx_send.at[peer, c], ctx_recv.at[me, c], {"tensor": peer},
        )

    def ctx_arrival(peer, c):
        rows = pl.ds(pl.multiple_of(c * 128, 128), 128)
        return remote(
            ctxp.at[rows], ctxs.at[peer, rows],
            ctx_send.at[peer, c], ctx_recv.at[peer, c], {"tensor": peer},
        )

    for peer in (across, diagonal, sibling):
        ctx_copy(peer, 0).start()
    weights[1].start()
    for c in range(1, CHUNKS):
        for peer in (across, diagonal, sibling):
            ctx_copy(peer, c).start()

    out_a[...] = jnp.zeros((256, 512), bf16)
    out_b[...] = jnp.zeros((256, 512), bf16)

    def unpack_small(source, t_of):
        for ty in range(2):
            t = t_of(ty)
            lanes = pl.ds(pl.multiple_of(t * 128, 128), 128)
            for d in range(8):
                piece = source[2 * d + ty, 256:288, :].astype(f32)
                out_a[32 * d : 32 * d + 32, lanes] = piece.astype(bf16)
                out_b[32 * d : 32 * d + 32, lanes] = pltpu.roll(piece, 64, 1).astype(bf16)
            for b in range(4):
                both = source[4 * b + ty, 288:304, :] + source[4 * b + 2 + ty, 288:304, :]
                shift[:, pl.ds(pl.multiple_of(t * 512 + 128 * b, 128), 128)] = (
                    both.astype(f32)[6:7]
                )

    def unpack_large(source, t_of):
        for ty in range(2):
            t = t_of(ty)

            def one_row(d, _):
                rows = pl.ds(pl.multiple_of(d * 32, 32), 32)
                for b in range(4):
                    lanes = pl.ds(pl.multiple_of(t * 512 + 128 * b, 128), 128)
                    up[rows, lanes] = source[2 * d + ty, 32 * b : 32 * b + 32, :]
                    down[rows, lanes] = source[2 * d + ty, 128 + 32 * b : 160 + 32 * b, :]
                return 0

            lax.fori_loop(0, 8, one_row, 0)

    mine_t = lambda ty: 2 * ty + core
    other_t = lambda ty: 2 * ty + 1 - core
    for b in range(2):
        total = jnp.zeros((16, 128), f32)
        for d in range(4 * b, 4 * b + 4):
            total = total + half[2 * d, 288:304, :].astype(f32)
        vec[:, 128 * b : 128 * b + 128] = total[0:8]
    unpack_small(half, mine_t)
    unpack_large(half, mine_t)
    weights[0].wait_recv()
    unpack_small(other, other_t)
    weights[1].wait_recv()
    unpack_large(other, other_t)
    load_tok.wait()
    load_cot.wait()

    def enc_rows(owner, c):
        return pl.ds(pl.multiple_of(owner * OWN_ROWS + c * CHUNK, CHUNK), CHUNK)

    def enc_copies(c):
        rows = enc_rows(me, c)
        return (
            remote(enc_all.at[rows], enc_all.at[rows], enc_send.at[0, c], enc_recv.at[0, c],
                   {"tensor": across}),
            remote(enc_all.at[rows], enc_all.at[rows], enc_send.at[1, c], enc_recv.at[1, c],
                   {"tensor": sibling}),
        )

    def enc_arrival(owner, kind, c):
        rows = enc_rows(owner, c)
        return remote(enc_all.at[rows], enc_all.at[rows], enc_send.at[2, c],
                      enc_recv.at[kind, c], {"tensor": sibling})

    def enc_store(owner, n, c):
        rows = enc_rows(owner, c)
        return pltpu.make_async_copy(enc_all.at[rows], encoded.at[rows], local_sem.at[n, c])

    def dctx_copy(peer, c):
        rows = pl.ds(pl.multiple_of(c * 128, 128), 128)
        return remote(
            grads_ctx.at[peer, rows],
            dctx.at[pl.ds(pl.multiple_of(me * 512 + c * 128, 128), 128)],
            dctx_send.at[peer, c], dctx_recv.at[me, c], {"tensor": peer},
        )

    def dctx_arrival(peer, c):
        rows = pl.ds(pl.multiple_of(c * 128, 128), 128)
        return remote(
            grads_ctx.at[peer, rows],
            dctx.at[pl.ds(pl.multiple_of(peer * 512 + c * 128, 128), 128)],
            dctx_send.at[peer, c], dctx_recv.at[peer, c], {"tensor": peer},
        )

    def dctx_local(c):
        rows = pl.ds(pl.multiple_of(c * 128, 128), 128)
        return pltpu.make_async_copy(
            grads_ctx.at[me, rows],
            dctx.at[pl.ds(pl.multiple_of(me * 512 + c * 128, 128), 128)],
            local_sem.at[4, c],
        )

    def chunk_step(c, _):
        for peer in order:
            ctx_arrival(peer, c).wait_recv()
        rows = pl.ds(pl.multiple_of(c * CHUNK, CHUNK), CHUNK)
        pair_rows = pl.ds(pl.multiple_of(c * 128, 128), 128)
        context = jnp.concatenate([ctxs[t, pair_rows, :] for t in range(4)], axis=1)
        attended = jnp.concatenate(
            [mm(context, out_a[...], NT), mm(context, out_b[...], NT)], axis=0
        )
        first_sum = tok[rows, :].astype(f32) + attended + vec[4:5]
        scaled_one, inverse_one = norm_rows(first_sum)
        normed = scaled_one * vec[0:1] + vec[1:2]
        low = normed.astype(bf16)
        normed_low[rows, :] = low
        for n in range(4):
            span = slice(512 * n, 512 * n + 512)
            hidden = mm(low, up[:, span]) + shift[:, span]
            cumulative = 0.5 * (1.0 + lax.erf(hidden * 0.7071067811865476))
            active[rows, span] = (hidden * cumulative).astype(bf16)
            slope[:, span] = cumulative + hidden * (
                0.3989422804014327 * jnp.exp(-0.5 * hidden * hidden)
            )
        second_sum = normed + mm(active[rows, :], down[...], NT) + vec[5:6]
        scaled_two, inverse_two = norm_rows(second_sum)
        enc_all[enc_rows(me, c), :] = (scaled_two * vec[2:3] + vec[3:4]).astype(bf16)
        for copy in enc_copies(c):
            copy.start()
        enc_store(me, 0, c).start()
        upstream = cot[rows, :].astype(f32)
        second_grad = norm_rows_back(upstream * vec[2:3], scaled_two, inverse_two)
        low_two = second_grad.astype(bf16)
        second_low[rows, :] = low_two
        for n in range(4):
            span = slice(512 * n, 512 * n + 512)
            hgrad[rows, span] = (mm(low_two, down[:, span]) * slope[:, span]).astype(bf16)
        normed_grad = second_grad + mm(hgrad[rows, :], up[...], NT)
        first_grad = norm_rows_back(normed_grad * vec[0:1], scaled_one, inverse_one)
        first[rows, :] = first_grad
        low_one = first_grad.astype(bf16)
        first_a[pair_rows, :] = low_one[0:128]
        first_b[pair_rows, :] = low_one[128:256]
        back = (mm(low_one[0:128], out_a[...]) + mm(low_one[128:256], out_b[...])).astype(bf16)
        for t in range(4):
            grads_ctx[t, pair_rows, :] = back[:, 128 * t : 128 * t + 128]
        for peer in (across, diagonal, sibling):
            dctx_copy(peer, c).start()
        dctx_local(c).start()
        fold = lambda value: jnp.sum(value, axis=0, keepdims=True)
        sums[0:1] += fold(normed_grad * scaled_one)
        sums[1:2] += fold(normed_grad)
        sums[2:3] += fold(upstream * scaled_two)
        sums[3:4] += fold(upstream)
        sums[4:5] += fold(first_grad)
        sums[5:6] += fold(second_grad)
        return 0

    lax.fori_loop(0, CHUNKS, chunk_step, 0)

    ones = jnp.ones((8, OWN_ROWS), bf16)

    def weight_grads(t_of, target, kind):
        for ty in range(2):
            t = t_of(ty)
            lanes = pl.ds(pl.multiple_of(t * 512, 512), 512)
            grad_up = mm(normed_low[...], hgrad[:, lanes], TN).astype(kind)
            grad_down = mm(second_low[...], active[:, lanes], TN).astype(kind)
            part_a = mm(first_a[...], ctxs[t], TN)
            part_b = pltpu.roll(mm(first_b[...], ctxs[t], TN), 64, 1)
            grad_out = jnp.where(
                iota((256, 128), 1) < 64, part_a + part_b, 0.0
            ).astype(kind)
            shift_sum = mm(ones, hgrad[:, lanes])
            for d in range(8):
                j = 2 * d + ty
                block = slice(32 * d, 32 * d + 32)
                for b in range(4):
                    cols = slice(128 * b, 128 * b + 128)
                    target[j, 32 * b : 32 * b + 32, :] = grad_up[block, cols]
                    target[j, 128 + 32 * b : 160 + 32 * b, :] = grad_down[block, cols]
                target[j, 256:288, :] = grad_out[block]
                vector = sums[:, 128 * (d // 4) : 128 * (d // 4) + 128]
                cols = slice(128 * (d // 2), 128 * (d // 2) + 128)
                tail = jnp.where(iota((8, 128), 0) == 6, shift_sum[:, cols], vector)
                target[j, 288:304, :] = jnp.concatenate(
                    [tail, jnp.zeros((8, 128), f32)], axis=0
                ).astype(kind)

    weight_grads(other_t, give, bf16)
    trade = remote(give, take, g_sem.at[0], g_sem.at[1], {"tensor": sibling})
    trade.start()
    for c in range(CHUNKS):
        enc_arrival(across, 0, c).wait_recv()
        enc_arrival(across, 2, c).start()
        enc_store(across, 1, c).start()
    weight_grads(mine_t, keep, f32)
    trade.wait_recv()

    def merge(j, _):
        gout[j] = (keep[j] + take[j].astype(f32)).astype(bf16)
        return 0

    lax.fori_loop(0, GROUPS, merge, 0)
    trade.wait_send()
    for copy in weights:
        copy.wait_send()
    for c in range(CHUNKS):
        for peer in order:
            ctx_copy(peer, c).wait_send()
            dctx_copy(peer, c).wait_send()
            dctx_arrival(peer, c).wait_recv()
        dctx_local(c).wait()
        far, near = enc_copies(c)
        far.wait_send()
        near.wait_send()
        enc_arrival(sibling, 1, c).wait_recv()
        enc_store(sibling, 2, c).start()
        enc_arrival(across, 2, c).wait_send()
        enc_arrival(diagonal, 2, c).wait_recv()
        enc_store(diagonal, 3, c).start()
    for c in range(CHUNKS):
        for n, owner in enumerate((me, across, sibling, diagonal)):
            enc_store(owner, n, c).wait()


def dense(ctxp, half, tokens, cotangent):
    dma = pltpu.SemaphoreType.DMA
    return pl.pallas_call(
        dense_kernel,
        out_shape=(
            jax.ShapeDtypeStruct((PACK_ROWS, 256), bf16),
            jax.ShapeDtypeStruct((PACK_ROWS // 2, 128), bf16),
            jax.ShapeDtypeStruct((OWN_ROWS, 256), f32),
            jax.ShapeDtypeStruct((GROUPS, SHARD_ROWS, 128), bf16),
        ),
        in_specs=[VMEM_SPEC, VMEM_SPEC, ANY_SPEC, ANY_SPEC],
        out_specs=[ANY_SPEC, ANY_SPEC, VMEM_SPEC, VMEM_SPEC],
        scratch_shapes=[
            pltpu.VMEM((GROUPS, SHARD_ROWS, 128), bf16),
            pltpu.VMEM((4, 512, 128), bf16),
            pltpu.VMEM((256, 2048), bf16),
            pltpu.VMEM((256, 2048), bf16),
            pltpu.VMEM((256, 512), bf16),
            pltpu.VMEM((256, 512), bf16),
            pltpu.VMEM((8, 256), f32),
            pltpu.VMEM((1, 2048), f32),
            pltpu.VMEM((OWN_ROWS, 256), bf16),
            pltpu.VMEM((OWN_ROWS, 256), bf16),
            pltpu.VMEM((4, 512, 128), bf16),
            pltpu.VMEM((OWN_ROWS, 256), bf16),
            pltpu.VMEM((OWN_ROWS, 256), bf16),
            pltpu.VMEM((512, 256), bf16),
            pltpu.VMEM((512, 256), bf16),
            pltpu.VMEM((OWN_ROWS, 2048), bf16),
            pltpu.VMEM((OWN_ROWS, 2048), bf16),
            pltpu.VMEM((CHUNK, 2048), f32),
            pltpu.VMEM((8, 256), f32),
            pltpu.VMEM((GROUPS, SHARD_ROWS, 128), bf16),
            pltpu.VMEM((GROUPS, SHARD_ROWS, 128), bf16),
            pltpu.VMEM((GROUPS, SHARD_ROWS, 128), f32),
            dma((4,)),
            dma((2,)),
            dma((4, CHUNKS)),
            dma((4, CHUNKS)),
            dma((4, CHUNKS)),
            dma((4, CHUNKS)),
            dma((3, CHUNKS)),
            dma((3, CHUNKS)),
            dma((5, CHUNKS)),
            dma((2,)),
            pltpu.VMEM((PACK_ROWS, 256), bf16),
        ],
        compiler_params=pltpu.CompilerParams(
            collective_id=1, has_side_effects=True, vmem_limit_bytes=LIMIT_DENSE
        ),
        cost_estimate=pl.CostEstimate(
            flops=7 * 10**9, bytes_accessed=8 * 10**6, transcendentals=4 * 10**6
        ),
    )(ctxp, half, tokens, cotangent)


def tail_kernel(
    gq, gkv, tok, pos, w3, first,
    tg, gin,
    wall, near_send, near_recv, far_send, far_recv, mine, in_send, in_recv,
    n_send, n_recv, f_send, f_recv, t_send, t_recv, i_send, i_recv, local_sem,
):
    me = lax.axis_index("tensor")
    rank = lax.axis_index("dp")
    core = lax.rem(me, 2)
    sibling = me + 1 - 2 * core
    across = lax.rem(me + 2, 4)
    diagonal = lax.rem(sibling + 2, 4)
    peers = [lax.rem(rank + k, 8) for k in range(1, 8)]
    ready = greet(
        [{"tensor": sibling}, {"tensor": across}] + [{"dp": peer} for peer in peers]
    )
    lane = iota((256, 128), 1)
    wall[:, 0:128] = w3[0]
    wall[:, 128:256] = jnp.where(
        lane < 64, w3[1].astype(f32), pltpu.roll(w3[2].astype(f32), 64, 1)
    ).astype(bf16)

    def rows_of(even, odd, i):
        owner = jnp.where(lax.rem(i, 2) == 0, even, odd)
        return pl.ds(pl.multiple_of(owner * OWN_ROWS + (i // 2) * CHUNK, CHUNK), CHUNK)

    def slot(i):
        return pl.ds(pl.multiple_of(i * CHUNK, CHUNK), CHUNK)

    def partial(rows):
        return mm(jnp.concatenate([gq[rows, :], gkv[rows, :]], axis=1), wall[...], NT)

    def near_copy(i):
        return remote(near_send.at[slot(i)], near_recv.at[slot(i)],
                      n_send.at[i], n_recv.at[i], {"tensor": sibling})

    def far_copy(i):
        theirs = i + 1 - 2 * lax.rem(i, 2)
        return remote(far_send.at[slot(i)], far_recv.at[slot(theirs)],
                      f_send.at[i], f_recv.at[theirs], {"tensor": across})

    def far_arrival(i):
        return remote(far_send.at[slot(i)], far_recv.at[slot(i)],
                      f_send.at[i], f_recv.at[i], {"tensor": across})

    def share_copy(i):
        return remote(mine.at[slot(i)], tg.at[rows_of(across, me, i)],
                      t_send.at[i], t_recv.at[i], {"tensor": sibling})

    def share_arrival(i):
        return remote(mine.at[slot(i)], tg.at[rows_of(diagonal, sibling, i)],
                      t_send.at[i], t_recv.at[i], {"tensor": sibling})

    def keep_copy(i):
        return pltpu.make_async_copy(
            mine.at[slot(i)], tg.at[rows_of(across, me, i)], local_sem.at[i]
        )

    def first_stage(i, _):
        near_send[slot(i), :] = partial(rows_of(diagonal, sibling, i)).astype(bf16)
        near_copy(i).start()
        return 0

    def second_stage(i, _):
        value = partial(rows_of(across, me, i))
        odd = lax.rem(i, 2).astype(f32)
        half = pl.ds(pl.multiple_of((i // 2) * CHUNK, CHUNK), CHUNK)
        value = value + first[half, :] * odd
        near_copy(i).wait_recv()
        far_send[slot(i), :] = (value + near_recv[slot(i), :].astype(f32)).astype(bf16)
        far_copy(i).start()
        return 0

    ready()
    lax.fori_loop(0, 2, first_stage, 0)

    def both_stages(i, _):
        first_stage(i + 2, 0)
        second_stage(i, 0)
        return 0

    lax.fori_loop(0, 6, both_stages, 0)
    lax.fori_loop(6, 8, second_stage, 0)

    def inward_step(i, carry):
        left, right, total = carry
        rows = pl.ds(pl.multiple_of(i * 1024, 1024), 1024)
        token = tok[rows, :]
        query_in = (token.astype(f32) + pos[rows, :].astype(f32)).astype(bf16)
        both = jnp.concatenate([gq[rows, :], gkv[rows, :]], axis=1)
        left = left + mm(query_in, both, TN)
        right = right + mm(token, gkv[rows, :], TN)
        total = total + mm(jnp.ones((8, 1024), bf16), both)
        return left, right, total

    left, right, total = lax.fori_loop(
        0, 4, inward_step,
        (jnp.zeros((256, 256), f32), jnp.zeros((256, 128), f32), jnp.zeros((8, 256), f32)),
    )
    joined = jnp.concatenate([jnp.where(lane < 64, left[:, 0:128], right), left[:, 128:256]], 1)
    for d in range(8):
        in_send[d, 0:32, :] = joined[32 * d : 32 * d + 32]
        in_send[d, 32:40, :] = total
    in_copies = []
    for k, peer in enumerate(peers):
        copy = remote(
            in_send.at[peer], in_recv.at[rank], i_send.at[k], i_recv.at[rank], {"dp": peer}
        )
        copy.start()
        in_copies.append(copy)

    def third_stage(i, _):
        far_arrival(i).wait_recv()
        mine[slot(i), :] = (
            far_send[slot(i), :].astype(f32) + far_recv[slot(i), :].astype(f32)
        ).astype(bf16)
        share_copy(i).start()
        keep_copy(i).start()
        return 0

    def third_pair(i, _):
        third_stage(2 * i + 1, 0)
        third_stage(2 * i, 0)
        return 0

    lax.fori_loop(0, 4, third_pair, 0)

    gathered = in_send[rank]
    for peer in peers:
        remote(
            in_send.at[peer], in_recv.at[peer], i_send.at[0], i_recv.at[peer], {"dp": peer}
        ).wait_recv()
        gathered = gathered + in_recv[peer]
    gin[...] = gathered

    for copy in in_copies:
        copy.wait_send()

    def finish(i, _):
        near_copy(i).wait_send()
        far_copy(i).wait_send()
        share_copy(i).wait_send()
        keep_copy(i).wait()
        share_arrival(i).wait_recv()
        return 0

    lax.fori_loop(0, 8, finish, 0)


def tail(gq, gkv, tokens, positions, w3, first):
    dma = pltpu.SemaphoreType.DMA
    return pl.pallas_call(
        tail_kernel,
        out_shape=(
            jax.ShapeDtypeStruct((PACK_ROWS, 256), bf16),
            jax.ShapeDtypeStruct((40, 256), f32),
        ),
        in_specs=[VMEM_SPEC] * 6,
        out_specs=[ANY_SPEC, VMEM_SPEC],
        scratch_shapes=[pltpu.VMEM((256, 256), bf16)]
        + [pltpu.VMEM((8 * CHUNK, 256), bf16)] * 5
        + [
            pltpu.VMEM((8, 40, 256), f32),
            pltpu.VMEM((8, 40, 256), f32),
            dma((8,)),
            dma((8,)),
            dma((8,)),
            dma((8,)),
            dma((8,)),
            dma((8,)),
            dma((7,)),
            dma((8,)),
            dma((8,)),
        ],
        compiler_params=pltpu.CompilerParams(
            collective_id=2, has_side_effects=True, vmem_limit_bytes=LIMIT_TAIL
        ),
        cost_estimate=pl.CostEstimate(
            flops=3 * 10**9, bytes_accessed=16 * 10**6, transcendentals=0
        ),
    )(gq, gkv, tokens, positions, w3, first)


def update_kernel(pieces, gin, narrow, *refs):
    masters, firsts, seconds = refs[0:7], refs[7:14], refs[14:21]
    wide_out = refs[21]
    grads, news, lows, moms, varis = (
        refs[22:29], refs[29:36], refs[36:40], refs[40:47], refs[47:54],
    )
    stage, sem = refs[54:56]
    me = lax.axis_index("dp")
    copies = []
    for i in range(8):
        rows = pl.ds(512 * i, 512)
        stage[rows, :] = narrow[rows, :].astype(f32)
        copy = pltpu.make_async_copy(stage.at[rows], wide_out.at[rows], sem.at[i])
        copy.start()
        copies.append(copy)

    def add(j, total):
        return total + pieces[j].astype(f32)

    total = lax.fori_loop(0, GROUPS, add, jnp.zeros((SHARD_ROWS, 128), f32))
    wide = gin[...]
    small = total[288:296]
    vec_grad = pltpu.roll(small, lax.rem(128 - lax.rem(me, 4) * 32, 128), 1)[0:6, 0:32]
    shift_grad = pltpu.roll(small, lax.rem(128 - lax.rem(me, 2) * 64, 128), 1)[6:7, 0:64]
    off_q = pltpu.roll(wide[32:40, 0:128], lax.rem(128 - me * 8, 128), 1)
    off_v = pltpu.roll(wide[32:40, 128:256], 64 - me * 8, 1)
    off_grad = jnp.where(iota((8, 128), 0) == 0, off_q, off_v)[0:2, 0:8]
    left, right = wide[0:32, 0:128], wide[0:32, 128:256]
    inward_grads = (left[:, 0:64], right[:, 0:64], pltpu.roll(left, 64, 1)[:, 0:64])
    joined = lambda base: jnp.concatenate(
        [total[base + 32 * b : base + 32 * b + 32] for b in range(4)], axis=1
    )
    plain = (None, total[256:288, 0:64], joined(0), joined(128), vec_grad, off_grad, shift_grad)

    def apply(index, at, gradient):
        new, momentum, variance = adamw(
            masters[index][at], gradient, firsts[index][at], seconds[index][at],
            step_rates[index],
        )
        grads[index][at] = gradient
        news[index][at] = new
        moms[index][at] = momentum
        varis[index][at] = variance
        if index < 4:
            lows[index][at] = new.astype(bf16)

    for which in range(3):
        apply(0, which, inward_grads[which])
    for index in range(1, 7):
        apply(index, Ellipsis, plain[index])
    for copy in copies:
        copy.wait()


def update(pieces, gin, narrow, masters, firsts, seconds):
    shapes = [m.shape for m in masters]
    of = lambda kind, count: [jax.ShapeDtypeStruct(s, kind) for s in shapes[:count]]
    out = [jax.ShapeDtypeStruct((PACK_ROWS, 256), f32)]
    out = out + of(f32, 7) + of(f32, 7) + of(bf16, 4) + of(f32, 7) + of(f32, 7)
    return pl.pallas_call(
        update_kernel,
        out_shape=out,
        in_specs=[VMEM_SPEC] * 24,
        out_specs=[ANY_SPEC] + [VMEM_SPEC] * (len(out) - 1),
        scratch_shapes=[pltpu.VMEM((PACK_ROWS, 256), f32), pltpu.SemaphoreType.DMA((8,))],
        compiler_params=pltpu.CompilerParams(vmem_limit_bytes=LIMIT_UPDATE),
    )(pieces, gin, narrow, *masters, *firsts, *seconds)


def exchange(pieces):
    groups = [[4 * d + 2 * y + c for d in range(8) for y in range(2)] for c in range(2)]
    return lax.all_to_all(
        pieces, ("dp", "tensor"), 0, 0, axis_index_groups=groups, tiled=True
    )


def turned(group):
    inward, outward, upward, downward, vectors, offsets, shifts = group
    return [inward, outward.T, upward, downward.T, vectors, offsets, shifts.reshape(1, -1)]


def returned(group):
    if len(group) == 4:
        return [group[0], group[1].T, group[2], group[3].T]
    inward, outward, upward, downward, vectors, offsets, shifts = group
    return [inward, outward.T, upward, downward.T, vectors, offsets, shifts.reshape(-1)]


def body_pods(tokens, positions, segment_ids, pad_flags, cotangent, *state):
    masters, firsts, seconds = (turned(state[7 * i : 7 * i + 7]) for i in range(3))
    inward, out_t, upward, down_t, vectors, offsets, shifts = masters
    pack, w3, off = gather_weights(upward, down_t, out_t, vectors, shifts, inward, offsets)
    half = exchange(pack)
    ctxp, *saved = attend_forward(tokens, positions, w3, off, segment_ids, pad_flags)
    encoded, dctx, first, gout = dense(ctxp, half, tokens, cotangent)
    pieces = exchange(gout)
    gq, gkv, encoded = attend_backward(dctx, *saved, encoded)
    narrow, gin = tail(gq, gkv, tokens, positions, w3, first)
    token_grad, *outs = update(pieces, gin, narrow, masters, firsts, seconds)
    grads, news, lows, moms, varis = outs[:7], outs[7:14], outs[14:18], outs[18:25], outs[25:]
    return (
        encoded,
        token_grad,
        *returned(grads),
        *returned(news),
        *returned(lows),
        *returned(moms),
        *returned(varis),
    )


def body(
    tokens,
    positions,
    segment_ids,
    pad_flags,
    cotangent,
    inward,
    outward,
    upward,
    downward,
    vectors,
    offsets,
    shifts,
    first_inward,
    first_outward,
    first_upward,
    first_downward,
    first_vectors,
    first_offsets,
    first_shifts,
    second_inward,
    second_outward,
    second_upward,
    second_downward,
    second_vectors,
    second_offsets,
    second_shifts,
):
    w_inward, w_outward, w_upward, w_downward, vector_low, offset_low, shift_low = (
        lax.all_gather(inward.astype(jnp.bfloat16), "dp", axis=1, tiled=True),
        lax.all_gather(outward.astype(jnp.bfloat16), "dp", axis=1, tiled=True),
        lax.all_gather(upward.astype(jnp.bfloat16), "dp", axis=0, tiled=True),
        lax.all_gather(downward.astype(jnp.bfloat16), "dp", axis=1, tiled=True),
        lax.all_gather(vectors.astype(jnp.bfloat16), "dp", axis=1, tiled=True),
        lax.all_gather(offsets.astype(jnp.bfloat16), "dp", axis=1, tiled=True),
        lax.all_gather(shifts.astype(jnp.bfloat16), "dp", axis=0, tiled=True),
    )
    vector_wide = vector_low.astype(jnp.float32)
    offset_wide = offset_low.astype(jnp.float32)
    shift_wide = shift_low.astype(jnp.float32)
    input_wide = tokens.astype(jnp.float32)
    query_in = (input_wide + positions.astype(jnp.float32)).astype(jnp.bfloat16)
    w_lanes = jnp.pad(w_inward, ((0, 0), (0, 0), (0, 64)))
    off_lanes = jnp.pad(offset_wide, ((0, 6), (0, 64)))
    packed, *saved = attend_forward(
        tokens, positions, w_lanes, off_lanes, segment_ids, pad_flags
    )
    pairs = packed.reshape(16, 128, 2, 64)
    context_low = pairs.transpose(0, 2, 1, 3).reshape(PACK_ROWS, 64)
    first_sum = input_wide + summed(product(context_low, w_outward)) + vector_wide[4]
    normed, scaled_one, inverse_one = norm_forward(first_sum, vector_wide[0], vector_wide[1])
    normed_low = normed.astype(jnp.bfloat16)
    hidden = product(normed_low, w_upward) + shift_wide
    unit_value, unit_back = jax.vjp(smooth_unit, hidden)
    active = unit_value.astype(jnp.bfloat16)
    second_sum = normed + summed(product(active, w_downward)) + vector_wide[5]
    result, scaled_two, inverse_two = norm_forward(second_sum, vector_wide[2], vector_wide[3])
    encoded = result.astype(jnp.bfloat16)
    upstream = cotangent.astype(jnp.float32)
    second_grad, gain_two, shift_two = norm_backward(
        upstream, scaled_two, inverse_two, vector_wide[2]
    )
    down_low = second_grad.astype(jnp.bfloat16)
    grad_downward = product_left(active, down_low)
    hidden_low = unit_back(product_right(down_low, w_downward))[0].astype(jnp.bfloat16)
    grad_upward = product_left(normed_low, hidden_low)
    grad_shifts = jnp.sum(hidden_low.astype(jnp.float32), axis=0)
    normed_grad = second_grad + summed(product_right(hidden_low, w_upward))
    first_grad, gain_one, shift_one = norm_backward(
        normed_grad, scaled_one, inverse_one, vector_wide[0]
    )
    first_low = first_grad.astype(jnp.bfloat16)
    grad_outward = product_left(context_low, first_low)
    context_grad = product_right(first_low, w_outward).astype(jnp.bfloat16)
    halves = context_grad.reshape(16, 2, 128, 64)
    gq, gkv, encoded = attend_backward(
        halves.transpose(0, 2, 1, 3).reshape(2048, 128), *saved, encoded
    )
    query_grad, key_grad, value_grad = gq[:, :64], gkv[:, :64], gkv[:, 64:]
    grad_inward = jnp.stack(
        [
            product_left(query_in, query_grad),
            product_left(query_in, key_grad),
            product_left(tokens, value_grad),
        ]
    )
    grad_offsets = jnp.stack(
        [
            jnp.sum(query_grad.astype(jnp.float32), axis=0),
            jnp.sum(value_grad.astype(jnp.float32), axis=0),
        ]
    )
    input_part = (
        product_right(query_grad, w_inward[0])
        + product_right(key_grad, w_inward[1])
        + product_right(value_grad, w_inward[2])
    )
    input_grad = first_grad + summed(input_part)
    grad_vectors = jnp.stack(
        [
            gain_one,
            shift_one,
            gain_two,
            shift_two,
            jnp.sum(first_grad, axis=0),
            jnp.sum(second_grad, axis=0),
        ]
    )
    reduced = (
        lax.psum_scatter(grad_inward, "dp", scatter_dimension=1, tiled=True),
        lax.psum_scatter(grad_outward, "dp", scatter_dimension=1, tiled=True),
        lax.psum_scatter(grad_upward, "dp", scatter_dimension=0, tiled=True),
        lax.psum_scatter(grad_downward, "dp", scatter_dimension=1, tiled=True),
        lax.psum_scatter(grad_vectors, "dp", scatter_dimension=1, tiled=True),
        lax.psum_scatter(grad_offsets, "dp", scatter_dimension=1, tiled=True),
        lax.psum_scatter(grad_shifts, "dp", scatter_dimension=0, tiled=True),
    )
    masters = (inward, outward, upward, downward, vectors, offsets, shifts)
    firsts = (
        first_inward,
        first_outward,
        first_upward,
        first_downward,
        first_vectors,
        first_offsets,
        first_shifts,
    )
    seconds = (
        second_inward,
        second_outward,
        second_upward,
        second_downward,
        second_vectors,
        second_offsets,
        second_shifts,
    )
    updated = []
    momenta = []
    variances = []
    for master, gradient, old_first, old_second, step_rate in zip(
        masters, reduced, firsts, seconds, step_rates
    ):
        new_master, momentum, variance = adamw(master, gradient, old_first, old_second, step_rate)
        updated.append(new_master)
        momenta.append(momentum)
        variances.append(variance)
    return (
        encoded,
        input_grad,
        reduced[0],
        reduced[1],
        reduced[2],
        reduced[3],
        reduced[4],
        reduced[5],
        reduced[6],
        updated[0],
        updated[1],
        updated[2],
        updated[3],
        updated[4],
        updated[5],
        updated[6],
        updated[0].astype(jnp.bfloat16),
        updated[1].astype(jnp.bfloat16),
        updated[2].astype(jnp.bfloat16),
        updated[3].astype(jnp.bfloat16),
        momenta[0],
        momenta[1],
        momenta[2],
        momenta[3],
        momenta[4],
        momenta[5],
        momenta[6],
        variances[0],
        variances[1],
        variances[2],
        variances[3],
        variances[4],
        variances[5],
        variances[6],
    )


def solution(mesh):
    in_specs = (
        P("dp", None),
        P("dp", None),
        P("dp", None),
        P("dp", None),
        P("dp", None),
        P(None, "dp", "tensor"),
        P("tensor", "dp"),
        P("dp", "tensor"),
        P("tensor", "dp"),
        P(None, "dp"),
        P(None, ("tensor", "dp")),
        P(("tensor", "dp")),
        P(None, "dp", "tensor"),
        P("tensor", "dp"),
        P("dp", "tensor"),
        P("tensor", "dp"),
        P(None, "dp"),
        P(None, ("tensor", "dp")),
        P(("tensor", "dp")),
        P(None, "dp", "tensor"),
        P("tensor", "dp"),
        P("dp", "tensor"),
        P("tensor", "dp"),
        P(None, "dp"),
        P(None, ("tensor", "dp")),
        P(("tensor", "dp")),
    )
    out_specs = (
        P("dp", None),
        P("dp", None),
        P(None, "dp", "tensor"),
        P("tensor", "dp"),
        P("dp", "tensor"),
        P("tensor", "dp"),
        P(None, "dp"),
        P(None, ("tensor", "dp")),
        P(("tensor", "dp")),
        P(None, "dp", "tensor"),
        P("tensor", "dp"),
        P("dp", "tensor"),
        P("tensor", "dp"),
        P(None, "dp"),
        P(None, ("tensor", "dp")),
        P(("tensor", "dp")),
        P(None, "dp", "tensor"),
        P("tensor", "dp"),
        P("dp", "tensor"),
        P("tensor", "dp"),
        P(None, "dp", "tensor"),
        P("tensor", "dp"),
        P("dp", "tensor"),
        P("tensor", "dp"),
        P(None, "dp"),
        P(None, ("tensor", "dp")),
        P(("tensor", "dp")),
        P(None, "dp", "tensor"),
        P("tensor", "dp"),
        P("dp", "tensor"),
        P("tensor", "dp"),
        P(None, "dp"),
        P(None, ("tensor", "dp")),
        P(("tensor", "dp")),
    )
    pods = mesh.shape["dp"] == 8 and mesh.shape["tensor"] == 4
    chosen = body_pods if pods else body
    return jax.shard_map(chosen, mesh=mesh, in_specs=in_specs, out_specs=out_specs, check_vma=False)
```

```python
import functools
import jax
import jax.numpy as jnp
from jax import lax
from jax.experimental import pallas as pl
from jax.experimental.pallas import tpu as pltpu
from jax.sharding import PartitionSpec as P

HEAD_DIM = 32
MIB = 2**20
LIMIT_GATHER = 58 * MIB
LIMIT_FORWARD = 58 * MIB
LIMIT_DENSE = 58 * MIB
LIMIT_BACKWARD = 58 * MIB
LIMIT_TAIL = 58 * MIB
LIMIT_UPDATE = 58 * MIB
PACK_ROWS = 4096
IMAGES = 5
SPAN = PACK_ROWS + 512
BACK_QUERY = (512, 256)
BACK_KEY = (1024, 512, 256)
FORWARD_QUERY = (1024, 512, 256)
FORWARD_KEY = (1024, 512, 256)
LOG_SCALE = HEAD_DIM**-0.5 * 1.4426950408889634
FENCE = 2.0**100
LARGE = 2.0**100
SMALL = 2.0**-60
NN = (((1,), (0,)), ((), ()))
NT = (((1,), (1,)), ((), ()))
TN = (((0,), (0,)), ((), ()))
bf16 = jnp.bfloat16
f32 = jnp.float32


def mm(left, right, dims=NN):
    return lax.dot_general(left, right, dims, preferred_element_type=f32)


def iota(shape, dim):
    return lax.broadcasted_iota(jnp.int32, shape, dim)


def plan(length, sizes):
    out = []
    offset = 0
    least = sizes[-1]
    for size in sizes:
        left = jnp.maximum(length - offset, 0)
        count = (left + least - 1) // size
        out.append((size, offset, count))
        offset = offset + count * size
    return out


def twice(step):
    def both(i, carry):
        return step(2 * i + 1, step(2 * i, carry))

    return both


def pieces_of(value):
    one = value.astype(bf16).astype(f32)
    rest = value - one
    two = rest.astype(bf16).astype(f32)
    return one, two, rest - two


def attend_forward_kernel(
    tok_hbm, pos_hbm, w3, off, seg, pad,
    packed, ctx_hbm, qa_hbm, qw_hbm, ka_hbm, va_hbm, rank, bounds,
    tok, pos, raw, ctx_pair, qa, qw, ka, va, wqd, wkd, compact, dst, load_sem, save_sem,
):
    loads = []
    for part in range(4):
        rows = pl.ds(1024 * part, 1024)
        for which, (source, target) in enumerate(((tok_hbm, tok), (pos_hbm, pos))):
            copy = pltpu.make_async_copy(
                source.at[rows], target.at[rows], load_sem.at[2 * part + which]
            )
            copy.start()
            loads.append(copy)
    lane = iota((256, 128), 1)
    for which, spread in ((0, wqd), (1, wkd)):
        base = w3[which].astype(f32)
        left = pltpu.roll(base, 32, 1)
        right = pltpu.roll(base, 96, 1)
        spread[:, :128] = jnp.where(lane < 32, base, jnp.where(lane < 64, left, 0.0)).astype(bf16)
        spread[:, 128:] = jnp.where(lane < 32, right, jnp.where(lane < 64, base, 0.0)).astype(bf16)
    lane8 = iota((8, 128), 1)
    off_rows = off[...]
    off_left = pltpu.roll(off_rows, 32, 1)
    off_right = pltpu.roll(off_rows, 96, 1)
    q_bias = jnp.concatenate(
        [
            jnp.where(lane8 < 32, off_rows, jnp.where(lane8 < 64, off_left, 0.0))[0:1],
            jnp.where(lane8 < 32, off_right, jnp.where(lane8 < 64, off_rows, 0.0))[0:1],
        ],
        axis=1,
    )
    v_bias = jnp.where(lane8 < 64, off_rows, 0.0)[1:2]

    segment = seg[...]
    open_key = jnp.where(pad[...] == 0, 1.0, 0.0)
    grid_row = iota((32, 128), 0)
    before = (iota((128, 128), 0) < iota((128, 128), 1)).astype(bf16)
    in_row = mm(open_key.astype(bf16), before)
    row_total = jnp.broadcast_to(jnp.sum(open_key, axis=1, keepdims=True), (32, 128))
    above = (iota((32, 32), 1) < iota((32, 32), 0)).astype(bf16)
    place = (in_row + mm(above, row_total.astype(bf16))).astype(jnp.int32)
    place = jnp.where(open_key > 0.5, place, -1)
    for r in range(32):
        rank[r, :, :] = place[r : r + 1, :]
    for s in range(IMAGES + 1):
        if s == 0:
            bounds[0] = 0
            bounds[8] = 0
        else:
            low = (segment < s).astype(f32)
            bounds[s] = jnp.sum(low).astype(jnp.int32)
            bounds[8 + s] = jnp.sum(low * open_key).astype(jnp.int32)
    for i in range(16):
        dst[i] = jnp.sum(jnp.where(grid_row < 2 * i, open_key, 0.0)).astype(jnp.int32)
    for i in range(16):
        bounds[16 + i] = dst[i]
    total = bounds[8 + IMAGES]

    lane_row = iota((1, 128), 1)
    q_from = jnp.full((1, 128), SPAN, jnp.int32)
    q_to = jnp.full((1, 128), SPAN, jnp.int32)
    k_from = jnp.full((1, 128), SPAN, jnp.int32)
    k_to = jnp.full((1, 128), SPAN, jnp.int32)
    for s in range(IMAGES):
        at = lane_row == 64 + s
        q_from = jnp.where(at, bounds[s], q_from)
        q_to = jnp.where(at, bounds[s + 1], q_to)
        k_from = jnp.where(at, bounds[8 + s], k_from)
        k_to = jnp.where(at, bounds[9 + s], k_to)

    compact[pl.ds(0, 16), :] = jnp.zeros((16, 512), bf16)
    qa[:, pl.ds(PACK_ROWS, SPAN - PACK_ROWS), :] = jnp.zeros((2, SPAN - PACK_ROWS, 128), bf16)
    qw[pl.ds(PACK_ROWS, SPAN - PACK_ROWS), :] = jnp.zeros((SPAN - PACK_ROWS, 128), bf16)

    lane_q = iota((256, 128), 1)
    row_q = iota((256, 128), 0)

    def project(i, _):
        first = pl.multiple_of(i * 256, 256)
        rows = pl.ds(first, 256)
        token = tok[rows, :]
        query_in = (token.astype(f32) + pos[rows, :].astype(f32)).astype(bf16)
        both = (mm(query_in, wqd[...]) + q_bias).astype(bf16).astype(f32)
        here = row_q + first
        outside = (here < q_from) | (here >= q_to)
        feature = jnp.where(
            lane_q < 64 + IMAGES, jnp.where(outside, 1.0, 0.0), jnp.where(lane_q == 69, 1.0, 0.0)
        )
        for h in range(2):
            exact = both[:, 128 * h : 128 * h + 128] * LOG_SCALE
            high = exact.astype(bf16).astype(f32)
            qa[h, rows, :] = jnp.where(
                lane_q < 32, high, jnp.where(lane_q < 64, exact - high, feature)
            ).astype(bf16)
        qw[rows, :] = jnp.where(
            lane_q < 32, both[:, :128], jnp.where(lane_q < 64, both[:, 128:], 0.0)
        ).astype(bf16)
        start = dst[i]
        aligned = pl.multiple_of((start // 16) * 16, 16)
        places = jnp.concatenate([rank[2 * i], rank[2 * i + 1]], axis=1)
        hot = jnp.where(iota((272, 256), 0) + aligned == places, 1.0, 0.0).astype(bf16)
        moved = mm(hot, jnp.concatenate([query_in, token], axis=1)).astype(bf16)
        head = pl.ds(aligned, 16)
        compact[head, :] = compact[head, :] + moved[:16]
        compact[pl.ds(pl.multiple_of(aligned + 16, 16), 256), :] = moved[16:]
        return 0

    for part in range(4):
        loads[2 * part].wait()
        loads[2 * part + 1].wait()
        lax.fori_loop(2 * part, 2 * part + 2, twice(project), 0)

    lane_k = iota((512, 128), 1)
    row_k = iota((512, 128), 0)

    def project_keys(i, _):
        first = pl.multiple_of(i * 512, 512)
        rows = pl.ds(first, 512)
        here = row_k + first
        real = here < total
        both = mm(compact[rows, 0:256], wkd[...])
        value = mm(compact[rows, 256:512], w3[2]) + v_bias
        value = jnp.where(real, value, 0.0)
        inside = (here >= k_from) & (here < k_to)
        feature = jnp.where(inside, -FENCE, 0.0)
        feature = jnp.where(lane_k == 69, jnp.where(real, 0.0, -FENCE), feature)
        for h in range(2):
            spot = (lane_k >= 70 + 3 * h) & (lane_k < 73 + 3 * h)
            key = jnp.where(real, both[:, 128 * h : 128 * h + 128], 0.0)
            ka[h, rows, :] = jnp.where(
                lane_k < 64, key, jnp.where(spot, 1.0, feature)
            ).astype(bf16)
        va[0, rows, :] = jnp.where(
            lane_k < 32, value, jnp.where(lane_k < 35, 1.0, 0.0)
        ).astype(bf16)
        va[1, rows, :] = jnp.where(
            lane_k < 3, 1.0, jnp.where((lane_k >= 32) & (lane_k < 64), value, 0.0)
        ).astype(bf16)
        return 0

    lax.fori_loop(0, (total + 767) // 512, project_keys, 0)
    saves = [
        pltpu.make_async_copy(source, target, save_sem.at[n])
        for n, (source, target) in enumerate(
            ((qw, qw_hbm), (ka, ka_hbm), (va, va_hbm), (qa, qa_hbm), (ctx_pair, ctx_hbm))
        )
    ]
    for copy in saves[:3]:
        copy.start()

    def per_segment(safe, s, _):
        q_start, q_end = bounds[s], bounds[s + 1]
        k_start, k_end = bounds[8 + s], bounds[9 + s]
        q_first = (q_start // 16) * 16
        k_first = (k_start // 16) * 16

        def per_query(size, base, i, _):
            q_row = pl.multiple_of(base + i * size, 16)
            q_rows = pl.ds(q_row, size)
            head = pl.ds(q_row, 16)
            kept = iota((16, 128), 0) + q_row < q_start
            olds = [raw[h, head, :] for h in range(2)]
            for h in range(2):
                raw[h, q_rows, :] = jnp.zeros((size, 128), f32)

            def per_key(tops, span, first_key, j, _):
                k_rows = pl.ds(pl.multiple_of(first_key + j * span, 16), span)
                for h in range(2):
                    score = mm(qa[h, q_rows, :], ka[h, k_rows, :], NT)
                    if tops is not None:
                        score = score - tops[h]
                    weight = jnp.exp2(score).astype(bf16)
                    raw[h, q_rows, :] += mm(weight, va[h, k_rows, :])
                return 0

            def peak(j, tops):
                k_rows = pl.ds(pl.multiple_of(k_first + j * 256, 16), 256)
                out = []
                for h in range(2):
                    score = mm(qa[h, q_rows, :], ka[h, k_rows, :], NT)
                    out.append(jnp.maximum(tops[h], jnp.max(score, axis=1, keepdims=True)))
                return tuple(out)

            if safe:
                steps = (k_end - k_first + 255) // 256
                low = jnp.full((size, 1), -3.0e38, f32)
                tops = lax.fori_loop(0, steps, peak, (low, low))
                lane = iota((size, 128), 1)
                raw[0, q_rows, :] = jnp.where(
                    lane == 64, tops[0], jnp.where(lane == 65, tops[1], 0.0)
                )
                lax.fori_loop(0, steps, functools.partial(per_key, tops, 256, k_first), 0)
            else:
                for span, offset, count in plan(k_end - k_first, FORWARD_KEY):
                    lax.fori_loop(
                        0, count, functools.partial(per_key, None, span, k_first + offset), 0
                    )
            for h in range(2):
                raw[h, head, :] = jnp.where(kept, olds[h], raw[h, head, :])
            return 0

        for size, offset, count in plan(q_end - q_first, FORWARD_QUERY):
            lax.fori_loop(0, count, functools.partial(per_query, size, q_first + offset), 0)
        return 0

    lax.fori_loop(0, IMAGES, functools.partial(per_segment, False), 0)

    def extremes(i, carry):
        rows = pl.ds(pl.multiple_of(i * 512, 512), 512)
        lane = iota((512, 128), 1)
        both = jnp.where(lane == 32, raw[0, rows, :], jnp.where(lane == 0, raw[1, rows, :], 1.0))
        return (
            jnp.maximum(carry[0], jnp.max(both, axis=0, keepdims=True)),
            jnp.minimum(carry[1], jnp.min(both, axis=0, keepdims=True)),
        )

    one_row = jnp.ones((1, 128), f32)
    most, least = lax.fori_loop(0, 8, extremes, (one_row, one_row))
    fine = (jnp.max(most) < LARGE) & (jnp.min(least) > SMALL)

    @pl.when(jnp.logical_not(fine))
    def _():
        lax.fori_loop(0, IMAGES, functools.partial(per_segment, True), 0)

    def close(b, _):
        rows = pl.ds(pl.multiple_of(b * 256, 256), 256)
        pair_rows = pl.ds(pl.multiple_of(b * 128, 128), 128)
        lane = iota((256, 128), 1)
        zero, one = raw[0, rows, :], raw[1, rows, :]
        l_zero = jnp.broadcast_to(zero[:, 32:33], (256, 128))
        l_one = jnp.broadcast_to(one[:, 0:1], (256, 128))
        lower = lane < 32
        joined = jnp.where(lower, zero, one) / jnp.where(lower, l_zero, l_one)
        early = lane < 73
        shift = jnp.where(
            early,
            jnp.broadcast_to(zero[:, 64:65], (256, 128)),
            jnp.broadcast_to(zero[:, 65:66], (256, 128)),
        )
        parts = pieces_of(-(shift + jnp.log2(jnp.where(early, l_zero, l_one))))
        for h in range(2):
            at = 70 + 3 * h
            value = qa[h, rows, :].astype(f32)
            for n in range(3):
                value = jnp.where(lane == at + n, parts[n], value)
            qa[h, rows, :] = value.astype(bf16)
        pair = jnp.where(
            iota((128, 128), 1) < 64, joined[0:128], pltpu.roll(joined[128:256], 64, 1)
        )
        ctx_pair[pair_rows, :] = pair
        packed[pair_rows, :] = pair.astype(bf16)
        return 0

    lax.fori_loop(0, 8, twice(close), 0)
    for copy in saves[3:]:
        copy.start()
    for copy in saves:
        copy.wait()


VMEM_SPEC = pl.BlockSpec(memory_space=pltpu.VMEM)
SMEM_SPEC = pl.BlockSpec(memory_space=pltpu.SMEM)
ANY_SPEC = pl.BlockSpec(memory_space=pl.ANY)


def attend_forward(tokens, positions, w3, off, segment, padding):
    return pl.pallas_call(
        attend_forward_kernel,
        out_shape=(
            jax.ShapeDtypeStruct((2048, 128), bf16),
            jax.ShapeDtypeStruct((2048, 128), f32),
            jax.ShapeDtypeStruct((2, SPAN, 128), bf16),
            jax.ShapeDtypeStruct((SPAN, 128), bf16),
            jax.ShapeDtypeStruct((2, SPAN, 128), bf16),
            jax.ShapeDtypeStruct((2, SPAN, 128), bf16),
            jax.ShapeDtypeStruct((32, 1, 128), jnp.int32),
            jax.ShapeDtypeStruct((32,), jnp.int32),
        ),
        in_specs=[ANY_SPEC] * 2 + [VMEM_SPEC] * 4,
        out_specs=[VMEM_SPEC] + [ANY_SPEC] * 5 + [VMEM_SPEC, SMEM_SPEC],
        scratch_shapes=[
            pltpu.VMEM((PACK_ROWS, 256), bf16),
            pltpu.VMEM((PACK_ROWS, 256), bf16),
            pltpu.VMEM((2, SPAN, 128), f32),
            pltpu.VMEM((2048, 128), f32),
            pltpu.VMEM((2, SPAN, 128), bf16),
            pltpu.VMEM((SPAN, 128), bf16),
            pltpu.VMEM((2, SPAN, 128), bf16),
            pltpu.VMEM((2, SPAN, 128), bf16),
            pltpu.VMEM((256, 256), bf16),
            pltpu.VMEM((256, 256), bf16),
            pltpu.VMEM((SPAN, 512), bf16),
            pltpu.SMEM((16,), jnp.int32),
            pltpu.SemaphoreType.DMA((8,)),
            pltpu.SemaphoreType.DMA((5,)),
        ],
        compiler_params=pltpu.CompilerParams(vmem_limit_bytes=LIMIT_FORWARD),
        cost_estimate=pl.CostEstimate(
            flops=20 * 10**9, bytes_accessed=20 * 10**6, transcendentals=10**7
        ),
    )(tokens, positions, w3, off, segment.reshape(32, 128), padding.reshape(32, 128))


def attend_backward_kernel(
    packed, ctx_hbm, qa_hbm, qw_hbm, ka_hbm, va_hbm, rank, bounds,
    gq, gkv,
    ctx, qa, qw, ka, va, do, kw, dq, dkv, turned_sum, load_sem,
):
    loads = [
        pltpu.make_async_copy(source, target, load_sem.at[n])
        for n, (source, target) in enumerate(
            ((ctx_hbm, ctx), (qa_hbm, qa), (ka_hbm, ka), (va_hbm, va), (qw_hbm, qw))
        )
    ]
    for copy in loads:
        copy.start()
    for i in range(SPAN // 512):
        rows = pl.ds(512 * i, 512)
        dq[rows, :] = jnp.zeros((512, 128), f32)
        dkv[rows, :] = jnp.zeros((512, 128), f32)
    do[:, pl.ds(PACK_ROWS, SPAN - PACK_ROWS), :] = jnp.zeros((2, SPAN - PACK_ROWS, 128), bf16)
    loads[0].wait()
    lane = iota((128, 128), 1)
    for b in range(16):
        pair = packed[pl.ds(128 * b, 128), :].astype(f32)
        product = pair * ctx[pl.ds(128 * b, 128), :]
        for half in range(2):
            rows = pl.ds(256 * b + 128 * half, 128)
            grad = pair if half == 0 else pltpu.roll(pair, 64, 1)
            at = 64 * half
            tails = []
            for h in range(2):
                inside = (lane >= at + 32 * h) & (lane < at + 32 * h + 32)
                delta = jnp.sum(jnp.where(inside, product, 0.0), axis=1, keepdims=True)
                one, two, three = pieces_of(-jnp.broadcast_to(delta, (128, 128)))
                spot = 32 - 32 * h
                tails.append(jnp.where(lane == spot, one, jnp.where(lane == spot + 1, two, three)))
            do[0, rows, :] = jnp.where(
                lane < 32, grad, jnp.where(lane < 35, tails[0], 0.0)
            ).astype(bf16)
            do[1, rows, :] = jnp.where(
                lane < 3, tails[1], jnp.where((lane >= 32) & (lane < 64), grad, 0.0)
            ).astype(bf16)
    for copy in loads[1:]:
        copy.wait()

    def per_segment(s, _):
        q_start, q_end = bounds[s], bounds[s + 1]
        k_start, k_end = bounds[8 + s], bounds[9 + s]
        q_first = (q_start // 16) * 16
        k_first = (k_start // 16) * 16
        q_plan = plan(q_end - q_first, BACK_QUERY)

        def per_key(span, first_key, j, _):
            k_row = pl.multiple_of(first_key + j * span, 16)
            k_rows = pl.ds(k_row, span)
            lane = iota((span, 128), 1)
            at = iota((span, 128), 0) + k_row
            mine = (at >= k_start) & (at < k_end)
            here = pl.ds(0, span)
            for h in range(2):
                mask = mine & (lane >= 32 * h) & (lane < 32 * h + 32)
                kw[h, here, :] = jnp.where(mask, ka[h, k_rows, :].astype(f32), 0.0).astype(bf16)

            turned_sum[:, here] = jnp.zeros((128, span), f32)

            def per_query(size, first_row, i, _):
                q_rows = pl.ds(pl.multiple_of(first_row + i * size, 16), size)
                for h in range(2):
                    score = mm(qa[h, q_rows, :], ka[h, k_rows, :], NT)
                    prob = jnp.exp2(score)
                    prob_grad = mm(do[h, q_rows, :], va[h, k_rows, :], NT)
                    score_grad = (prob * prob_grad).astype(bf16)
                    dq[q_rows, :] += mm(score_grad, kw[h, here, :])
                    cols = slice(32 * h, 32 * h + 32)
                    turned_sum[32 * h : 32 * h + 32, here] += mm(qw[q_rows, cols], score_grad, TN)
                    turned_sum[64 + 32 * h : 96 + 32 * h, here] += mm(
                        do[h, q_rows, cols], prob.astype(bf16), TN
                    )
                return 0

            for size, offset, count in q_plan:
                lax.fori_loop(0, count, functools.partial(per_query, size, q_first + offset), 0)
            fresh = turned_sum[:, here].T
            dkv[k_rows, :] = dkv[k_rows, :] + jnp.where(mine, fresh, 0.0)
            return 0

        for span, offset, count in plan(k_end - k_first, BACK_KEY):
            lax.fori_loop(0, count, functools.partial(per_key, span, k_first + offset), 0)
        return 0

    lax.fori_loop(0, IMAGES, per_segment, 0)

    def emit(i, _):
        rows = pl.ds(pl.multiple_of(i * 256, 256), 256)
        gq[rows, :] = (dq[rows, :] * HEAD_DIM**-0.5).astype(bf16)
        start = bounds[16 + i]
        aligned = pl.multiple_of((start // 16) * 16, 16)
        places = jnp.concatenate([rank[2 * i], rank[2 * i + 1]], axis=1)
        hot = jnp.where(iota((272, 256), 0) + aligned == places, 1.0, 0.0).astype(bf16)
        piece = dkv[pl.ds(aligned, 272), :]
        scale = jnp.where(iota((272, 128), 1) < 64, HEAD_DIM**-0.5, 1.0)
        gkv[rows, :] = mm(hot, (piece * scale).astype(bf16), TN).astype(bf16)
        return 0

    lax.fori_loop(0, 8, twice(emit), 0)


def attend_backward(packed, ctx, qa, qw, ka, va, rank, bounds):
    return pl.pallas_call(
        attend_backward_kernel,
        out_shape=(
            jax.ShapeDtypeStruct((PACK_ROWS, 128), bf16),
            jax.ShapeDtypeStruct((PACK_ROWS, 128), bf16),
        ),
        in_specs=[VMEM_SPEC] + [ANY_SPEC] * 5 + [VMEM_SPEC, SMEM_SPEC],
        out_specs=[VMEM_SPEC] * 2,
        scratch_shapes=[
            pltpu.VMEM((2048, 128), f32),
            pltpu.VMEM((2, SPAN, 128), bf16),
            pltpu.VMEM((SPAN, 128), bf16),
            pltpu.VMEM((2, SPAN, 128), bf16),
            pltpu.VMEM((2, SPAN, 128), bf16),
            pltpu.VMEM((2, SPAN, 128), bf16),
            pltpu.VMEM((2, BACK_KEY[0], 128), bf16),
            pltpu.VMEM((SPAN, 128), f32),
            pltpu.VMEM((SPAN, 128), f32),
            pltpu.VMEM((128, BACK_KEY[0]), f32),
            pltpu.SemaphoreType.DMA((5,)),
        ],
        compiler_params=pltpu.CompilerParams(vmem_limit_bytes=LIMIT_BACKWARD),
        cost_estimate=pl.CostEstimate(
            flops=50 * 10**9, bytes_accessed=20 * 10**6, transcendentals=10**7
        ),
    )(packed, ctx, qa, qw, ka, va, rank, bounds)


STEP = 10


neg_fill = -1e30
norm_eps = 1e-05
beta_one = 0.5
beta_two = 0.5
adam_eps = 1e-08
decay_rate = 0.0001
step_rates = (0.06, 0.15, 0.06, 0.03, 0.1, 0.1, 0.1)


def product(left_side, right_side):
    return jnp.dot(left_side, right_side, preferred_element_type=jnp.float32)


def product_left(left_side, right_side):
    return lax.dot_general(
        left_side, right_side, (((0,), (0,)), ((), ())), preferred_element_type=jnp.float32
    )


def product_right(left_side, right_side):
    return lax.dot_general(
        left_side, right_side, (((1,), (1,)), ((), ())), preferred_element_type=jnp.float32
    )


def smooth_unit(values):
    return jax.nn.gelu(values, approximate=False)


def norm_forward(values, gain_row, shift_row):
    center = values - jnp.mean(values, axis=-1, keepdims=True)
    inverse = lax.rsqrt(jnp.mean(center * center, axis=-1, keepdims=True) + norm_eps)
    scaled = center * inverse
    return (scaled * gain_row + shift_row, scaled, inverse)


def norm_backward(upstream, scaled, inverse, gain_row):
    spread = upstream * gain_row
    centred = (
        spread
        - jnp.mean(spread, axis=-1, keepdims=True)
        - scaled * jnp.mean(spread * scaled, axis=-1, keepdims=True)
    )
    return (inverse * centred, jnp.sum(upstream * scaled, axis=0), jnp.sum(upstream, axis=0))


def summed(partial_value):
    return lax.psum(partial_value, "tensor")


def adamw(master, gradient, old_first, old_second, step_rate):
    momentum = beta_one * old_first + (1.0 - beta_one) * gradient
    variance = beta_two * old_second + (1.0 - beta_two) * gradient * gradient
    normal_step = (
        momentum / (1.0 - beta_one**STEP) / (jnp.sqrt(variance / (1.0 - beta_two**STEP)) + adam_eps)
    )
    return (master - step_rate * (normal_step + decay_rate * master), momentum, variance)


MESH = pl.DeviceIdType.MESH
SHARD_ROWS = 304
GROUPS = 16
CHUNK = 256
CHUNKS = 4
STEPS = 4
BLOCK = 1024 // STEPS
PAIRS = BLOCK // 2
OWN_ROWS = CHUNK * CHUNKS


def greet(peers):
    barrier = pltpu.get_barrier_semaphore()
    for peer in peers:
        pl.semaphore_signal(barrier, inc=1, device_id=peer, device_id_type=MESH)
    return lambda: pl.semaphore_wait(barrier, len(peers))


def remote(source, target, send_sem, recv_sem, peer):
    return pltpu.make_async_remote_copy(
        src_ref=source,
        dst_ref=target,
        send_sem=send_sem,
        recv_sem=recv_sem,
        device_id=peer,
        device_id_type=MESH,
    )


def gather_kernel(
    up_hbm, down_hbm, outer, vec, shift, inward, off,
    pack, w3, offs,
    up, down, local_sem, small, one, send_buf, recv_buf, send_sem, recv_sem,
):
    me = lax.axis_index("dp")
    peers = [lax.rem(me + k, 8) for k in range(1, 8)]
    ready = greet([{"dp": p} for p in peers])
    loads = [
        pltpu.make_async_copy(up_hbm, up, local_sem.at[16]),
        pltpu.make_async_copy(down_hbm, down, local_sem.at[17]),
    ]
    for copy in loads:
        copy.start()
    send_buf[...] = jnp.zeros((112, 128), bf16)
    for which in range(3):
        send_buf[32 * which : 32 * which + 32, 0:64] = inward[which].astype(bf16)
    small[...] = jnp.zeros((3, 16, 128), f32)
    small[0, 0:2, 0:8] = off[...]
    small[1, 0:6, 0:32] = vec[...]
    small[2, 6:7, 0:64] = shift[...]
    send_buf[96:112, :] = pltpu.roll(small[0], me * 8, 1).astype(bf16)
    recv_buf[me] = send_buf[...]
    ready()
    copies = []
    for k, peer in enumerate(peers):
        copy = remote(
            send_buf, recv_buf.at[me], send_sem.at[k], recv_sem.at[me], {"dp": peer}
        )
        copy.start()
        copies.append(copy)
    for copy in loads:
        copy.wait()
    for b in range(4):
        one[32 * b : 32 * b + 32, :] = up[:, 128 * b : 128 * b + 128].astype(bf16)
        one[128 + 32 * b : 160 + 32 * b, :] = down[:, 128 * b : 128 * b + 128].astype(bf16)
    one[256:304, :] = jnp.zeros((48, 128), bf16)
    one[256:288, 0:64] = outer[...].astype(bf16)
    placed = pltpu.roll(small[1], lax.rem(me, 4) * 32, 1)
    placed = placed + pltpu.roll(small[2], lax.rem(me, 2) * 64, 1)
    one[288:304, :] = placed.astype(bf16)
    spreads = [
        pltpu.make_async_copy(one, pack.at[j], local_sem.at[j]) for j in range(GROUPS)
    ]
    for copy in spreads:
        copy.start()
    for peer in peers:
        remote(
            send_buf, recv_buf.at[peer], send_sem.at[0], recv_sem.at[peer], {"dp": peer}
        ).wait_recv()
    total = jnp.zeros((16, 128), f32)
    for d in range(8):
        for which in range(3):
            w3[which, 32 * d : 32 * d + 32, :] = recv_buf[d, 32 * which : 32 * which + 32, :]
        total = total + recv_buf[d, 96:112, :].astype(f32)
    offs[...] = total[0:8]
    for copy in copies:
        copy.wait_send()
    for copy in spreads:
        copy.wait()


def gather_weights(upward, down_t, out_t, vectors, shifts, inward, offsets):
    return pl.pallas_call(
        gather_kernel,
        out_shape=(
            jax.ShapeDtypeStruct((GROUPS, SHARD_ROWS, 128), bf16),
            jax.ShapeDtypeStruct((3, 256, 128), bf16),
            jax.ShapeDtypeStruct((8, 128), f32),
        ),
        in_specs=[ANY_SPEC] * 2 + [VMEM_SPEC] * 5,
        out_specs=[ANY_SPEC] + [VMEM_SPEC] * 2,
        scratch_shapes=[
            pltpu.VMEM((32, 512), f32),
            pltpu.VMEM((32, 512), f32),
            pltpu.SemaphoreType.DMA((18,)),
            pltpu.VMEM((3, 16, 128), f32),
            pltpu.VMEM((SHARD_ROWS, 128), bf16),
            pltpu.VMEM((112, 128), bf16),
            pltpu.VMEM((8, 112, 128), bf16),
            pltpu.SemaphoreType.DMA((7,)),
            pltpu.SemaphoreType.DMA((8,)),
        ],
        compiler_params=pltpu.CompilerParams(
            collective_id=0, has_side_effects=True, vmem_limit_bytes=LIMIT_GATHER
        ),
    )(upward, down_t, out_t, vectors, shifts, inward, offsets)


def norm_rows(values):
    center = values - jnp.mean(values, axis=1, keepdims=True)
    inverse = lax.rsqrt(jnp.mean(center * center, axis=1, keepdims=True) + norm_eps)
    return center * inverse, inverse


def norm_rows_back(spread, scaled, inverse):
    return inverse * (
        spread
        - jnp.mean(spread, axis=1, keepdims=True)
        - scaled * jnp.mean(spread * scaled, axis=1, keepdims=True)
    )


def dense_kernel(
    ctxp_hbm, half_hbm, tok_hbm, cot_hbm,
    encoded, dctx, first_hbm, gout,
    ctxp, half, first, enc, stage, other, ctxs, up, down, out_a, out_b, vec, shift,
    tok, cot, grads_ctx, normed_low, second_low, first_a, first_b,
    active, hgrad, slope, sums, give, take, keep,
    w_sem, load_sem, ctx_send, ctx_recv, dctx_send, dctx_recv,
    local_sem, enc_sem, first_sem, g_sem,
):
    me = lax.axis_index("tensor")
    core = lax.rem(me, 2)
    sibling = me + 1 - 2 * core
    across = lax.rem(me + 2, 4)
    diagonal = lax.rem(sibling + 2, 4)
    order = (sibling, across, diagonal)
    ready = greet([{"tensor": p} for p in order])
    own = pl.multiple_of(me * OWN_ROWS, OWN_ROWS)
    load_tok = pltpu.make_async_copy(tok_hbm.at[pl.ds(own, OWN_ROWS)], tok, load_sem.at[0])
    load_cot = pltpu.make_async_copy(cot_hbm.at[pl.ds(own, OWN_ROWS)], cot, load_sem.at[1])
    load_half = pltpu.make_async_copy(half_hbm, half, load_sem.at[2])
    load_ctxp = pltpu.make_async_copy(ctxp_hbm, ctxp, load_sem.at[3])
    load_half.start()
    load_ctxp.start()
    load_tok.start()
    load_cot.start()
    load_ctxp.wait()
    ctxs[me] = ctxp[pl.ds(pl.multiple_of(me * 512, 512), 512), :]
    sums[...] = jnp.zeros((8, 256), f32)
    ready()
    weights = [
        remote(
            half.at[:, pl.ds(256, 48)], other.at[:, pl.ds(256, 48)],
            w_sem.at[0], w_sem.at[1], {"tensor": sibling},
        ),
        remote(
            half.at[:, pl.ds(0, 256)], other.at[:, pl.ds(0, 256)],
            w_sem.at[2], w_sem.at[3], {"tensor": sibling},
        ),
    ]
    load_half.wait()
    weights[0].start()

    def ctx_copy(peer, c):
        rows = pl.ds(pl.multiple_of(peer * 512 + c * PAIRS, PAIRS), PAIRS)
        return remote(
            ctxp.at[rows], ctxs.at[me, pl.ds(pl.multiple_of(c * PAIRS, PAIRS), PAIRS)],
            ctx_send.at[peer, c], ctx_recv.at[me, c], {"tensor": peer},
        )

    def ctx_arrival(peer, c):
        rows = pl.ds(pl.multiple_of(c * PAIRS, PAIRS), PAIRS)
        return remote(
            ctxp.at[rows], ctxs.at[peer, rows],
            ctx_send.at[peer, c], ctx_recv.at[peer, c], {"tensor": peer},
        )

    for peer in (across, diagonal, sibling):
        ctx_copy(peer, 0).start()
    weights[1].start()
    for c in range(1, STEPS):
        for peer in (across, diagonal, sibling):
            ctx_copy(peer, c).start()

    out_a[...] = jnp.zeros((256, 512), bf16)
    out_b[...] = jnp.zeros((256, 512), bf16)

    def unpack_small(source, t_of):
        for ty in range(2):
            t = t_of(ty)
            lanes = pl.ds(pl.multiple_of(t * 128, 128), 128)
            for d in range(8):
                piece = source[8 * ty + d, 256:288, :].astype(f32)
                out_a[32 * d : 32 * d + 32, lanes] = piece.astype(bf16)
                out_b[32 * d : 32 * d + 32, lanes] = pltpu.roll(piece, 64, 1).astype(bf16)
            for b in range(4):
                both = source[8 * ty + 2 * b, 288:304, :] + source[8 * ty + 2 * b + 1, 288:304, :]
                shift[:, pl.ds(pl.multiple_of(t * 512 + 128 * b, 128), 128)] = (
                    both.astype(f32)[6:7]
                )

    def unpack_large(source, t_of):
        for ty in range(2):
            t = t_of(ty)

            def one_row(d, _):
                rows = pl.ds(pl.multiple_of(d * 32, 32), 32)
                for b in range(4):
                    lanes = pl.ds(pl.multiple_of(t * 512 + 128 * b, 128), 128)
                    up[rows, lanes] = source[8 * ty + d, 32 * b : 32 * b + 32, :]
                    down[rows, lanes] = source[8 * ty + d, 128 + 32 * b : 160 + 32 * b, :]
                return 0

            lax.fori_loop(0, 8, one_row, 0)

    mine_t = lambda ty: 2 * ty + core
    other_t = lambda ty: 2 * ty + 1 - core
    for b in range(2):
        total = jnp.zeros((16, 128), f32)
        for d in range(4 * b, 4 * b + 4):
            total = total + half[d, 288:304, :].astype(f32)
        vec[:, 128 * b : 128 * b + 128] = total[0:8]
    unpack_small(half, mine_t)
    unpack_large(half, mine_t)
    weights[0].wait_recv()
    unpack_small(other, other_t)
    weights[1].wait_recv()
    unpack_large(other, other_t)
    load_tok.wait()
    load_cot.wait()

    def enc_store(c):
        rows = pl.ds(pl.multiple_of(c * BLOCK, BLOCK), BLOCK)
        return pltpu.make_async_copy(enc.at[rows], encoded.at[rows], enc_sem.at[c])

    def first_store(c):
        rows = pl.ds(pl.multiple_of(c * BLOCK, BLOCK), BLOCK)
        return pltpu.make_async_copy(first.at[rows], first_hbm.at[rows], first_sem.at[c])

    def dctx_copy(peer, c):
        rows = pl.ds(pl.multiple_of(c * PAIRS, PAIRS), PAIRS)
        return remote(
            grads_ctx.at[peer, rows],
            dctx.at[pl.ds(pl.multiple_of(me * 512 + c * PAIRS, PAIRS), PAIRS)],
            dctx_send.at[peer, c], dctx_recv.at[me, c], {"tensor": peer},
        )

    def dctx_arrival(peer, c):
        rows = pl.ds(pl.multiple_of(c * PAIRS, PAIRS), PAIRS)
        return remote(
            grads_ctx.at[peer, rows],
            dctx.at[pl.ds(pl.multiple_of(peer * 512 + c * PAIRS, PAIRS), PAIRS)],
            dctx_send.at[peer, c], dctx_recv.at[peer, c], {"tensor": peer},
        )

    def dctx_local(c):
        rows = pl.ds(pl.multiple_of(c * PAIRS, PAIRS), PAIRS)
        return pltpu.make_async_copy(
            grads_ctx.at[me, rows],
            dctx.at[pl.ds(pl.multiple_of(me * 512 + c * PAIRS, PAIRS), PAIRS)],
            local_sem.at[c],
        )

    def chunk_step(c, _):
        for peer in order:
            ctx_arrival(peer, c).wait_recv()
        rows = pl.ds(pl.multiple_of(c * BLOCK, BLOCK), BLOCK)
        pair_rows = pl.ds(pl.multiple_of(c * PAIRS, PAIRS), PAIRS)
        context = jnp.concatenate([ctxs[t, pair_rows, :] for t in range(4)], axis=1)
        upper, lower = mm(context, out_a[...], NT), mm(context, out_b[...], NT)
        attended = jnp.concatenate(
            [half_of[g : g + 128] for g in range(0, PAIRS, 128) for half_of in (upper, lower)],
            axis=0,
        )
        first_sum = tok[rows, :].astype(f32) + attended + vec[4:5]
        scaled_one, inverse_one = norm_rows(first_sum)
        normed = scaled_one * vec[0:1] + vec[1:2]
        low = normed.astype(bf16)
        normed_low[rows, :] = low
        for n in range(4):
            t = mine_t(n) if n < 2 else other_t(n - 2)
            span = pl.ds(pl.multiple_of(t * 512, 512), 512)
            hidden = mm(low, up[:, span]) + shift[:, span]
            cumulative = 0.5 * (1.0 + lax.erf(hidden * 0.7071067811865476))
            active[rows, span] = (hidden * cumulative).astype(bf16)
            slope[:, span] = cumulative + hidden * (
                0.3989422804014327 * jnp.exp(-0.5 * hidden * hidden)
            )
        second_sum = normed + mm(active[rows, :], down[...], NT) + vec[5:6]
        scaled_two, inverse_two = norm_rows(second_sum)
        enc[rows, :] = (scaled_two * vec[2:3] + vec[3:4]).astype(bf16)
        enc_store(c).start()
        upstream = cot[rows, :].astype(f32)
        second_grad = norm_rows_back(upstream * vec[2:3], scaled_two, inverse_two)
        low_two = second_grad.astype(bf16)
        second_low[rows, :] = low_two
        for n in range(4):
            span = slice(512 * n, 512 * n + 512)
            hgrad[rows, span] = (mm(low_two, down[:, span]) * slope[:, span]).astype(bf16)
        normed_grad = second_grad + mm(hgrad[rows, :], up[...], NT)
        first_grad = norm_rows_back(normed_grad * vec[0:1], scaled_one, inverse_one)
        first[rows, :] = first_grad
        first_store(c).start()
        low_one = first_grad.astype(bf16)
        parts = [
            jnp.concatenate([low_one[g + at : g + at + 128] for g in range(0, BLOCK, 256)], axis=0)
            for at in (0, 128)
        ]
        first_a[pair_rows, :] = parts[0]
        first_b[pair_rows, :] = parts[1]
        back = (mm(parts[0], out_a[...]) + mm(parts[1], out_b[...])).astype(bf16)
        for t in range(4):
            grads_ctx[t, pair_rows, :] = back[:, 128 * t : 128 * t + 128]
        for peer in (across, diagonal, sibling):
            dctx_copy(peer, c).start()
        dctx_local(c).start()
        fold = lambda value: jnp.sum(value, axis=0, keepdims=True)
        sums[0:1] += fold(normed_grad * scaled_one)
        sums[1:2] += fold(normed_grad)
        sums[2:3] += fold(upstream * scaled_two)
        sums[3:4] += fold(upstream)
        sums[4:5] += fold(first_grad)
        sums[5:6] += fold(second_grad)
        return 0

    lax.fori_loop(0, STEPS, chunk_step, 0)

    ones = jnp.ones((8, OWN_ROWS), bf16)

    def weight_grads(t, ty, target, kind):
        lanes = pl.ds(pl.multiple_of(t * 512, 512), 512)
        grad_up = mm(normed_low[...], hgrad[:, lanes], TN).astype(kind)
        grad_down = mm(second_low[...], active[:, lanes], TN).astype(kind)
        part_a = mm(first_a[...], ctxs[t], TN)
        part_b = pltpu.roll(mm(first_b[...], ctxs[t], TN), 64, 1)
        grad_out = jnp.where(iota((256, 128), 1) < 64, part_a + part_b, 0.0).astype(kind)
        shift_sum = mm(ones, hgrad[:, lanes])
        for d in range(8):
            j = 8 * ty + d
            block = slice(32 * d, 32 * d + 32)
            for b in range(4):
                cols = slice(128 * b, 128 * b + 128)
                target[j, 32 * b : 32 * b + 32, :] = grad_up[block, cols]
                target[j, 128 + 32 * b : 160 + 32 * b, :] = grad_down[block, cols]
            target[j, 256:288, :] = grad_out[block]
            vector = sums[:, 128 * (d // 4) : 128 * (d // 4) + 128]
            cols = slice(128 * (d // 2), 128 * (d // 2) + 128)
            last = jnp.where(iota((8, 128), 0) == 6, shift_sum[:, cols], vector)
            target[j, 288:304, :] = jnp.concatenate(
                [last, jnp.zeros((8, 128), f32)], axis=0
            ).astype(kind)

    def trade(ty):
        slots = pl.ds(8 * ty, 8)
        return remote(give.at[slots], take.at[slots], g_sem.at[ty], g_sem.at[2 + ty],
                      {"tensor": sibling})

    def weight_store(ty):
        slots = pl.ds(8 * ty, 8)
        return pltpu.make_async_copy(stage.at[slots], gout.at[slots], g_sem.at[4 + ty])

    for ty in range(2):
        weight_grads(other_t(ty), ty, give, bf16)
        trade(ty).start()
    for ty in range(2):
        weight_grads(mine_t(ty), ty, keep, f32)
    for ty in range(2):
        trade(ty).wait_recv()
        slots = slice(8 * ty, 8 * ty + 8)
        stage[slots] = (keep[slots] + take[slots].astype(f32)).astype(bf16)
        weight_store(ty).start()

    for copy in weights:
        copy.wait_send()
    for c in range(STEPS):
        for peer in order:
            ctx_copy(peer, c).wait_send()
            dctx_copy(peer, c).wait_send()
            dctx_arrival(peer, c).wait_recv()
        dctx_local(c).wait()
        enc_store(c).wait()
        first_store(c).wait()
    for ty in range(2):
        trade(ty).wait_send()
        weight_store(ty).wait()


def dense(ctxp, half, tokens, cotangent):
    dma = pltpu.SemaphoreType.DMA
    return pl.pallas_call(
        dense_kernel,
        out_shape=(
            jax.ShapeDtypeStruct((OWN_ROWS, 256), bf16),
            jax.ShapeDtypeStruct((PACK_ROWS // 2, 128), bf16),
            jax.ShapeDtypeStruct((OWN_ROWS, 256), f32),
            jax.ShapeDtypeStruct((GROUPS, SHARD_ROWS, 128), bf16),
        ),
        in_specs=[ANY_SPEC] * 4,
        out_specs=[ANY_SPEC] * 4,
        scratch_shapes=[
            pltpu.VMEM((PACK_ROWS // 2, 128), bf16),
            pltpu.VMEM((GROUPS, SHARD_ROWS, 128), bf16),
            pltpu.VMEM((OWN_ROWS, 256), f32),
            pltpu.VMEM((OWN_ROWS, 256), bf16),
            pltpu.VMEM((GROUPS, SHARD_ROWS, 128), bf16),
            pltpu.VMEM((GROUPS, SHARD_ROWS, 128), bf16),
            pltpu.VMEM((4, 512, 128), bf16),
            pltpu.VMEM((256, 2048), bf16),
            pltpu.VMEM((256, 2048), bf16),
            pltpu.VMEM((256, 512), bf16),
            pltpu.VMEM((256, 512), bf16),
            pltpu.VMEM((8, 256), f32),
            pltpu.VMEM((1, 2048), f32),
            pltpu.VMEM((OWN_ROWS, 256), bf16),
            pltpu.VMEM((OWN_ROWS, 256), bf16),
            pltpu.VMEM((4, 512, 128), bf16),
            pltpu.VMEM((OWN_ROWS, 256), bf16),
            pltpu.VMEM((OWN_ROWS, 256), bf16),
            pltpu.VMEM((512, 256), bf16),
            pltpu.VMEM((512, 256), bf16),
            pltpu.VMEM((OWN_ROWS, 2048), bf16),
            pltpu.VMEM((OWN_ROWS, 2048), bf16),
            pltpu.VMEM((BLOCK, 2048), f32),
            pltpu.VMEM((8, 256), f32),
            pltpu.VMEM((GROUPS, SHARD_ROWS, 128), bf16),
            pltpu.VMEM((GROUPS, SHARD_ROWS, 128), bf16),
            pltpu.VMEM((GROUPS, SHARD_ROWS, 128), f32),
            dma((4,)),
            dma((4,)),
            dma((4, STEPS)),
            dma((4, STEPS)),
            dma((4, STEPS)),
            dma((4, STEPS)),
            dma((STEPS,)),
            dma((STEPS,)),
            dma((STEPS,)),
            dma((6,)),
        ],
        compiler_params=pltpu.CompilerParams(
            collective_id=1, has_side_effects=True, vmem_limit_bytes=LIMIT_DENSE
        ),
        cost_estimate=pl.CostEstimate(
            flops=7 * 10**9, bytes_accessed=8 * 10**6, transcendentals=4 * 10**6
        ),
    )(ctxp, half, tokens, cotangent)


def tail_kernel(
    gq_hbm, gkv_hbm, tok_hbm, pos_hbm, w3, first_hbm,
    tg, gin,
    gq, gkv, tok, pos, first, load_sem,
    wall, near_send, near_recv, far_send, far_recv, mine, in_send, in_recv,
    n_send, n_recv, f_send, f_recv, t_send, t_recv, i_send, i_recv, local_sem,
):
    me = lax.axis_index("tensor")
    rank = lax.axis_index("dp")
    core = lax.rem(me, 2)
    sibling = me + 1 - 2 * core
    across = lax.rem(me + 2, 4)
    diagonal = lax.rem(sibling + 2, 4)
    peers = [lax.rem(rank + k, 8) for k in range(1, 8)]
    ready = greet(
        [{"tensor": sibling}, {"tensor": across}] + [{"dp": peer} for peer in peers]
    )
    loads = [
        pltpu.make_async_copy(source, target, load_sem.at[n])
        for n, (source, target) in enumerate(
            ((gq_hbm, gq), (gkv_hbm, gkv), (first_hbm, first), (tok_hbm, tok), (pos_hbm, pos))
        )
    ]
    for copy in loads:
        copy.start()
    lane = iota((256, 128), 1)
    wall[:, 0:128] = w3[0]
    wall[:, 128:256] = jnp.where(
        lane < 64, w3[1].astype(f32), pltpu.roll(w3[2].astype(f32), 64, 1)
    ).astype(bf16)

    def rows_of(even, odd, i):
        owner = jnp.where(lax.rem(i, 2) == 0, even, odd)
        return pl.ds(pl.multiple_of(owner * OWN_ROWS + (i // 2) * CHUNK, CHUNK), CHUNK)

    def slot(i):
        return pl.ds(pl.multiple_of(i * CHUNK, CHUNK), CHUNK)

    def partial(rows):
        return mm(jnp.concatenate([gq[rows, :], gkv[rows, :]], axis=1), wall[...], NT)

    def near_copy(i):
        return remote(near_send.at[slot(i)], near_recv.at[slot(i)],
                      n_send.at[i], n_recv.at[i], {"tensor": sibling})

    def far_copy(i):
        theirs = i + 1 - 2 * lax.rem(i, 2)
        return remote(far_send.at[slot(i)], far_recv.at[slot(theirs)],
                      f_send.at[i], f_recv.at[theirs], {"tensor": across})

    def far_arrival(i):
        return remote(far_send.at[slot(i)], far_recv.at[slot(i)],
                      f_send.at[i], f_recv.at[i], {"tensor": across})

    def share_copy(i):
        return remote(mine.at[slot(i)], tg.at[rows_of(across, me, i)],
                      t_send.at[i], t_recv.at[i], {"tensor": sibling})

    def share_arrival(i):
        return remote(mine.at[slot(i)], tg.at[rows_of(diagonal, sibling, i)],
                      t_send.at[i], t_recv.at[i], {"tensor": sibling})

    def keep_copy(i):
        return pltpu.make_async_copy(
            mine.at[slot(i)], tg.at[rows_of(across, me, i)], local_sem.at[i]
        )

    def first_stage(i, _):
        near_send[slot(i), :] = partial(rows_of(diagonal, sibling, i)).astype(bf16)
        near_copy(i).start()
        return 0

    def second_stage(i, _):
        value = partial(rows_of(across, me, i))
        odd = lax.rem(i, 2).astype(f32)
        half = pl.ds(pl.multiple_of((i // 2) * CHUNK, CHUNK), CHUNK)
        value = value + first[half, :] * odd
        near_copy(i).wait_recv()
        far_send[slot(i), :] = (value + near_recv[slot(i), :].astype(f32)).astype(bf16)
        far_copy(i).start()
        return 0

    loads[0].wait()
    loads[1].wait()
    ready()
    lax.fori_loop(0, 2, first_stage, 0)
    loads[2].wait()

    def both_stages(i, _):
        first_stage(i + 2, 0)
        second_stage(i, 0)
        return 0

    lax.fori_loop(0, 6, both_stages, 0)
    lax.fori_loop(6, 8, second_stage, 0)

    loads[3].wait()
    loads[4].wait()

    def inward_step(i, carry):
        left, right, total = carry
        rows = pl.ds(pl.multiple_of(i * 1024, 1024), 1024)
        token = tok[rows, :]
        query_in = (token.astype(f32) + pos[rows, :].astype(f32)).astype(bf16)
        both = jnp.concatenate([gq[rows, :], gkv[rows, :]], axis=1)
        left = left + mm(query_in, both, TN)
        right = right + mm(token, gkv[rows, :], TN)
        total = total + mm(jnp.ones((8, 1024), bf16), both)
        return left, right, total

    left, right, total = lax.fori_loop(
        0, 4, inward_step,
        (jnp.zeros((256, 256), f32), jnp.zeros((256, 128), f32), jnp.zeros((8, 256), f32)),
    )
    joined = jnp.concatenate([jnp.where(lane < 64, left[:, 0:128], right), left[:, 128:256]], 1)
    for d in range(8):
        in_send[d, 0:32, :] = joined[32 * d : 32 * d + 32]
        in_send[d, 32:40, :] = total
    in_copies = []
    for k, peer in enumerate(peers):
        copy = remote(
            in_send.at[peer], in_recv.at[rank], i_send.at[k], i_recv.at[rank], {"dp": peer}
        )
        copy.start()
        in_copies.append(copy)

    def third_stage(i, _):
        far_arrival(i).wait_recv()
        mine[slot(i), :] = (
            far_send[slot(i), :].astype(f32) + far_recv[slot(i), :].astype(f32)
        ).astype(bf16)
        share_copy(i).start()
        keep_copy(i).start()
        return 0

    def third_pair(i, _):
        third_stage(2 * i + 1, 0)
        third_stage(2 * i, 0)
        return 0

    lax.fori_loop(0, 4, third_pair, 0)

    gathered = in_send[rank]
    for peer in peers:
        remote(
            in_send.at[peer], in_recv.at[peer], i_send.at[0], i_recv.at[peer], {"dp": peer}
        ).wait_recv()
        gathered = gathered + in_recv[peer]
    gin[...] = gathered

    for copy in in_copies:
        copy.wait_send()

    def finish(i, _):
        near_copy(i).wait_send()
        far_copy(i).wait_send()
        share_copy(i).wait_send()
        keep_copy(i).wait()
        share_arrival(i).wait_recv()
        return 0

    lax.fori_loop(0, 8, finish, 0)


def tail(gq, gkv, tokens, positions, w3, first):
    dma = pltpu.SemaphoreType.DMA
    return pl.pallas_call(
        tail_kernel,
        out_shape=(
            jax.ShapeDtypeStruct((PACK_ROWS, 256), bf16),
            jax.ShapeDtypeStruct((40, 256), f32),
        ),
        in_specs=[ANY_SPEC] * 4 + [VMEM_SPEC, ANY_SPEC],
        out_specs=[ANY_SPEC, VMEM_SPEC],
        scratch_shapes=[
            pltpu.VMEM((PACK_ROWS, 128), bf16),
            pltpu.VMEM((PACK_ROWS, 128), bf16),
            pltpu.VMEM((PACK_ROWS, 256), bf16),
            pltpu.VMEM((PACK_ROWS, 256), bf16),
            pltpu.VMEM((OWN_ROWS, 256), f32),
            dma((5,)),
            pltpu.VMEM((256, 256), bf16),
        ]
        + [pltpu.VMEM((8 * CHUNK, 256), bf16)] * 5
        + [
            pltpu.VMEM((8, 40, 256), f32),
            pltpu.VMEM((8, 40, 256), f32),
            dma((8,)),
            dma((8,)),
            dma((8,)),
            dma((8,)),
            dma((8,)),
            dma((8,)),
            dma((7,)),
            dma((8,)),
            dma((8,)),
        ],
        compiler_params=pltpu.CompilerParams(
            collective_id=2, has_side_effects=True, vmem_limit_bytes=LIMIT_TAIL
        ),
        cost_estimate=pl.CostEstimate(
            flops=3 * 10**9, bytes_accessed=16 * 10**6, transcendentals=0
        ),
    )(gq, gkv, tokens, positions, w3, first)


def update_kernel(pieces, gin, narrow, *refs):
    blocks, refs = refs[0:4], refs[4:]
    masters, firsts, seconds = refs[0:7], refs[7:14], refs[14:21]
    wide_out, encoded = refs[21:23]
    grads, news, lows, moms, varis = (
        refs[23:30], refs[30:37], refs[37:41], refs[41:48], refs[48:55],
    )
    stage, sem = refs[55:57]
    me = lax.axis_index("dp")
    copies = []
    col = lax.axis_index("tensor")
    low, high = lax.rem(col, 2), col // 2
    owners = (col, 2 * high + 1 - low, 2 * (1 - high) + low, 2 * (1 - high) + 1 - low)
    for i in range(4):
        rows = pl.ds(pl.multiple_of(owners[i] * OWN_ROWS, OWN_ROWS), OWN_ROWS)
        copy = pltpu.make_async_copy(blocks[i], encoded.at[rows], sem.at[8 + i])
        copy.start()
        copies.append(copy)
    for i in range(8):
        rows = pl.ds(512 * i, 512)
        stage[rows, :] = narrow[rows, :].astype(f32)
        copy = pltpu.make_async_copy(stage.at[rows], wide_out.at[rows], sem.at[i])
        copy.start()
        copies.append(copy)

    def add(j, total):
        return total + pieces[j].astype(f32)

    total = lax.fori_loop(0, GROUPS, add, jnp.zeros((SHARD_ROWS, 128), f32))
    wide = gin[...]
    small = total[288:296]
    vec_grad = pltpu.roll(small, lax.rem(128 - lax.rem(me, 4) * 32, 128), 1)[0:6, 0:32]
    shift_grad = pltpu.roll(small, lax.rem(128 - lax.rem(me, 2) * 64, 128), 1)[6:7, 0:64]
    off_q = pltpu.roll(wide[32:40, 0:128], lax.rem(128 - me * 8, 128), 1)
    off_v = pltpu.roll(wide[32:40, 128:256], 64 - me * 8, 1)
    off_grad = jnp.where(iota((8, 128), 0) == 0, off_q, off_v)[0:2, 0:8]
    left, right = wide[0:32, 0:128], wide[0:32, 128:256]
    inward_grads = (left[:, 0:64], right[:, 0:64], pltpu.roll(left, 64, 1)[:, 0:64])
    joined = lambda base: jnp.concatenate(
        [total[base + 32 * b : base + 32 * b + 32] for b in range(4)], axis=1
    )
    plain = (None, total[256:288, 0:64], joined(0), joined(128), vec_grad, off_grad, shift_grad)

    def apply(index, at, gradient):
        new, momentum, variance = adamw(
            masters[index][at], gradient, firsts[index][at], seconds[index][at],
            step_rates[index],
        )
        grads[index][at] = gradient
        news[index][at] = new
        moms[index][at] = momentum
        varis[index][at] = variance
        if index < 4:
            lows[index][at] = new.astype(bf16)

    for which in range(3):
        apply(0, which, inward_grads[which])
    for index in range(1, 7):
        apply(index, Ellipsis, plain[index])
    for copy in copies:
        copy.wait()


def update(pieces, gin, narrow, blocks, masters, firsts, seconds):
    shapes = [m.shape for m in masters]
    of = lambda kind, count: [jax.ShapeDtypeStruct(s, kind) for s in shapes[:count]]
    out = [
        jax.ShapeDtypeStruct((PACK_ROWS, 256), f32),
        jax.ShapeDtypeStruct((PACK_ROWS, 256), bf16),
    ]
    out = out + of(f32, 7) + of(f32, 7) + of(bf16, 4) + of(f32, 7) + of(f32, 7)
    return pl.pallas_call(
        update_kernel,
        out_shape=out,
        in_specs=[VMEM_SPEC] * 28,
        out_specs=[ANY_SPEC] * 2 + [VMEM_SPEC] * (len(out) - 2),
        scratch_shapes=[pltpu.VMEM((PACK_ROWS, 256), f32), pltpu.SemaphoreType.DMA((12,))],
        compiler_params=pltpu.CompilerParams(vmem_limit_bytes=LIMIT_UPDATE),
    )(pieces, gin, narrow, *blocks, *masters, *firsts, *seconds)


def exchange(pieces):
    groups = [[4 * d + 2 * y + c for y in range(2) for d in range(8)] for c in range(2)]
    return lax.all_to_all(
        pieces, ("dp", "tensor"), 0, 0, axis_index_groups=groups, tiled=True
    )


def turned(group):
    inward, outward, upward, downward, vectors, offsets, shifts = group
    return [inward, outward.T, upward, downward.T, vectors, offsets, shifts.reshape(1, -1)]


def returned(group):
    if len(group) == 4:
        return [group[0], group[1].T, group[2], group[3].T]
    inward, outward, upward, downward, vectors, offsets, shifts = group
    return [inward, outward.T, upward, downward.T, vectors, offsets, shifts.reshape(-1)]


def body_pods(tokens, positions, segment_ids, pad_flags, cotangent, *state):
    masters, firsts, seconds = (turned(state[7 * i : 7 * i + 7]) for i in range(3))
    inward, out_t, upward, down_t, vectors, offsets, shifts = masters
    pack, w3, off = gather_weights(upward, down_t, out_t, vectors, shifts, inward, offsets)
    half = exchange(pack)
    ctxp, *saved = attend_forward(tokens, positions, w3, off, segment_ids, pad_flags)
    own, dctx, first, gout = dense(ctxp, half, tokens, cotangent)
    blocks = [own] + [
        lax.ppermute(own, "tensor", [(t, t ^ flip) for t in range(4)]) for flip in (1, 2, 3)
    ]
    pieces = exchange(gout)
    gq, gkv = attend_backward(dctx, *saved)
    narrow, gin = tail(gq, gkv, tokens, positions, w3, first)
    token_grad, encoded, *outs = update(pieces, gin, narrow, blocks, masters, firsts, seconds)
    grads, news, lows, moms, varis = outs[:7], outs[7:14], outs[14:18], outs[18:25], outs[25:]
    return (
        encoded,
        token_grad,
        *returned(grads),
        *returned(news),
        *returned(lows),
        *returned(moms),
        *returned(varis),
    )


def body(
    tokens,
    positions,
    segment_ids,
    pad_flags,
    cotangent,
    inward,
    outward,
    upward,
    downward,
    vectors,
    offsets,
    shifts,
    first_inward,
    first_outward,
    first_upward,
    first_downward,
    first_vectors,
    first_offsets,
    first_shifts,
    second_inward,
    second_outward,
    second_upward,
    second_downward,
    second_vectors,
    second_offsets,
    second_shifts,
):
    w_inward, w_outward, w_upward, w_downward, vector_low, offset_low, shift_low = (
        lax.all_gather(inward.astype(jnp.bfloat16), "dp", axis=1, tiled=True),
        lax.all_gather(outward.astype(jnp.bfloat16), "dp", axis=1, tiled=True),
        lax.all_gather(upward.astype(jnp.bfloat16), "dp", axis=0, tiled=True),
        lax.all_gather(downward.astype(jnp.bfloat16), "dp", axis=1, tiled=True),
        lax.all_gather(vectors.astype(jnp.bfloat16), "dp", axis=1, tiled=True),
        lax.all_gather(offsets.astype(jnp.bfloat16), "dp", axis=1, tiled=True),
        lax.all_gather(shifts.astype(jnp.bfloat16), "dp", axis=0, tiled=True),
    )
    vector_wide = vector_low.astype(jnp.float32)
    offset_wide = offset_low.astype(jnp.float32)
    shift_wide = shift_low.astype(jnp.float32)
    input_wide = tokens.astype(jnp.float32)
    query_in = (input_wide + positions.astype(jnp.float32)).astype(jnp.bfloat16)
    w_lanes = jnp.pad(w_inward, ((0, 0), (0, 0), (0, 64)))
    off_lanes = jnp.pad(offset_wide, ((0, 6), (0, 64)))
    packed, *saved = attend_forward(
        tokens, positions, w_lanes, off_lanes, segment_ids, pad_flags
    )
    pairs = packed.reshape(16, 128, 2, 64)
    context_low = pairs.transpose(0, 2, 1, 3).reshape(PACK_ROWS, 64)
    first_sum = input_wide + summed(product(context_low, w_outward)) + vector_wide[4]
    normed, scaled_one, inverse_one = norm_forward(first_sum, vector_wide[0], vector_wide[1])
    normed_low = normed.astype(jnp.bfloat16)
    hidden = product(normed_low, w_upward) + shift_wide
    unit_value, unit_back = jax.vjp(smooth_unit, hidden)
    active = unit_value.astype(jnp.bfloat16)
    second_sum = normed + summed(product(active, w_downward)) + vector_wide[5]
    result, scaled_two, inverse_two = norm_forward(second_sum, vector_wide[2], vector_wide[3])
    encoded = result.astype(jnp.bfloat16)
    upstream = cotangent.astype(jnp.float32)
    second_grad, gain_two, shift_two = norm_backward(
        upstream, scaled_two, inverse_two, vector_wide[2]
    )
    down_low = second_grad.astype(jnp.bfloat16)
    grad_downward = product_left(active, down_low)
    hidden_low = unit_back(product_right(down_low, w_downward))[0].astype(jnp.bfloat16)
    grad_upward = product_left(normed_low, hidden_low)
    grad_shifts = jnp.sum(hidden_low.astype(jnp.float32), axis=0)
    normed_grad = second_grad + summed(product_right(hidden_low, w_upward))
    first_grad, gain_one, shift_one = norm_backward(
        normed_grad, scaled_one, inverse_one, vector_wide[0]
    )
    first_low = first_grad.astype(jnp.bfloat16)
    grad_outward = product_left(context_low, first_low)
    context_grad = product_right(first_low, w_outward).astype(jnp.bfloat16)
    halves = context_grad.reshape(16, 2, 128, 64)
    gq, gkv = attend_backward(
        halves.transpose(0, 2, 1, 3).reshape(2048, 128), *saved
    )
    query_grad, key_grad, value_grad = gq[:, :64], gkv[:, :64], gkv[:, 64:]
    grad_inward = jnp.stack(
        [
            product_left(query_in, query_grad),
            product_left(query_in, key_grad),
            product_left(tokens, value_grad),
        ]
    )
    grad_offsets = jnp.stack(
        [
            jnp.sum(query_grad.astype(jnp.float32), axis=0),
            jnp.sum(value_grad.astype(jnp.float32), axis=0),
        ]
    )
    input_part = (
        product_right(query_grad, w_inward[0])
        + product_right(key_grad, w_inward[1])
        + product_right(value_grad, w_inward[2])
    )
    input_grad = first_grad + summed(input_part)
    grad_vectors = jnp.stack(
        [
            gain_one,
            shift_one,
            gain_two,
            shift_two,
            jnp.sum(first_grad, axis=0),
            jnp.sum(second_grad, axis=0),
        ]
    )
    reduced = (
        lax.psum_scatter(grad_inward, "dp", scatter_dimension=1, tiled=True),
        lax.psum_scatter(grad_outward, "dp", scatter_dimension=1, tiled=True),
        lax.psum_scatter(grad_upward, "dp", scatter_dimension=0, tiled=True),
        lax.psum_scatter(grad_downward, "dp", scatter_dimension=1, tiled=True),
        lax.psum_scatter(grad_vectors, "dp", scatter_dimension=1, tiled=True),
        lax.psum_scatter(grad_offsets, "dp", scatter_dimension=1, tiled=True),
        lax.psum_scatter(grad_shifts, "dp", scatter_dimension=0, tiled=True),
    )
    masters = (inward, outward, upward, downward, vectors, offsets, shifts)
    firsts = (
        first_inward,
        first_outward,
        first_upward,
        first_downward,
        first_vectors,
        first_offsets,
        first_shifts,
    )
    seconds = (
        second_inward,
        second_outward,
        second_upward,
        second_downward,
        second_vectors,
        second_offsets,
        second_shifts,
    )
    updated = []
    momenta = []
    variances = []
    for master, gradient, old_first, old_second, step_rate in zip(
        masters, reduced, firsts, seconds, step_rates
    ):
        new_master, momentum, variance = adamw(master, gradient, old_first, old_second, step_rate)
        updated.append(new_master)
        momenta.append(momentum)
        variances.append(variance)
    return (
        encoded,
        input_grad,
        reduced[0],
        reduced[1],
        reduced[2],
        reduced[3],
        reduced[4],
        reduced[5],
        reduced[6],
        updated[0],
        updated[1],
        updated[2],
        updated[3],
        updated[4],
        updated[5],
        updated[6],
        updated[0].astype(jnp.bfloat16),
        updated[1].astype(jnp.bfloat16),
        updated[2].astype(jnp.bfloat16),
        updated[3].astype(jnp.bfloat16),
        momenta[0],
        momenta[1],
        momenta[2],
        momenta[3],
        momenta[4],
        momenta[5],
        momenta[6],
        variances[0],
        variances[1],
        variances[2],
        variances[3],
        variances[4],
        variances[5],
        variances[6],
    )


def solution(mesh):
    in_specs = (
        P("dp", None),
        P("dp", None),
        P("dp", None),
        P("dp", None),
        P("dp", None),
        P(None, "dp", "tensor"),
        P("tensor", "dp"),
        P("dp", "tensor"),
        P("tensor", "dp"),
        P(None, "dp"),
        P(None, ("tensor", "dp")),
        P(("tensor", "dp")),
        P(None, "dp", "tensor"),
        P("tensor", "dp"),
        P("dp", "tensor"),
        P("tensor", "dp"),
        P(None, "dp"),
        P(None, ("tensor", "dp")),
        P(("tensor", "dp")),
        P(None, "dp", "tensor"),
        P("tensor", "dp"),
        P("dp", "tensor"),
        P("tensor", "dp"),
        P(None, "dp"),
        P(None, ("tensor", "dp")),
        P(("tensor", "dp")),
    )
    out_specs = (
        P("dp", None),
        P("dp", None),
        P(None, "dp", "tensor"),
        P("tensor", "dp"),
        P("dp", "tensor"),
        P("tensor", "dp"),
        P(None, "dp"),
        P(None, ("tensor", "dp")),
        P(("tensor", "dp")),
        P(None, "dp", "tensor"),
        P("tensor", "dp"),
        P("dp", "tensor"),
        P("tensor", "dp"),
        P(None, "dp"),
        P(None, ("tensor", "dp")),
        P(("tensor", "dp")),
        P(None, "dp", "tensor"),
        P("tensor", "dp"),
        P("dp", "tensor"),
        P("tensor", "dp"),
        P(None, "dp", "tensor"),
        P("tensor", "dp"),
        P("dp", "tensor"),
        P("tensor", "dp"),
        P(None, "dp"),
        P(None, ("tensor", "dp")),
        P(("tensor", "dp")),
        P(None, "dp", "tensor"),
        P("tensor", "dp"),
        P("dp", "tensor"),
        P("tensor", "dp"),
        P(None, "dp"),
        P(None, ("tensor", "dp")),
        P(("tensor", "dp")),
    )
    pods = mesh.shape["dp"] == 8 and mesh.shape["tensor"] == 4
    chosen = body_pods if pods else body
    return jax.shard_map(chosen, mesh=mesh, in_specs=in_specs, out_specs=out_specs, check_vma=False)
```

```python
import functools
import jax
import jax.numpy as jnp
from jax import lax
from jax.experimental import pallas as pl
from jax.experimental.pallas import tpu as pltpu
from jax.sharding import PartitionSpec as P

HEAD_DIM = 32
MIB = 2**20
LIMIT_GATHER = 58 * MIB
LIMIT_FORWARD = 58 * MIB
LIMIT_DENSE = 58 * MIB
LIMIT_BACKWARD = 58 * MIB
LIMIT_TAIL = 58 * MIB
LIMIT_UPDATE = 58 * MIB
PACK_ROWS = 4096
IMAGES = 5
SPAN = PACK_ROWS + 512
BACK_QUERY = (512, 256)
BACK_KEY = (1024, 512, 256)
FORWARD_QUERY = (1024, 512, 256)
FORWARD_KEY = (1024, 512, 256)
LOG_SCALE = HEAD_DIM**-0.5 * 1.4426950408889634
FENCE = 2.0**100
LARGE = 2.0**100
SMALL = 2.0**-60
NN = (((1,), (0,)), ((), ()))
NT = (((1,), (1,)), ((), ()))
TN = (((0,), (0,)), ((), ()))
bf16 = jnp.bfloat16
f32 = jnp.float32


def mm(left, right, dims=NN):
    return lax.dot_general(left, right, dims, preferred_element_type=f32)


def iota(shape, dim):
    return lax.broadcasted_iota(jnp.int32, shape, dim)


def plan(length, sizes):
    out = []
    offset = 0
    least = sizes[-1]
    for size in sizes:
        left = jnp.maximum(length - offset, 0)
        count = (left + least - 1) // size
        out.append((size, offset, count))
        offset = offset + count * size
    return out


def twice(step):
    def both(i, carry):
        return step(2 * i + 1, step(2 * i, carry))

    return both


def pieces_of(value):
    one = value.astype(bf16).astype(f32)
    rest = value - one
    two = rest.astype(bf16).astype(f32)
    return one, two, rest - two


def attend_forward_kernel(
    tok_hbm, pos_hbm, w3, off, seg, pad,
    packed_hbm, ctx_hbm, qa_hbm, qw_hbm, ka_hbm, va_hbm, rank, bounds,
    tok, pos, raw, ctx_pair, qa, qw, ka, va, wqd, wkd, compact, dst, packed, load_sem, save_sem, close_sem,
):
    loads = []
    for part in range(4):
        rows = pl.ds(1024 * part, 1024)
        for which, (source, target) in enumerate(((tok_hbm, tok), (pos_hbm, pos))):
            copy = pltpu.make_async_copy(
                source.at[rows], target.at[rows], load_sem.at[2 * part + which]
            )
            copy.start()
            loads.append(copy)
    lane = iota((256, 128), 1)
    for which, spread in ((0, wqd), (1, wkd)):
        base = w3[which].astype(f32)
        left = pltpu.roll(base, 32, 1)
        right = pltpu.roll(base, 96, 1)
        spread[:, :128] = jnp.where(lane < 32, base, jnp.where(lane < 64, left, 0.0)).astype(bf16)
        spread[:, 128:] = jnp.where(lane < 32, right, jnp.where(lane < 64, base, 0.0)).astype(bf16)
    lane8 = iota((8, 128), 1)
    off_rows = off[...]
    off_left = pltpu.roll(off_rows, 32, 1)
    off_right = pltpu.roll(off_rows, 96, 1)
    q_bias = jnp.concatenate(
        [
            jnp.where(lane8 < 32, off_rows, jnp.where(lane8 < 64, off_left, 0.0))[0:1],
            jnp.where(lane8 < 32, off_right, jnp.where(lane8 < 64, off_rows, 0.0))[0:1],
        ],
        axis=1,
    )
    v_bias = jnp.where(lane8 < 64, off_rows, 0.0)[1:2]

    segment = seg[...]
    open_key = jnp.where(pad[...] == 0, 1.0, 0.0)
    grid_row = iota((32, 128), 0)
    before = (iota((128, 128), 0) < iota((128, 128), 1)).astype(bf16)
    in_row = mm(open_key.astype(bf16), before)
    row_total = jnp.broadcast_to(jnp.sum(open_key, axis=1, keepdims=True), (32, 128))
    above = (iota((32, 32), 1) < iota((32, 32), 0)).astype(bf16)
    place = (in_row + mm(above, row_total.astype(bf16))).astype(jnp.int32)
    place = jnp.where(open_key > 0.5, place, -1)
    for r in range(32):
        rank[r, :, :] = place[r : r + 1, :]
    for s in range(IMAGES + 1):
        if s == 0:
            bounds[0] = 0
            bounds[8] = 0
        else:
            low = (segment < s).astype(f32)
            bounds[s] = jnp.sum(low).astype(jnp.int32)
            bounds[8 + s] = jnp.sum(low * open_key).astype(jnp.int32)
    for i in range(16):
        dst[i] = jnp.sum(jnp.where(grid_row < 2 * i, open_key, 0.0)).astype(jnp.int32)
    for i in range(16):
        bounds[16 + i] = dst[i]
    total = bounds[8 + IMAGES]

    lane_row = iota((1, 128), 1)
    q_from = jnp.full((1, 128), SPAN, jnp.int32)
    q_to = jnp.full((1, 128), SPAN, jnp.int32)
    k_from = jnp.full((1, 128), SPAN, jnp.int32)
    k_to = jnp.full((1, 128), SPAN, jnp.int32)
    for s in range(IMAGES):
        at = lane_row == 64 + s
        q_from = jnp.where(at, bounds[s], q_from)
        q_to = jnp.where(at, bounds[s + 1], q_to)
        k_from = jnp.where(at, bounds[8 + s], k_from)
        k_to = jnp.where(at, bounds[9 + s], k_to)

    compact[pl.ds(0, 16), :] = jnp.zeros((16, 512), bf16)
    qa[:, pl.ds(PACK_ROWS, SPAN - PACK_ROWS), :] = jnp.zeros((2, SPAN - PACK_ROWS, 128), bf16)
    qw[pl.ds(PACK_ROWS, SPAN - PACK_ROWS), :] = jnp.zeros((SPAN - PACK_ROWS, 128), bf16)

    lane_q = iota((256, 128), 1)
    row_q = iota((256, 128), 0)

    def project(i, _):
        first = pl.multiple_of(i * 256, 256)
        rows = pl.ds(first, 256)
        token = tok[rows, :]
        query_in = (token.astype(f32) + pos[rows, :].astype(f32)).astype(bf16)
        both = (mm(query_in, wqd[...]) + q_bias).astype(bf16).astype(f32)
        here = row_q + first
        outside = (here < q_from) | (here >= q_to)
        feature = jnp.where(
            lane_q < 64 + IMAGES, jnp.where(outside, 1.0, 0.0), jnp.where(lane_q == 69, 1.0, 0.0)
        )
        for h in range(2):
            exact = both[:, 128 * h : 128 * h + 128] * LOG_SCALE
            high = exact.astype(bf16).astype(f32)
            qa[h, rows, :] = jnp.where(
                lane_q < 32, high, jnp.where(lane_q < 64, exact - high, feature)
            ).astype(bf16)
        qw[rows, :] = jnp.where(
            lane_q < 32, both[:, :128], jnp.where(lane_q < 64, both[:, 128:], 0.0)
        ).astype(bf16)
        start = dst[i]
        aligned = pl.multiple_of((start // 16) * 16, 16)
        places = jnp.concatenate([rank[2 * i], rank[2 * i + 1]], axis=1)
        hot = jnp.where(iota((272, 256), 0) + aligned == places, 1.0, 0.0).astype(bf16)
        moved = mm(hot, jnp.concatenate([query_in, token], axis=1)).astype(bf16)
        head = pl.ds(aligned, 16)
        compact[head, :] = compact[head, :] + moved[:16]
        compact[pl.ds(pl.multiple_of(aligned + 16, 16), 256), :] = moved[16:]
        return 0

    for part in range(4):
        loads[2 * part].wait()
        loads[2 * part + 1].wait()
        lax.fori_loop(2 * part, 2 * part + 2, twice(project), 0)

    lane_k = iota((512, 128), 1)
    row_k = iota((512, 128), 0)

    def project_keys(i, _):
        first = pl.multiple_of(i * 512, 512)
        rows = pl.ds(first, 512)
        here = row_k + first
        real = here < total
        both = mm(compact[rows, 0:256], wkd[...])
        value = mm(compact[rows, 256:512], w3[2]) + v_bias
        value = jnp.where(real, value, 0.0)
        inside = (here >= k_from) & (here < k_to)
        feature = jnp.where(inside, -FENCE, 0.0)
        feature = jnp.where(lane_k == 69, jnp.where(real, 0.0, -FENCE), feature)
        for h in range(2):
            spot = (lane_k >= 70 + 3 * h) & (lane_k < 73 + 3 * h)
            key = jnp.where(real, both[:, 128 * h : 128 * h + 128], 0.0)
            ka[h, rows, :] = jnp.where(
                lane_k < 64, key, jnp.where(spot, 1.0, feature)
            ).astype(bf16)
        va[0, rows, :] = jnp.where(
            lane_k < 32, value, jnp.where(lane_k < 35, 1.0, 0.0)
        ).astype(bf16)
        va[1, rows, :] = jnp.where(
            lane_k < 3, 1.0, jnp.where((lane_k >= 32) & (lane_k < 64), value, 0.0)
        ).astype(bf16)
        return 0

    lax.fori_loop(0, (total + 767) // 512, project_keys, 0)
    extra = pl.ds(PACK_ROWS, SPAN - PACK_ROWS)
    saves = [
        pltpu.make_async_copy(source, target, save_sem.at[n])
        for n, (source, target) in enumerate(
            ((qw, qw_hbm), (ka, ka_hbm), (va, va_hbm), (qa.at[:, extra], qa_hbm.at[:, extra]))
        )
    ]
    for copy in saves:
        copy.start()

    def per_segment(safe, s, _):
        q_start, q_end = bounds[s], bounds[s + 1]
        k_start, k_end = bounds[8 + s], bounds[9 + s]
        q_first = (q_start // 16) * 16
        k_first = (k_start // 16) * 16

        def per_query(size, base, i, _):
            q_row = pl.multiple_of(base + i * size, 16)
            q_rows = pl.ds(q_row, size)
            head = pl.ds(q_row, 16)
            kept = iota((16, 128), 0) + q_row < q_start
            olds = [raw[h, head, :] for h in range(2)]
            for h in range(2):
                raw[h, q_rows, :] = jnp.zeros((size, 128), f32)

            def per_key(tops, span, first_key, j, _):
                k_rows = pl.ds(pl.multiple_of(first_key + j * span, 16), span)
                for h in range(2):
                    score = mm(qa[h, q_rows, :], ka[h, k_rows, :], NT)
                    if tops is not None:
                        score = score - tops[h]
                    weight = jnp.exp2(score).astype(bf16)
                    raw[h, q_rows, :] += mm(weight, va[h, k_rows, :])
                return 0

            def peak(j, tops):
                k_rows = pl.ds(pl.multiple_of(k_first + j * 256, 16), 256)
                out = []
                for h in range(2):
                    score = mm(qa[h, q_rows, :], ka[h, k_rows, :], NT)
                    out.append(jnp.maximum(tops[h], jnp.max(score, axis=1, keepdims=True)))
                return tuple(out)

            if safe:
                steps = (k_end - k_first + 255) // 256
                low = jnp.full((size, 1), -3.0e38, f32)
                tops = lax.fori_loop(0, steps, peak, (low, low))
                lane = iota((size, 128), 1)
                raw[0, q_rows, :] = jnp.where(
                    lane == 64, tops[0], jnp.where(lane == 65, tops[1], 0.0)
                )
                lax.fori_loop(0, steps, functools.partial(per_key, tops, 256, k_first), 0)
            else:
                for span, offset, count in plan(k_end - k_first, FORWARD_KEY):
                    lax.fori_loop(
                        0, count, functools.partial(per_key, None, span, k_first + offset), 0
                    )
            for h in range(2):
                raw[h, head, :] = jnp.where(kept, olds[h], raw[h, head, :])
            return 0

        for size, offset, count in plan(q_end - q_first, FORWARD_QUERY):
            lax.fori_loop(0, count, functools.partial(per_query, size, q_first + offset), 0)
        return 0

    lax.fori_loop(0, IMAGES, functools.partial(per_segment, False), 0)

    def extremes(i, carry):
        rows = pl.ds(pl.multiple_of(i * 512, 512), 512)
        lane = iota((512, 128), 1)
        both = jnp.where(lane == 32, raw[0, rows, :], jnp.where(lane == 0, raw[1, rows, :], 1.0))
        return (
            jnp.maximum(carry[0], jnp.max(both, axis=0, keepdims=True)),
            jnp.minimum(carry[1], jnp.min(both, axis=0, keepdims=True)),
        )

    one_row = jnp.ones((1, 128), f32)
    most, least = lax.fori_loop(0, 8, extremes, (one_row, one_row))
    fine = (jnp.max(most) < LARGE) & (jnp.min(least) > SMALL)

    @pl.when(jnp.logical_not(fine))
    def _():
        lax.fori_loop(0, IMAGES, functools.partial(per_segment, True), 0)

    def close(b, _):
        rows = pl.ds(pl.multiple_of(b * 256, 256), 256)
        pair_rows = pl.ds(pl.multiple_of(b * 128, 128), 128)
        lane = iota((256, 128), 1)
        zero, one = raw[0, rows, :], raw[1, rows, :]
        l_zero = jnp.broadcast_to(zero[:, 32:33], (256, 128))
        l_one = jnp.broadcast_to(one[:, 0:1], (256, 128))
        lower = lane < 32
        joined = jnp.where(lower, zero, one) / jnp.where(lower, l_zero, l_one)
        early = lane < 73
        shift = jnp.where(
            early,
            jnp.broadcast_to(zero[:, 64:65], (256, 128)),
            jnp.broadcast_to(zero[:, 65:66], (256, 128)),
        )
        parts = pieces_of(-(shift + jnp.log2(jnp.where(early, l_zero, l_one))))
        for h in range(2):
            at = 70 + 3 * h
            value = qa[h, rows, :].astype(f32)
            for n in range(3):
                value = jnp.where(lane == at + n, parts[n], value)
            qa[h, rows, :] = value.astype(bf16)
        pair = jnp.where(
            iota((128, 128), 1) < 64, joined[0:128], pltpu.roll(joined[128:256], 64, 1)
        )
        ctx_pair[pair_rows, :] = pair
        packed[pair_rows, :] = pair.astype(bf16)
        return 0

    def stores(i):
        rows = pl.ds(pl.multiple_of(i * 512, 512), 512)
        pairs = pl.ds(pl.multiple_of(i * 256, 256), 256)
        return (
            pltpu.make_async_copy(qa.at[:, rows], qa_hbm.at[:, rows], close_sem.at[0, i]),
            pltpu.make_async_copy(ctx_pair.at[pairs], ctx_hbm.at[pairs], close_sem.at[1, i]),
            pltpu.make_async_copy(packed.at[pairs], packed_hbm.at[pairs], close_sem.at[2, i]),
        )

    def close_two(i, _):
        twice(close)(i, 0)
        for copy in stores(i):
            copy.start()
        return 0

    def settle(i, _):
        for copy in stores(i):
            copy.wait()
        return 0

    lax.fori_loop(0, 8, close_two, 0)
    for copy in saves:
        copy.wait()
    lax.fori_loop(0, 8, settle, 0)


VMEM_SPEC = pl.BlockSpec(memory_space=pltpu.VMEM)
SMEM_SPEC = pl.BlockSpec(memory_space=pltpu.SMEM)
ANY_SPEC = pl.BlockSpec(memory_space=pl.ANY)


def attend_forward(tokens, positions, w3, off, segment, padding):
    return pl.pallas_call(
        attend_forward_kernel,
        out_shape=(
            jax.ShapeDtypeStruct((2048, 128), bf16),
            jax.ShapeDtypeStruct((2048, 128), f32),
            jax.ShapeDtypeStruct((2, SPAN, 128), bf16),
            jax.ShapeDtypeStruct((SPAN, 128), bf16),
            jax.ShapeDtypeStruct((2, SPAN, 128), bf16),
            jax.ShapeDtypeStruct((2, SPAN, 128), bf16),
            jax.ShapeDtypeStruct((32, 1, 128), jnp.int32),
            jax.ShapeDtypeStruct((32,), jnp.int32),
        ),
        in_specs=[ANY_SPEC] * 2 + [VMEM_SPEC] * 4,
        out_specs=[ANY_SPEC] * 6 + [VMEM_SPEC, SMEM_SPEC],
        scratch_shapes=[
            pltpu.VMEM((PACK_ROWS, 256), bf16),
            pltpu.VMEM((PACK_ROWS, 256), bf16),
            pltpu.VMEM((2, SPAN, 128), f32),
            pltpu.VMEM((2048, 128), f32),
            pltpu.VMEM((2, SPAN, 128), bf16),
            pltpu.VMEM((SPAN, 128), bf16),
            pltpu.VMEM((2, SPAN, 128), bf16),
            pltpu.VMEM((2, SPAN, 128), bf16),
            pltpu.VMEM((256, 256), bf16),
            pltpu.VMEM((256, 256), bf16),
            pltpu.VMEM((SPAN, 512), bf16),
            pltpu.SMEM((16,), jnp.int32),
            pltpu.VMEM((2048, 128), bf16),
            pltpu.SemaphoreType.DMA((8,)),
            pltpu.SemaphoreType.DMA((4,)),
            pltpu.SemaphoreType.DMA((3, 8)),
        ],
        compiler_params=pltpu.CompilerParams(vmem_limit_bytes=LIMIT_FORWARD),
        cost_estimate=pl.CostEstimate(
            flops=20 * 10**9, bytes_accessed=20 * 10**6, transcendentals=10**7
        ),
    )(tokens, positions, w3, off, segment.reshape(32, 128), padding.reshape(32, 128))


def attend_backward_kernel(
    packed, ctx_hbm, qa_hbm, qw_hbm, ka_hbm, va_hbm, rank, bounds,
    gq_hbm, gkv_hbm,
    ctx, qa, qw, ka, va, do, kw, dq, dkv, turned_sum, gq, gkv, load_sem, store_sem,
):
    loads = [
        pltpu.make_async_copy(source, target, load_sem.at[n])
        for n, (source, target) in enumerate(
            ((ctx_hbm, ctx), (qa_hbm, qa), (ka_hbm, ka), (va_hbm, va), (qw_hbm, qw))
        )
    ]
    for copy in loads:
        copy.start()
    for i in range(SPAN // 512):
        rows = pl.ds(512 * i, 512)
        dq[rows, :] = jnp.zeros((512, 128), f32)
        dkv[rows, :] = jnp.zeros((512, 128), f32)
    do[:, pl.ds(PACK_ROWS, SPAN - PACK_ROWS), :] = jnp.zeros((2, SPAN - PACK_ROWS, 128), bf16)
    loads[0].wait()
    lane = iota((128, 128), 1)
    for b in range(16):
        pair = packed[pl.ds(128 * b, 128), :].astype(f32)
        product = pair * ctx[pl.ds(128 * b, 128), :]
        for half in range(2):
            rows = pl.ds(256 * b + 128 * half, 128)
            grad = pair if half == 0 else pltpu.roll(pair, 64, 1)
            at = 64 * half
            tails = []
            for h in range(2):
                inside = (lane >= at + 32 * h) & (lane < at + 32 * h + 32)
                delta = jnp.sum(jnp.where(inside, product, 0.0), axis=1, keepdims=True)
                one, two, three = pieces_of(-jnp.broadcast_to(delta, (128, 128)))
                spot = 32 - 32 * h
                tails.append(jnp.where(lane == spot, one, jnp.where(lane == spot + 1, two, three)))
            do[0, rows, :] = jnp.where(
                lane < 32, grad, jnp.where(lane < 35, tails[0], 0.0)
            ).astype(bf16)
            do[1, rows, :] = jnp.where(
                lane < 3, tails[1], jnp.where((lane >= 32) & (lane < 64), grad, 0.0)
            ).astype(bf16)
    for copy in loads[1:]:
        copy.wait()

    def per_segment(s, _):
        q_start, q_end = bounds[s], bounds[s + 1]
        k_start, k_end = bounds[8 + s], bounds[9 + s]
        q_first = (q_start // 16) * 16
        k_first = (k_start // 16) * 16
        q_plan = plan(q_end - q_first, BACK_QUERY)

        def per_key(span, first_key, j, _):
            k_row = pl.multiple_of(first_key + j * span, 16)
            k_rows = pl.ds(k_row, span)
            lane = iota((span, 128), 1)
            at = iota((span, 128), 0) + k_row
            mine = (at >= k_start) & (at < k_end)
            here = pl.ds(0, span)
            for h in range(2):
                mask = mine & (lane >= 32 * h) & (lane < 32 * h + 32)
                kw[h, here, :] = jnp.where(mask, ka[h, k_rows, :].astype(f32), 0.0).astype(bf16)

            turned_sum[:, here] = jnp.zeros((128, span), f32)

            def per_query(size, first_row, i, _):
                q_rows = pl.ds(pl.multiple_of(first_row + i * size, 16), size)
                for h in range(2):
                    score = mm(qa[h, q_rows, :], ka[h, k_rows, :], NT)
                    prob = jnp.exp2(score)
                    prob_grad = mm(do[h, q_rows, :], va[h, k_rows, :], NT)
                    score_grad = (prob * prob_grad).astype(bf16)
                    dq[q_rows, :] += mm(score_grad, kw[h, here, :])
                    cols = slice(32 * h, 32 * h + 32)
                    turned_sum[32 * h : 32 * h + 32, here] += mm(qw[q_rows, cols], score_grad, TN)
                    turned_sum[64 + 32 * h : 96 + 32 * h, here] += mm(
                        do[h, q_rows, cols], prob.astype(bf16), TN
                    )
                return 0

            for size, offset, count in q_plan:
                lax.fori_loop(0, count, functools.partial(per_query, size, q_first + offset), 0)
            fresh = turned_sum[:, here].T
            dkv[k_rows, :] = dkv[k_rows, :] + jnp.where(mine, fresh, 0.0)
            return 0

        for span, offset, count in plan(k_end - k_first, BACK_KEY):
            lax.fori_loop(0, count, functools.partial(per_key, span, k_first + offset), 0)
        return 0

    lax.fori_loop(0, IMAGES, per_segment, 0)

    def emit(i, _):
        rows = pl.ds(pl.multiple_of(i * 256, 256), 256)
        gq[rows, :] = (dq[rows, :] * HEAD_DIM**-0.5).astype(bf16)
        start = bounds[16 + i]
        aligned = pl.multiple_of((start // 16) * 16, 16)
        places = jnp.concatenate([rank[2 * i], rank[2 * i + 1]], axis=1)
        hot = jnp.where(iota((272, 256), 0) + aligned == places, 1.0, 0.0).astype(bf16)
        piece = dkv[pl.ds(aligned, 272), :]
        scale = jnp.where(iota((272, 128), 1) < 64, HEAD_DIM**-0.5, 1.0)
        gkv[rows, :] = mm(hot, (piece * scale).astype(bf16), TN).astype(bf16)
        return 0

    def stores(i):
        rows = pl.ds(pl.multiple_of(i * 512, 512), 512)
        return (
            pltpu.make_async_copy(gq.at[rows], gq_hbm.at[rows], store_sem.at[0, i]),
            pltpu.make_async_copy(gkv.at[rows], gkv_hbm.at[rows], store_sem.at[1, i]),
        )

    def emit_two(i, _):
        twice(emit)(i, 0)
        for copy in stores(i):
            copy.start()
        return 0

    def settle(i, _):
        for copy in stores(i):
            copy.wait()
        return 0

    lax.fori_loop(0, 8, emit_two, 0)
    lax.fori_loop(0, 8, settle, 0)


def attend_backward(packed, ctx, qa, qw, ka, va, rank, bounds):
    return pl.pallas_call(
        attend_backward_kernel,
        out_shape=(
            jax.ShapeDtypeStruct((PACK_ROWS, 128), bf16),
            jax.ShapeDtypeStruct((PACK_ROWS, 128), bf16),
        ),
        in_specs=[VMEM_SPEC] + [ANY_SPEC] * 5 + [VMEM_SPEC, SMEM_SPEC],
        out_specs=[ANY_SPEC] * 2,
        scratch_shapes=[
            pltpu.VMEM((2048, 128), f32),
            pltpu.VMEM((2, SPAN, 128), bf16),
            pltpu.VMEM((SPAN, 128), bf16),
            pltpu.VMEM((2, SPAN, 128), bf16),
            pltpu.VMEM((2, SPAN, 128), bf16),
            pltpu.VMEM((2, SPAN, 128), bf16),
            pltpu.VMEM((2, BACK_KEY[0], 128), bf16),
            pltpu.VMEM((SPAN, 128), f32),
            pltpu.VMEM((SPAN, 128), f32),
            pltpu.VMEM((128, BACK_KEY[0]), f32),
            pltpu.VMEM((PACK_ROWS, 128), bf16),
            pltpu.VMEM((PACK_ROWS, 128), bf16),
            pltpu.SemaphoreType.DMA((5,)),
            pltpu.SemaphoreType.DMA((2, 8)),
        ],
        compiler_params=pltpu.CompilerParams(vmem_limit_bytes=LIMIT_BACKWARD),
        cost_estimate=pl.CostEstimate(
            flops=50 * 10**9, bytes_accessed=20 * 10**6, transcendentals=10**7
        ),
    )(packed, ctx, qa, qw, ka, va, rank, bounds)


STEP = 10


neg_fill = -1e30
norm_eps = 1e-05
beta_one = 0.5
beta_two = 0.5
adam_eps = 1e-08
decay_rate = 0.0001
step_rates = (0.06, 0.15, 0.06, 0.03, 0.1, 0.1, 0.1)


def product(left_side, right_side):
    return jnp.dot(left_side, right_side, preferred_element_type=jnp.float32)


def product_left(left_side, right_side):
    return lax.dot_general(
        left_side, right_side, (((0,), (0,)), ((), ())), preferred_element_type=jnp.float32
    )


def product_right(left_side, right_side):
    return lax.dot_general(
        left_side, right_side, (((1,), (1,)), ((), ())), preferred_element_type=jnp.float32
    )


def smooth_unit(values):
    return jax.nn.gelu(values, approximate=False)


def norm_forward(values, gain_row, shift_row):
    center = values - jnp.mean(values, axis=-1, keepdims=True)
    inverse = lax.rsqrt(jnp.mean(center * center, axis=-1, keepdims=True) + norm_eps)
    scaled = center * inverse
    return (scaled * gain_row + shift_row, scaled, inverse)


def norm_backward(upstream, scaled, inverse, gain_row):
    spread = upstream * gain_row
    centred = (
        spread
        - jnp.mean(spread, axis=-1, keepdims=True)
        - scaled * jnp.mean(spread * scaled, axis=-1, keepdims=True)
    )
    return (inverse * centred, jnp.sum(upstream * scaled, axis=0), jnp.sum(upstream, axis=0))


def summed(partial_value):
    return lax.psum(partial_value, "tensor")


def adamw(master, gradient, old_first, old_second, step_rate):
    momentum = beta_one * old_first + (1.0 - beta_one) * gradient
    variance = beta_two * old_second + (1.0 - beta_two) * gradient * gradient
    normal_step = (
        momentum / (1.0 - beta_one**STEP) / (jnp.sqrt(variance / (1.0 - beta_two**STEP)) + adam_eps)
    )
    return (master - step_rate * (normal_step + decay_rate * master), momentum, variance)


MESH = pl.DeviceIdType.MESH
SHARD_ROWS = 304
GROUPS = 16
CHUNK = 256
CHUNKS = 4
STEPS = 2
BLOCK = 1024 // STEPS
PAIRS = BLOCK // 2
OWN_ROWS = CHUNK * CHUNKS


def greet(peers):
    barrier = pltpu.get_barrier_semaphore()
    for peer in peers:
        pl.semaphore_signal(barrier, inc=1, device_id=peer, device_id_type=MESH)
    return lambda: pl.semaphore_wait(barrier, len(peers))


def remote(source, target, send_sem, recv_sem, peer):
    return pltpu.make_async_remote_copy(
        src_ref=source,
        dst_ref=target,
        send_sem=send_sem,
        recv_sem=recv_sem,
        device_id=peer,
        device_id_type=MESH,
    )


def gather_kernel(
    up_hbm, down_hbm, outer, vec, shift, inward, off,
    pack, w3, offs,
    up, down, local_sem, small, one, send_buf, recv_buf, send_sem, recv_sem,
):
    me = lax.axis_index("dp")
    peers = [lax.rem(me + k, 8) for k in range(1, 8)]
    ready = greet([{"dp": p} for p in peers])
    loads = [
        pltpu.make_async_copy(up_hbm, up, local_sem.at[16]),
        pltpu.make_async_copy(down_hbm, down, local_sem.at[17]),
    ]
    for copy in loads:
        copy.start()
    send_buf[...] = jnp.zeros((112, 128), bf16)
    for which in range(3):
        send_buf[32 * which : 32 * which + 32, 0:64] = inward[which].astype(bf16)
    small[...] = jnp.zeros((3, 16, 128), f32)
    small[0, 0:2, 0:8] = off[...]
    small[1, 0:6, 0:32] = vec[...]
    small[2, 6:7, 0:64] = shift[...]
    send_buf[96:112, :] = pltpu.roll(small[0], me * 8, 1).astype(bf16)
    recv_buf[me] = send_buf[...]
    ready()
    copies = []
    for k, peer in enumerate(peers):
        copy = remote(
            send_buf, recv_buf.at[me], send_sem.at[k], recv_sem.at[me], {"dp": peer}
        )
        copy.start()
        copies.append(copy)
    for copy in loads:
        copy.wait()
    for b in range(4):
        one[32 * b : 32 * b + 32, :] = up[:, 128 * b : 128 * b + 128].astype(bf16)
        one[128 + 32 * b : 160 + 32 * b, :] = down[:, 128 * b : 128 * b + 128].astype(bf16)
    one[256:304, :] = jnp.zeros((48, 128), bf16)
    one[256:288, 0:64] = outer[...].astype(bf16)
    placed = pltpu.roll(small[1], lax.rem(me, 4) * 32, 1)
    placed = placed + pltpu.roll(small[2], lax.rem(me, 2) * 64, 1)
    one[288:304, :] = placed.astype(bf16)
    spreads = [
        pltpu.make_async_copy(one, pack.at[j], local_sem.at[j]) for j in range(GROUPS)
    ]
    for copy in spreads:
        copy.start()
    for peer in peers:
        remote(
            send_buf, recv_buf.at[peer], send_sem.at[0], recv_sem.at[peer], {"dp": peer}
        ).wait_recv()
    total = jnp.zeros((16, 128), f32)
    for d in range(8):
        for which in range(3):
            w3[which, 32 * d : 32 * d + 32, :] = recv_buf[d, 32 * which : 32 * which + 32, :]
        total = total + recv_buf[d, 96:112, :].astype(f32)
    offs[...] = total[0:8]
    for copy in copies:
        copy.wait_send()
    for copy in spreads:
        copy.wait()


def gather_weights(upward, down_t, out_t, vectors, shifts, inward, offsets):
    return pl.pallas_call(
        gather_kernel,
        out_shape=(
            jax.ShapeDtypeStruct((GROUPS, SHARD_ROWS, 128), bf16),
            jax.ShapeDtypeStruct((3, 256, 128), bf16),
            jax.ShapeDtypeStruct((8, 128), f32),
        ),
        in_specs=[ANY_SPEC] * 2 + [VMEM_SPEC] * 5,
        out_specs=[ANY_SPEC] + [VMEM_SPEC] * 2,
        scratch_shapes=[
            pltpu.VMEM((32, 512), f32),
            pltpu.VMEM((32, 512), f32),
            pltpu.SemaphoreType.DMA((18,)),
            pltpu.VMEM((3, 16, 128), f32),
            pltpu.VMEM((SHARD_ROWS, 128), bf16),
            pltpu.VMEM((112, 128), bf16),
            pltpu.VMEM((8, 112, 128), bf16),
            pltpu.SemaphoreType.DMA((7,)),
            pltpu.SemaphoreType.DMA((8,)),
        ],
        compiler_params=pltpu.CompilerParams(
            collective_id=0, has_side_effects=True, vmem_limit_bytes=LIMIT_GATHER
        ),
    )(upward, down_t, out_t, vectors, shifts, inward, offsets)


def norm_rows(values):
    center = values - jnp.mean(values, axis=1, keepdims=True)
    inverse = lax.rsqrt(jnp.mean(center * center, axis=1, keepdims=True) + norm_eps)
    return center * inverse, inverse


def norm_rows_back(spread, scaled, inverse):
    return inverse * (
        spread
        - jnp.mean(spread, axis=1, keepdims=True)
        - scaled * jnp.mean(spread * scaled, axis=1, keepdims=True)
    )


def dense_kernel(
    ctxp_hbm, half_hbm, tok_hbm, cot_hbm,
    encoded, dctx, first_hbm, gout,
    ctxp, half, first, enc, stage, other, ctxs, up, down, out_a, out_b, vec, shift,
    tok, cot, grads_ctx, normed_low, second_low, first_a, first_b,
    active, hgrad, slope, sums, give, take, keep,
    w_sem, load_sem, ctx_send, ctx_recv, dctx_send, dctx_recv,
    local_sem, enc_sem, first_sem, g_sem,
):
    me = lax.axis_index("tensor")
    core = lax.rem(me, 2)
    sibling = me + 1 - 2 * core
    across = lax.rem(me + 2, 4)
    diagonal = lax.rem(sibling + 2, 4)
    order = (sibling, across, diagonal)
    ready = greet([{"tensor": p} for p in order])
    own = pl.multiple_of(me * OWN_ROWS, OWN_ROWS)
    load_tok = pltpu.make_async_copy(tok_hbm.at[pl.ds(own, OWN_ROWS)], tok, load_sem.at[0])
    load_cot = pltpu.make_async_copy(cot_hbm.at[pl.ds(own, OWN_ROWS)], cot, load_sem.at[1])
    load_half = pltpu.make_async_copy(half_hbm, half, load_sem.at[2])
    load_ctxp = pltpu.make_async_copy(ctxp_hbm, ctxp, load_sem.at[3])
    load_half.start()
    load_ctxp.start()
    load_tok.start()
    load_cot.start()
    load_ctxp.wait()
    ctxs[me] = ctxp[pl.ds(pl.multiple_of(me * 512, 512), 512), :]
    sums[...] = jnp.zeros((8, 256), f32)
    ready()
    weights = [
        remote(
            half.at[:, pl.ds(256, 48)], other.at[:, pl.ds(256, 48)],
            w_sem.at[0], w_sem.at[1], {"tensor": sibling},
        ),
        remote(
            half.at[:, pl.ds(0, 256)], other.at[:, pl.ds(0, 256)],
            w_sem.at[2], w_sem.at[3], {"tensor": sibling},
        ),
    ]
    load_half.wait()
    weights[0].start()

    def ctx_copy(peer, c):
        rows = pl.ds(pl.multiple_of(peer * 512 + c * PAIRS, PAIRS), PAIRS)
        return remote(
            ctxp.at[rows], ctxs.at[me, pl.ds(pl.multiple_of(c * PAIRS, PAIRS), PAIRS)],
            ctx_send.at[peer, c], ctx_recv.at[me, c], {"tensor": peer},
        )

    def ctx_arrival(peer, c):
        rows = pl.ds(pl.multiple_of(c * PAIRS, PAIRS), PAIRS)
        return remote(
            ctxp.at[rows], ctxs.at[peer, rows],
            ctx_send.at[peer, c], ctx_recv.at[peer, c], {"tensor": peer},
        )

    for peer in (across, diagonal, sibling):
        ctx_copy(peer, 0).start()
    weights[1].start()
    for c in range(1, STEPS):
        for peer in (across, diagonal, sibling):
            ctx_copy(peer, c).start()

    out_a[...] = jnp.zeros((256, 512), bf16)
    out_b[...] = jnp.zeros((256, 512), bf16)

    def unpack_small(source, t_of):
        for ty in range(2):
            t = t_of(ty)
            lanes = pl.ds(pl.multiple_of(t * 128, 128), 128)
            for d in range(8):
                piece = source[8 * ty + d, 256:288, :].astype(f32)
                out_a[32 * d : 32 * d + 32, lanes] = piece.astype(bf16)
                out_b[32 * d : 32 * d + 32, lanes] = pltpu.roll(piece, 64, 1).astype(bf16)
            for b in range(4):
                both = source[8 * ty + 2 * b, 288:304, :] + source[8 * ty + 2 * b + 1, 288:304, :]
                shift[:, pl.ds(pl.multiple_of(t * 512 + 128 * b, 128), 128)] = (
                    both.astype(f32)[6:7]
                )

    def unpack_large(source, t_of):
        for ty in range(2):
            t = t_of(ty)

            def one_row(d, _):
                rows = pl.ds(pl.multiple_of(d * 32, 32), 32)
                for b in range(4):
                    lanes = pl.ds(pl.multiple_of(t * 512 + 128 * b, 128), 128)
                    up[rows, lanes] = source[8 * ty + d, 32 * b : 32 * b + 32, :]
                    down[rows, lanes] = source[8 * ty + d, 128 + 32 * b : 160 + 32 * b, :]
                return 0

            lax.fori_loop(0, 8, one_row, 0)

    mine_t = lambda ty: 2 * ty + core
    other_t = lambda ty: 2 * ty + 1 - core
    for b in range(2):
        total = jnp.zeros((16, 128), f32)
        for d in range(4 * b, 4 * b + 4):
            total = total + half[d, 288:304, :].astype(f32)
        vec[:, 128 * b : 128 * b + 128] = total[0:8]
    unpack_small(half, mine_t)
    unpack_large(half, mine_t)
    weights[0].wait_recv()
    unpack_small(other, other_t)
    weights[1].wait_recv()
    unpack_large(other, other_t)
    load_tok.wait()
    load_cot.wait()

    def enc_store(c):
        rows = pl.ds(pl.multiple_of(c * BLOCK, BLOCK), BLOCK)
        return pltpu.make_async_copy(enc.at[rows], encoded.at[rows], enc_sem.at[c])

    def first_store(c):
        rows = pl.ds(pl.multiple_of(c * BLOCK, BLOCK), BLOCK)
        return pltpu.make_async_copy(first.at[rows], first_hbm.at[rows], first_sem.at[c])

    def dctx_copy(peer, c):
        rows = pl.ds(pl.multiple_of(c * PAIRS, PAIRS), PAIRS)
        return remote(
            grads_ctx.at[peer, rows],
            dctx.at[pl.ds(pl.multiple_of(me * 512 + c * PAIRS, PAIRS), PAIRS)],
            dctx_send.at[peer, c], dctx_recv.at[me, c], {"tensor": peer},
        )

    def dctx_arrival(peer, c):
        rows = pl.ds(pl.multiple_of(c * PAIRS, PAIRS), PAIRS)
        return remote(
            grads_ctx.at[peer, rows],
            dctx.at[pl.ds(pl.multiple_of(peer * 512 + c * PAIRS, PAIRS), PAIRS)],
            dctx_send.at[peer, c], dctx_recv.at[peer, c], {"tensor": peer},
        )

    def dctx_local(c):
        rows = pl.ds(pl.multiple_of(c * PAIRS, PAIRS), PAIRS)
        return pltpu.make_async_copy(
            grads_ctx.at[me, rows],
            dctx.at[pl.ds(pl.multiple_of(me * 512 + c * PAIRS, PAIRS), PAIRS)],
            local_sem.at[c],
        )

    def chunk_step(c, _):
        for peer in order:
            ctx_arrival(peer, c).wait_recv()
        rows = pl.ds(pl.multiple_of(c * BLOCK, BLOCK), BLOCK)
        pair_rows = pl.ds(pl.multiple_of(c * PAIRS, PAIRS), PAIRS)
        context = jnp.concatenate([ctxs[t, pair_rows, :] for t in range(4)], axis=1)
        upper, lower = mm(context, out_a[...], NT), mm(context, out_b[...], NT)
        attended = jnp.concatenate(
            [half_of[g : g + 128] for g in range(0, PAIRS, 128) for half_of in (upper, lower)],
            axis=0,
        )
        first_sum = tok[rows, :].astype(f32) + attended + vec[4:5]
        scaled_one, inverse_one = norm_rows(first_sum)
        normed = scaled_one * vec[0:1] + vec[1:2]
        low = normed.astype(bf16)
        normed_low[rows, :] = low
        for n in range(4):
            span = slice(512 * n, 512 * n + 512)
            hidden = mm(low, up[:, span]) + shift[:, span]
            cumulative = 0.5 * (1.0 + lax.erf(hidden * 0.7071067811865476))
            active[rows, span] = (hidden * cumulative).astype(bf16)
            slope[:, span] = cumulative + hidden * (
                0.3989422804014327 * jnp.exp(-0.5 * hidden * hidden)
            )
        second_sum = normed + mm(active[rows, :], down[...], NT) + vec[5:6]
        scaled_two, inverse_two = norm_rows(second_sum)
        enc[rows, :] = (scaled_two * vec[2:3] + vec[3:4]).astype(bf16)
        enc_store(c).start()
        upstream = cot[rows, :].astype(f32)
        second_grad = norm_rows_back(upstream * vec[2:3], scaled_two, inverse_two)
        low_two = second_grad.astype(bf16)
        second_low[rows, :] = low_two
        for n in range(4):
            span = slice(512 * n, 512 * n + 512)
            hgrad[rows, span] = (mm(low_two, down[:, span]) * slope[:, span]).astype(bf16)
        normed_grad = second_grad + mm(hgrad[rows, :], up[...], NT)
        first_grad = norm_rows_back(normed_grad * vec[0:1], scaled_one, inverse_one)
        first[rows, :] = first_grad
        first_store(c).start()
        low_one = first_grad.astype(bf16)
        parts = [
            jnp.concatenate([low_one[g + at : g + at + 128] for g in range(0, BLOCK, 256)], axis=0)
            for at in (0, 128)
        ]
        first_a[pair_rows, :] = parts[0]
        first_b[pair_rows, :] = parts[1]
        back = (mm(parts[0], out_a[...]) + mm(parts[1], out_b[...])).astype(bf16)
        for t in range(4):
            grads_ctx[t, pair_rows, :] = back[:, 128 * t : 128 * t + 128]
        for peer in (across, diagonal, sibling):
            dctx_copy(peer, c).start()
        dctx_local(c).start()
        fold = lambda value: jnp.sum(value, axis=0, keepdims=True)
        sums[0:1] += fold(normed_grad * scaled_one)
        sums[1:2] += fold(normed_grad)
        sums[2:3] += fold(upstream * scaled_two)
        sums[3:4] += fold(upstream)
        sums[4:5] += fold(first_grad)
        sums[5:6] += fold(second_grad)
        return 0

    lax.fori_loop(0, STEPS, chunk_step, 0)

    ones = jnp.ones((8, OWN_ROWS), bf16)

    def weight_grads(t, ty, target, kind):
        lanes = pl.ds(pl.multiple_of(t * 512, 512), 512)
        grad_up = mm(normed_low[...], hgrad[:, lanes], TN).astype(kind)
        grad_down = mm(second_low[...], active[:, lanes], TN).astype(kind)
        part_a = mm(first_a[...], ctxs[t], TN)
        part_b = pltpu.roll(mm(first_b[...], ctxs[t], TN), 64, 1)
        grad_out = jnp.where(iota((256, 128), 1) < 64, part_a + part_b, 0.0).astype(kind)
        shift_sum = mm(ones, hgrad[:, lanes])
        for d in range(8):
            j = 8 * ty + d
            block = slice(32 * d, 32 * d + 32)
            for b in range(4):
                cols = slice(128 * b, 128 * b + 128)
                target[j, 32 * b : 32 * b + 32, :] = grad_up[block, cols]
                target[j, 128 + 32 * b : 160 + 32 * b, :] = grad_down[block, cols]
            target[j, 256:288, :] = grad_out[block]
            vector = sums[:, 128 * (d // 4) : 128 * (d // 4) + 128]
            cols = slice(128 * (d // 2), 128 * (d // 2) + 128)
            last = jnp.where(iota((8, 128), 0) == 6, shift_sum[:, cols], vector)
            target[j, 288:304, :] = jnp.concatenate(
                [last, jnp.zeros((8, 128), f32)], axis=0
            ).astype(kind)

    def trade(ty):
        slots = pl.ds(8 * ty, 8)
        return remote(give.at[slots], take.at[slots], g_sem.at[ty], g_sem.at[2 + ty],
                      {"tensor": sibling})

    def weight_store(ty):
        slots = pl.ds(8 * ty, 8)
        return pltpu.make_async_copy(stage.at[slots], gout.at[slots], g_sem.at[4 + ty])

    for ty in range(2):
        weight_grads(other_t(ty), ty, give, bf16)
        trade(ty).start()
    for ty in range(2):
        weight_grads(mine_t(ty), ty, keep, f32)
    for ty in range(2):
        trade(ty).wait_recv()
        slots = slice(8 * ty, 8 * ty + 8)
        stage[slots] = (keep[slots] + take[slots].astype(f32)).astype(bf16)
        weight_store(ty).start()

    for copy in weights:
        copy.wait_send()
    for c in range(STEPS):
        for peer in order:
            ctx_copy(peer, c).wait_send()
            dctx_copy(peer, c).wait_send()
            dctx_arrival(peer, c).wait_recv()
        dctx_local(c).wait()
        enc_store(c).wait()
        first_store(c).wait()
    for ty in range(2):
        trade(ty).wait_send()
        weight_store(ty).wait()


def dense(ctxp, half, tokens, cotangent):
    dma = pltpu.SemaphoreType.DMA
    return pl.pallas_call(
        dense_kernel,
        out_shape=(
            jax.ShapeDtypeStruct((OWN_ROWS, 256), bf16),
            jax.ShapeDtypeStruct((PACK_ROWS // 2, 128), bf16),
            jax.ShapeDtypeStruct((OWN_ROWS, 256), f32),
            jax.ShapeDtypeStruct((GROUPS, SHARD_ROWS, 128), bf16),
        ),
        in_specs=[ANY_SPEC] * 4,
        out_specs=[ANY_SPEC] * 4,
        scratch_shapes=[
            pltpu.VMEM((PACK_ROWS // 2, 128), bf16),
            pltpu.VMEM((GROUPS, SHARD_ROWS, 128), bf16),
            pltpu.VMEM((OWN_ROWS, 256), f32),
            pltpu.VMEM((OWN_ROWS, 256), bf16),
            pltpu.VMEM((GROUPS, SHARD_ROWS, 128), bf16),
            pltpu.VMEM((GROUPS, SHARD_ROWS, 128), bf16),
            pltpu.VMEM((4, 512, 128), bf16),
            pltpu.VMEM((256, 2048), bf16),
            pltpu.VMEM((256, 2048), bf16),
            pltpu.VMEM((256, 512), bf16),
            pltpu.VMEM((256, 512), bf16),
            pltpu.VMEM((8, 256), f32),
            pltpu.VMEM((1, 2048), f32),
            pltpu.VMEM((OWN_ROWS, 256), bf16),
            pltpu.VMEM((OWN_ROWS, 256), bf16),
            pltpu.VMEM((4, 512, 128), bf16),
            pltpu.VMEM((OWN_ROWS, 256), bf16),
            pltpu.VMEM((OWN_ROWS, 256), bf16),
            pltpu.VMEM((512, 256), bf16),
            pltpu.VMEM((512, 256), bf16),
            pltpu.VMEM((OWN_ROWS, 2048), bf16),
            pltpu.VMEM((OWN_ROWS, 2048), bf16),
            pltpu.VMEM((BLOCK, 2048), f32),
            pltpu.VMEM((8, 256), f32),
            pltpu.VMEM((GROUPS, SHARD_ROWS, 128), bf16),
            pltpu.VMEM((GROUPS, SHARD_ROWS, 128), bf16),
            pltpu.VMEM((GROUPS, SHARD_ROWS, 128), f32),
            dma((4,)),
            dma((4,)),
            dma((4, STEPS)),
            dma((4, STEPS)),
            dma((4, STEPS)),
            dma((4, STEPS)),
            dma((STEPS,)),
            dma((STEPS,)),
            dma((STEPS,)),
            dma((6,)),
        ],
        compiler_params=pltpu.CompilerParams(
            collective_id=1, has_side_effects=True, vmem_limit_bytes=LIMIT_DENSE
        ),
        cost_estimate=pl.CostEstimate(
            flops=7 * 10**9, bytes_accessed=8 * 10**6, transcendentals=4 * 10**6
        ),
    )(ctxp, half, tokens, cotangent)


def tail_kernel(
    gq_hbm, gkv_hbm, tok_hbm, pos_hbm, w3, first_hbm,
    tg, gin,
    gq, gkv, tok, pos, first, load_sem,
    wall, near_send, near_recv, far_send, far_recv, mine, in_send, in_recv,
    n_send, n_recv, f_send, f_recv, t_send, t_recv, i_send, i_recv, local_sem,
):
    me = lax.axis_index("tensor")
    rank = lax.axis_index("dp")
    core = lax.rem(me, 2)
    sibling = me + 1 - 2 * core
    across = lax.rem(me + 2, 4)
    diagonal = lax.rem(sibling + 2, 4)
    peers = [lax.rem(rank + k, 8) for k in range(1, 8)]
    ready = greet(
        [{"tensor": sibling}, {"tensor": across}] + [{"dp": peer} for peer in peers]
    )
    loads = [
        pltpu.make_async_copy(source, target, load_sem.at[n])
        for n, (source, target) in enumerate(
            ((gq_hbm, gq), (gkv_hbm, gkv), (first_hbm, first), (tok_hbm, tok), (pos_hbm, pos))
        )
    ]
    for copy in loads:
        copy.start()
    lane = iota((256, 128), 1)
    wall[:, 0:128] = w3[0]
    wall[:, 128:256] = jnp.where(
        lane < 64, w3[1].astype(f32), pltpu.roll(w3[2].astype(f32), 64, 1)
    ).astype(bf16)

    def rows_of(even, odd, i):
        owner = jnp.where(lax.rem(i, 2) == 0, even, odd)
        return pl.ds(pl.multiple_of(owner * OWN_ROWS + (i // 2) * CHUNK, CHUNK), CHUNK)

    def slot(i):
        return pl.ds(pl.multiple_of(i * CHUNK, CHUNK), CHUNK)

    def partial(rows):
        return mm(jnp.concatenate([gq[rows, :], gkv[rows, :]], axis=1), wall[...], NT)

    def near_copy(i):
        return remote(near_send.at[slot(i)], near_recv.at[slot(i)],
                      n_send.at[i], n_recv.at[i], {"tensor": sibling})

    def far_copy(i):
        theirs = i + 1 - 2 * lax.rem(i, 2)
        return remote(far_send.at[slot(i)], far_recv.at[slot(theirs)],
                      f_send.at[i], f_recv.at[theirs], {"tensor": across})

    def far_arrival(i):
        return remote(far_send.at[slot(i)], far_recv.at[slot(i)],
                      f_send.at[i], f_recv.at[i], {"tensor": across})

    def share_copy(i):
        return remote(mine.at[slot(i)], tg.at[rows_of(across, me, i)],
                      t_send.at[i], t_recv.at[i], {"tensor": sibling})

    def share_arrival(i):
        return remote(mine.at[slot(i)], tg.at[rows_of(diagonal, sibling, i)],
                      t_send.at[i], t_recv.at[i], {"tensor": sibling})

    def keep_copy(i):
        return pltpu.make_async_copy(
            mine.at[slot(i)], tg.at[rows_of(across, me, i)], local_sem.at[i]
        )

    def first_stage(i, _):
        near_send[slot(i), :] = partial(rows_of(diagonal, sibling, i)).astype(bf16)
        near_copy(i).start()
        return 0

    def second_stage(i, _):
        value = partial(rows_of(across, me, i))
        odd = lax.rem(i, 2).astype(f32)
        half = pl.ds(pl.multiple_of((i // 2) * CHUNK, CHUNK), CHUNK)
        value = value + first[half, :] * odd
        near_copy(i).wait_recv()
        far_send[slot(i), :] = (value + near_recv[slot(i), :].astype(f32)).astype(bf16)
        far_copy(i).start()
        return 0

    loads[0].wait()
    loads[1].wait()
    ready()
    lax.fori_loop(0, 2, first_stage, 0)
    loads[2].wait()

    def both_stages(i, _):
        first_stage(i + 2, 0)
        second_stage(i, 0)
        return 0

    lax.fori_loop(0, 6, both_stages, 0)
    lax.fori_loop(6, 8, second_stage, 0)

    loads[3].wait()
    loads[4].wait()

    def inward_step(i, carry):
        left, right, total = carry
        rows = pl.ds(pl.multiple_of(i * 1024, 1024), 1024)
        token = tok[rows, :]
        query_in = (token.astype(f32) + pos[rows, :].astype(f32)).astype(bf16)
        both = jnp.concatenate([gq[rows, :], gkv[rows, :]], axis=1)
        left = left + mm(query_in, both, TN)
        right = right + mm(token, gkv[rows, :], TN)
        total = total + mm(jnp.ones((8, 1024), bf16), both)
        return left, right, total

    left, right, total = lax.fori_loop(
        0, 4, inward_step,
        (jnp.zeros((256, 256), f32), jnp.zeros((256, 128), f32), jnp.zeros((8, 256), f32)),
    )
    joined = jnp.concatenate([jnp.where(lane < 64, left[:, 0:128], right), left[:, 128:256]], 1)
    for d in range(8):
        in_send[d, 0:32, :] = joined[32 * d : 32 * d + 32]
        in_send[d, 32:40, :] = total
    in_copies = []
    for k, peer in enumerate(peers):
        copy = remote(
            in_send.at[peer], in_recv.at[rank], i_send.at[k], i_recv.at[rank], {"dp": peer}
        )
        copy.start()
        in_copies.append(copy)

    def third_stage(i, _):
        far_arrival(i).wait_recv()
        mine[slot(i), :] = (
            far_send[slot(i), :].astype(f32) + far_recv[slot(i), :].astype(f32)
        ).astype(bf16)
        share_copy(i).start()
        keep_copy(i).start()
        return 0

    def third_pair(i, _):
        third_stage(2 * i + 1, 0)
        third_stage(2 * i, 0)
        return 0

    lax.fori_loop(0, 4, third_pair, 0)

    gathered = in_send[rank]
    for peer in peers:
        remote(
            in_send.at[peer], in_recv.at[peer], i_send.at[0], i_recv.at[peer], {"dp": peer}
        ).wait_recv()
        gathered = gathered + in_recv[peer]
    gin[...] = gathered

    for copy in in_copies:
        copy.wait_send()

    def finish(i, _):
        near_copy(i).wait_send()
        far_copy(i).wait_send()
        share_copy(i).wait_send()
        keep_copy(i).wait()
        share_arrival(i).wait_recv()
        return 0

    lax.fori_loop(0, 8, finish, 0)


def tail(gq, gkv, tokens, positions, w3, first):
    dma = pltpu.SemaphoreType.DMA
    return pl.pallas_call(
        tail_kernel,
        out_shape=(
            jax.ShapeDtypeStruct((PACK_ROWS, 256), bf16),
            jax.ShapeDtypeStruct((40, 256), f32),
        ),
        in_specs=[ANY_SPEC] * 4 + [VMEM_SPEC, ANY_SPEC],
        out_specs=[ANY_SPEC, VMEM_SPEC],
        scratch_shapes=[
            pltpu.VMEM((PACK_ROWS, 128), bf16),
            pltpu.VMEM((PACK_ROWS, 128), bf16),
            pltpu.VMEM((PACK_ROWS, 256), bf16),
            pltpu.VMEM((PACK_ROWS, 256), bf16),
            pltpu.VMEM((OWN_ROWS, 256), f32),
            dma((5,)),
            pltpu.VMEM((256, 256), bf16),
        ]
        + [pltpu.VMEM((8 * CHUNK, 256), bf16)] * 5
        + [
            pltpu.VMEM((8, 40, 256), f32),
            pltpu.VMEM((8, 40, 256), f32),
            dma((8,)),
            dma((8,)),
            dma((8,)),
            dma((8,)),
            dma((8,)),
            dma((8,)),
            dma((7,)),
            dma((8,)),
            dma((8,)),
        ],
        compiler_params=pltpu.CompilerParams(
            collective_id=2, has_side_effects=True, vmem_limit_bytes=LIMIT_TAIL
        ),
        cost_estimate=pl.CostEstimate(
            flops=3 * 10**9, bytes_accessed=16 * 10**6, transcendentals=0
        ),
    )(gq, gkv, tokens, positions, w3, first)


def update_kernel(pieces, gin, narrow, *refs):
    blocks, refs = refs[0:4], refs[4:]
    masters, firsts, seconds = refs[0:7], refs[7:14], refs[14:21]
    wide_out, encoded = refs[21:23]
    grads, news, lows, moms, varis = (
        refs[23:30], refs[30:37], refs[37:41], refs[41:48], refs[48:55],
    )
    stage, sem = refs[55:57]
    me = lax.axis_index("dp")
    copies = []
    col = lax.axis_index("tensor")
    low, high = lax.rem(col, 2), col // 2
    owners = (col, 2 * high + 1 - low, 2 * (1 - high) + low, 2 * (1 - high) + 1 - low)
    for i in range(4):
        rows = pl.ds(pl.multiple_of(owners[i] * OWN_ROWS, OWN_ROWS), OWN_ROWS)
        copy = pltpu.make_async_copy(blocks[i], encoded.at[rows], sem.at[8 + i])
        copy.start()
        copies.append(copy)
    for i in range(8):
        rows = pl.ds(512 * i, 512)
        stage[rows, :] = narrow[rows, :].astype(f32)
        copy = pltpu.make_async_copy(stage.at[rows], wide_out.at[rows], sem.at[i])
        copy.start()
        copies.append(copy)

    def add(j, total):
        return total + pieces[j].astype(f32)

    total = lax.fori_loop(0, GROUPS, add, jnp.zeros((SHARD_ROWS, 128), f32))
    wide = gin[...]
    small = total[288:296]
    vec_grad = pltpu.roll(small, lax.rem(128 - lax.rem(me, 4) * 32, 128), 1)[0:6, 0:32]
    shift_grad = pltpu.roll(small, lax.rem(128 - lax.rem(me, 2) * 64, 128), 1)[6:7, 0:64]
    off_q = pltpu.roll(wide[32:40, 0:128], lax.rem(128 - me * 8, 128), 1)
    off_v = pltpu.roll(wide[32:40, 128:256], 64 - me * 8, 1)
    off_grad = jnp.where(iota((8, 128), 0) == 0, off_q, off_v)[0:2, 0:8]
    left, right = wide[0:32, 0:128], wide[0:32, 128:256]
    inward_grads = (left[:, 0:64], right[:, 0:64], pltpu.roll(left, 64, 1)[:, 0:64])
    joined = lambda base: jnp.concatenate(
        [total[base + 32 * b : base + 32 * b + 32] for b in range(4)], axis=1
    )
    plain = (None, total[256:288, 0:64], joined(0), joined(128), vec_grad, off_grad, shift_grad)

    def apply(index, at, gradient):
        new, momentum, variance = adamw(
            masters[index][at], gradient, firsts[index][at], seconds[index][at],
            step_rates[index],
        )
        grads[index][at] = gradient
        news[index][at] = new
        moms[index][at] = momentum
        varis[index][at] = variance
        if index < 4:
            lows[index][at] = new.astype(bf16)

    for which in range(3):
        apply(0, which, inward_grads[which])
    for index in range(1, 7):
        apply(index, Ellipsis, plain[index])
    for copy in copies:
        copy.wait()


def update(pieces, gin, narrow, blocks, masters, firsts, seconds):
    shapes = [m.shape for m in masters]
    of = lambda kind, count: [jax.ShapeDtypeStruct(s, kind) for s in shapes[:count]]
    out = [
        jax.ShapeDtypeStruct((PACK_ROWS, 256), f32),
        jax.ShapeDtypeStruct((PACK_ROWS, 256), bf16),
    ]
    out = out + of(f32, 7) + of(f32, 7) + of(bf16, 4) + of(f32, 7) + of(f32, 7)
    return pl.pallas_call(
        update_kernel,
        out_shape=out,
        in_specs=[VMEM_SPEC] * 28,
        out_specs=[ANY_SPEC] * 2 + [VMEM_SPEC] * (len(out) - 2),
        scratch_shapes=[pltpu.VMEM((PACK_ROWS, 256), f32), pltpu.SemaphoreType.DMA((12,))],
        compiler_params=pltpu.CompilerParams(vmem_limit_bytes=LIMIT_UPDATE),
    )(pieces, gin, narrow, *blocks, *masters, *firsts, *seconds)


def exchange(pieces):
    groups = [[4 * d + 2 * y + c for y in range(2) for d in range(8)] for c in range(2)]
    return lax.all_to_all(
        pieces, ("dp", "tensor"), 0, 0, axis_index_groups=groups, tiled=True
    )


def turned(group):
    inward, outward, upward, downward, vectors, offsets, shifts = group
    return [inward, outward.T, upward, downward.T, vectors, offsets, shifts.reshape(1, -1)]


def returned(group):
    if len(group) == 4:
        return [group[0], group[1].T, group[2], group[3].T]
    inward, outward, upward, downward, vectors, offsets, shifts = group
    return [inward, outward.T, upward, downward.T, vectors, offsets, shifts.reshape(-1)]


def body_pods(tokens, positions, segment_ids, pad_flags, cotangent, *state):
    masters, firsts, seconds = (turned(state[7 * i : 7 * i + 7]) for i in range(3))
    inward, out_t, upward, down_t, vectors, offsets, shifts = masters
    pack, w3, off = gather_weights(upward, down_t, out_t, vectors, shifts, inward, offsets)
    half = exchange(pack)
    ctxp, *saved = attend_forward(tokens, positions, w3, off, segment_ids, pad_flags)
    own, dctx, first, gout = dense(ctxp, half, tokens, cotangent)
    blocks = [own] + [
        lax.ppermute(own, "tensor", [(t, t ^ flip) for t in range(4)]) for flip in (1, 2, 3)
    ]
    pieces = exchange(gout)
    gq, gkv = attend_backward(dctx, *saved)
    narrow, gin = tail(gq, gkv, tokens, positions, w3, first)
    token_grad, encoded, *outs = update(pieces, gin, narrow, blocks, masters, firsts, seconds)
    grads, news, lows, moms, varis = outs[:7], outs[7:14], outs[14:18], outs[18:25], outs[25:]
    return (
        encoded,
        token_grad,
        *returned(grads),
        *returned(news),
        *returned(lows),
        *returned(moms),
        *returned(varis),
    )


def body(
    tokens,
    positions,
    segment_ids,
    pad_flags,
    cotangent,
    inward,
    outward,
    upward,
    downward,
    vectors,
    offsets,
    shifts,
    first_inward,
    first_outward,
    first_upward,
    first_downward,
    first_vectors,
    first_offsets,
    first_shifts,
    second_inward,
    second_outward,
    second_upward,
    second_downward,
    second_vectors,
    second_offsets,
    second_shifts,
):
    w_inward, w_outward, w_upward, w_downward, vector_low, offset_low, shift_low = (
        lax.all_gather(inward.astype(jnp.bfloat16), "dp", axis=1, tiled=True),
        lax.all_gather(outward.astype(jnp.bfloat16), "dp", axis=1, tiled=True),
        lax.all_gather(upward.astype(jnp.bfloat16), "dp", axis=0, tiled=True),
        lax.all_gather(downward.astype(jnp.bfloat16), "dp", axis=1, tiled=True),
        lax.all_gather(vectors.astype(jnp.bfloat16), "dp", axis=1, tiled=True),
        lax.all_gather(offsets.astype(jnp.bfloat16), "dp", axis=1, tiled=True),
        lax.all_gather(shifts.astype(jnp.bfloat16), "dp", axis=0, tiled=True),
    )
    vector_wide = vector_low.astype(jnp.float32)
    offset_wide = offset_low.astype(jnp.float32)
    shift_wide = shift_low.astype(jnp.float32)
    input_wide = tokens.astype(jnp.float32)
    query_in = (input_wide + positions.astype(jnp.float32)).astype(jnp.bfloat16)
    w_lanes = jnp.pad(w_inward, ((0, 0), (0, 0), (0, 64)))
    off_lanes = jnp.pad(offset_wide, ((0, 6), (0, 64)))
    packed, *saved = attend_forward(
        tokens, positions, w_lanes, off_lanes, segment_ids, pad_flags
    )
    pairs = packed.reshape(16, 128, 2, 64)
    context_low = pairs.transpose(0, 2, 1, 3).reshape(PACK_ROWS, 64)
    first_sum = input_wide + summed(product(context_low, w_outward)) + vector_wide[4]
    normed, scaled_one, inverse_one = norm_forward(first_sum, vector_wide[0], vector_wide[1])
    normed_low = normed.astype(jnp.bfloat16)
    hidden = product(normed_low, w_upward) + shift_wide
    unit_value, unit_back = jax.vjp(smooth_unit, hidden)
    active = unit_value.astype(jnp.bfloat16)
    second_sum = normed + summed(product(active, w_downward)) + vector_wide[5]
    result, scaled_two, inverse_two = norm_forward(second_sum, vector_wide[2], vector_wide[3])
    encoded = result.astype(jnp.bfloat16)
    upstream = cotangent.astype(jnp.float32)
    second_grad, gain_two, shift_two = norm_backward(
        upstream, scaled_two, inverse_two, vector_wide[2]
    )
    down_low = second_grad.astype(jnp.bfloat16)
    grad_downward = product_left(active, down_low)
    hidden_low = unit_back(product_right(down_low, w_downward))[0].astype(jnp.bfloat16)
    grad_upward = product_left(normed_low, hidden_low)
    grad_shifts = jnp.sum(hidden_low.astype(jnp.float32), axis=0)
    normed_grad = second_grad + summed(product_right(hidden_low, w_upward))
    first_grad, gain_one, shift_one = norm_backward(
        normed_grad, scaled_one, inverse_one, vector_wide[0]
    )
    first_low = first_grad.astype(jnp.bfloat16)
    grad_outward = product_left(context_low, first_low)
    context_grad = product_right(first_low, w_outward).astype(jnp.bfloat16)
    halves = context_grad.reshape(16, 2, 128, 64)
    gq, gkv = attend_backward(
        halves.transpose(0, 2, 1, 3).reshape(2048, 128), *saved
    )
    query_grad, key_grad, value_grad = gq[:, :64], gkv[:, :64], gkv[:, 64:]
    grad_inward = jnp.stack(
        [
            product_left(query_in, query_grad),
            product_left(query_in, key_grad),
            product_left(tokens, value_grad),
        ]
    )
    grad_offsets = jnp.stack(
        [
            jnp.sum(query_grad.astype(jnp.float32), axis=0),
            jnp.sum(value_grad.astype(jnp.float32), axis=0),
        ]
    )
    input_part = (
        product_right(query_grad, w_inward[0])
        + product_right(key_grad, w_inward[1])
        + product_right(value_grad, w_inward[2])
    )
    input_grad = first_grad + summed(input_part)
    grad_vectors = jnp.stack(
        [
            gain_one,
            shift_one,
            gain_two,
            shift_two,
            jnp.sum(first_grad, axis=0),
            jnp.sum(second_grad, axis=0),
        ]
    )
    reduced = (
        lax.psum_scatter(grad_inward, "dp", scatter_dimension=1, tiled=True),
        lax.psum_scatter(grad_outward, "dp", scatter_dimension=1, tiled=True),
        lax.psum_scatter(grad_upward, "dp", scatter_dimension=0, tiled=True),
        lax.psum_scatter(grad_downward, "dp", scatter_dimension=1, tiled=True),
        lax.psum_scatter(grad_vectors, "dp", scatter_dimension=1, tiled=True),
        lax.psum_scatter(grad_offsets, "dp", scatter_dimension=1, tiled=True),
        lax.psum_scatter(grad_shifts, "dp", scatter_dimension=0, tiled=True),
    )
    masters = (inward, outward, upward, downward, vectors, offsets, shifts)
    firsts = (
        first_inward,
        first_outward,
        first_upward,
        first_downward,
        first_vectors,
        first_offsets,
        first_shifts,
    )
    seconds = (
        second_inward,
        second_outward,
        second_upward,
        second_downward,
        second_vectors,
        second_offsets,
        second_shifts,
    )
    updated = []
    momenta = []
    variances = []
    for master, gradient, old_first, old_second, step_rate in zip(
        masters, reduced, firsts, seconds, step_rates
    ):
        new_master, momentum, variance = adamw(master, gradient, old_first, old_second, step_rate)
        updated.append(new_master)
        momenta.append(momentum)
        variances.append(variance)
    return (
        encoded,
        input_grad,
        reduced[0],
        reduced[1],
        reduced[2],
        reduced[3],
        reduced[4],
        reduced[5],
        reduced[6],
        updated[0],
        updated[1],
        updated[2],
        updated[3],
        updated[4],
        updated[5],
        updated[6],
        updated[0].astype(jnp.bfloat16),
        updated[1].astype(jnp.bfloat16),
        updated[2].astype(jnp.bfloat16),
        updated[3].astype(jnp.bfloat16),
        momenta[0],
        momenta[1],
        momenta[2],
        momenta[3],
        momenta[4],
        momenta[5],
        momenta[6],
        variances[0],
        variances[1],
        variances[2],
        variances[3],
        variances[4],
        variances[5],
        variances[6],
    )


def solution(mesh):
    in_specs = (
        P("dp", None),
        P("dp", None),
        P("dp", None),
        P("dp", None),
        P("dp", None),
        P(None, "dp", "tensor"),
        P("tensor", "dp"),
        P("dp", "tensor"),
        P("tensor", "dp"),
        P(None, "dp"),
        P(None, ("tensor", "dp")),
        P(("tensor", "dp")),
        P(None, "dp", "tensor"),
        P("tensor", "dp"),
        P("dp", "tensor"),
        P("tensor", "dp"),
        P(None, "dp"),
        P(None, ("tensor", "dp")),
        P(("tensor", "dp")),
        P(None, "dp", "tensor"),
        P("tensor", "dp"),
        P("dp", "tensor"),
        P("tensor", "dp"),
        P(None, "dp"),
        P(None, ("tensor", "dp")),
        P(("tensor", "dp")),
    )
    out_specs = (
        P("dp", None),
        P("dp", None),
        P(None, "dp", "tensor"),
        P("tensor", "dp"),
        P("dp", "tensor"),
        P("tensor", "dp"),
        P(None, "dp"),
        P(None, ("tensor", "dp")),
        P(("tensor", "dp")),
        P(None, "dp", "tensor"),
        P("tensor", "dp"),
        P("dp", "tensor"),
        P("tensor", "dp"),
        P(None, "dp"),
        P(None, ("tensor", "dp")),
        P(("tensor", "dp")),
        P(None, "dp", "tensor"),
        P("tensor", "dp"),
        P("dp", "tensor"),
        P("tensor", "dp"),
        P(None, "dp", "tensor"),
        P("tensor", "dp"),
        P("dp", "tensor"),
        P("tensor", "dp"),
        P(None, "dp"),
        P(None, ("tensor", "dp")),
        P(("tensor", "dp")),
        P(None, "dp", "tensor"),
        P("tensor", "dp"),
        P("dp", "tensor"),
        P("tensor", "dp"),
        P(None, "dp"),
        P(None, ("tensor", "dp")),
        P(("tensor", "dp")),
    )
    pods = mesh.shape["dp"] == 8 and mesh.shape["tensor"] == 4
    chosen = body_pods if pods else body
    return jax.shard_map(chosen, mesh=mesh, in_specs=in_specs, out_specs=out_specs, check_vma=False)
```

```python
import functools
import jax
import jax.numpy as jnp
from jax import lax
from jax.experimental import pallas as pl
from jax.experimental.pallas import tpu as pltpu
from jax.sharding import PartitionSpec as P

HEAD_DIM = 32
MIB = 2**20
LIMIT_GATHER = 58 * MIB
LIMIT_FORWARD = 58 * MIB
LIMIT_DENSE = 58 * MIB
LIMIT_BACKWARD = 58 * MIB
LIMIT_TAIL = 58 * MIB
LIMIT_UPDATE = 58 * MIB
PACK_ROWS = 4096
IMAGES = 5
SPAN = PACK_ROWS + 512
BACK_QUERY = (512, 256)
BACK_KEY = (1024, 512, 256)
FORWARD_QUERY = (1024, 512, 256)
FORWARD_KEY = (1024, 512, 256)
LOG_SCALE = HEAD_DIM**-0.5 * 1.4426950408889634
FENCE = 2.0**100
LARGE = 2.0**100
SMALL = 2.0**-60
NN = (((1,), (0,)), ((), ()))
NT = (((1,), (1,)), ((), ()))
TN = (((0,), (0,)), ((), ()))
bf16 = jnp.bfloat16
f32 = jnp.float32


def mm(left, right, dims=NN):
    return lax.dot_general(left, right, dims, preferred_element_type=f32)


def iota(shape, dim):
    return lax.broadcasted_iota(jnp.int32, shape, dim)


def plan(length, sizes):
    out = []
    offset = 0
    least = sizes[-1]
    for size in sizes:
        left = jnp.maximum(length - offset, 0)
        count = (left + least - 1) // size
        out.append((size, offset, count))
        offset = offset + count * size
    return out


def twice(step):
    def both(i, carry):
        return step(2 * i + 1, step(2 * i, carry))

    return both


def pieces_of(value):
    one = value.astype(bf16).astype(f32)
    rest = value - one
    two = rest.astype(bf16).astype(f32)
    return one, two, rest - two


def attend_forward_kernel(
    tok_hbm, pos_hbm, w3, off, seg, pad,
    packed_hbm, ctx_hbm, qa_hbm, qw_hbm, ka_hbm, va_hbm, rank, bounds,
    tok, pos, raw, ctx_pair, qa, qw, ka, va, wqd, wkd, compact, dst, packed, load_sem, save_sem, close_sem,
):
    loads = []
    for part in range(4):
        rows = pl.ds(1024 * part, 1024)
        for which, (source, target) in enumerate(((tok_hbm, tok), (pos_hbm, pos))):
            copy = pltpu.make_async_copy(
                source.at[rows], target.at[rows], load_sem.at[2 * part + which]
            )
            copy.start()
            loads.append(copy)
    lane = iota((256, 128), 1)
    for which, spread in ((0, wqd), (1, wkd)):
        base = w3[which].astype(f32)
        left = pltpu.roll(base, 32, 1)
        right = pltpu.roll(base, 96, 1)
        spread[:, :128] = jnp.where(lane < 32, base, jnp.where(lane < 64, left, 0.0)).astype(bf16)
        spread[:, 128:] = jnp.where(lane < 32, right, jnp.where(lane < 64, base, 0.0)).astype(bf16)
    lane8 = iota((8, 128), 1)
    off_rows = off[...]
    off_left = pltpu.roll(off_rows, 32, 1)
    off_right = pltpu.roll(off_rows, 96, 1)
    q_bias = jnp.concatenate(
        [
            jnp.where(lane8 < 32, off_rows, jnp.where(lane8 < 64, off_left, 0.0))[0:1],
            jnp.where(lane8 < 32, off_right, jnp.where(lane8 < 64, off_rows, 0.0))[0:1],
        ],
        axis=1,
    )
    v_bias = jnp.where(lane8 < 64, off_rows, 0.0)[1:2]

    segment = seg[...]
    open_key = jnp.where(pad[...] == 0, 1.0, 0.0)
    grid_row = iota((32, 128), 0)
    before = (iota((128, 128), 0) < iota((128, 128), 1)).astype(bf16)
    in_row = mm(open_key.astype(bf16), before)
    row_total = jnp.broadcast_to(jnp.sum(open_key, axis=1, keepdims=True), (32, 128))
    above = (iota((32, 32), 1) < iota((32, 32), 0)).astype(bf16)
    place = (in_row + mm(above, row_total.astype(bf16))).astype(jnp.int32)
    place = jnp.where(open_key > 0.5, place, -1)
    for r in range(32):
        rank[r, :, :] = place[r : r + 1, :]
    for s in range(IMAGES + 1):
        if s == 0:
            bounds[0] = 0
            bounds[8] = 0
        else:
            low = (segment < s).astype(f32)
            bounds[s] = jnp.sum(low).astype(jnp.int32)
            bounds[8 + s] = jnp.sum(low * open_key).astype(jnp.int32)
    for i in range(16):
        dst[i] = jnp.sum(jnp.where(grid_row < 2 * i, open_key, 0.0)).astype(jnp.int32)
    for i in range(16):
        bounds[16 + i] = dst[i]
    total = bounds[8 + IMAGES]

    lane_row = iota((1, 128), 1)
    q_from = jnp.full((1, 128), SPAN, jnp.int32)
    q_to = jnp.full((1, 128), SPAN, jnp.int32)
    k_from = jnp.full((1, 128), SPAN, jnp.int32)
    k_to = jnp.full((1, 128), SPAN, jnp.int32)
    for s in range(IMAGES):
        at = lane_row == 64 + s
        q_from = jnp.where(at, bounds[s], q_from)
        q_to = jnp.where(at, bounds[s + 1], q_to)
        k_from = jnp.where(at, bounds[8 + s], k_from)
        k_to = jnp.where(at, bounds[9 + s], k_to)

    compact[pl.ds(0, 16), :] = jnp.zeros((16, 512), bf16)
    qa[:, pl.ds(PACK_ROWS, SPAN - PACK_ROWS), :] = jnp.zeros((2, SPAN - PACK_ROWS, 128), bf16)
    qw[pl.ds(PACK_ROWS, SPAN - PACK_ROWS), :] = jnp.zeros((SPAN - PACK_ROWS, 128), bf16)

    lane_q = iota((256, 128), 1)
    row_q = iota((256, 128), 0)

    def project(i, _):
        first = pl.multiple_of(i * 256, 256)
        rows = pl.ds(first, 256)
        token = tok[rows, :]
        query_in = (token.astype(f32) + pos[rows, :].astype(f32)).astype(bf16)
        both = (mm(query_in, wqd[...]) + q_bias).astype(bf16).astype(f32)
        here = row_q + first
        outside = (here < q_from) | (here >= q_to)
        feature = jnp.where(
            lane_q < 64 + IMAGES, jnp.where(outside, 1.0, 0.0), jnp.where(lane_q == 69, 1.0, 0.0)
        )
        for h in range(2):
            exact = both[:, 128 * h : 128 * h + 128] * LOG_SCALE
            high = exact.astype(bf16).astype(f32)
            qa[h, rows, :] = jnp.where(
                lane_q < 32, high, jnp.where(lane_q < 64, exact - high, feature)
            ).astype(bf16)
        qw[rows, :] = jnp.where(
            lane_q < 32, both[:, :128], jnp.where(lane_q < 64, both[:, 128:], 0.0)
        ).astype(bf16)
        start = dst[i]
        aligned = pl.multiple_of((start // 16) * 16, 16)
        places = jnp.concatenate([rank[2 * i], rank[2 * i + 1]], axis=1)
        hot = jnp.where(iota((272, 256), 0) + aligned == places, 1.0, 0.0).astype(bf16)
        moved = mm(hot, jnp.concatenate([query_in, token], axis=1)).astype(bf16)
        head = pl.ds(aligned, 16)
        compact[head, :] = compact[head, :] + moved[:16]
        compact[pl.ds(pl.multiple_of(aligned + 16, 16), 256), :] = moved[16:]
        return 0

    for part in range(4):
        loads[2 * part].wait()
        loads[2 * part + 1].wait()
        lax.fori_loop(2 * part, 2 * part + 2, twice(project), 0)

    lane_k = iota((512, 128), 1)
    row_k = iota((512, 128), 0)

    def project_keys(i, _):
        first = pl.multiple_of(i * 512, 512)
        rows = pl.ds(first, 512)
        here = row_k + first
        real = here < total
        both = mm(compact[rows, 0:256], wkd[...])
        value = mm(compact[rows, 256:512], w3[2]) + v_bias
        value = jnp.where(real, value, 0.0)
        inside = (here >= k_from) & (here < k_to)
        feature = jnp.where(inside, -FENCE, 0.0)
        feature = jnp.where(lane_k == 69, jnp.where(real, 0.0, -FENCE), feature)
        for h in range(2):
            spot = (lane_k >= 70 + 3 * h) & (lane_k < 73 + 3 * h)
            key = jnp.where(real, both[:, 128 * h : 128 * h + 128], 0.0)
            ka[h, rows, :] = jnp.where(
                lane_k < 64, key, jnp.where(spot, 1.0, feature)
            ).astype(bf16)
        va[0, rows, :] = jnp.where(
            lane_k < 32, value, jnp.where(lane_k < 35, 1.0, 0.0)
        ).astype(bf16)
        va[1, rows, :] = jnp.where(
            lane_k < 3, 1.0, jnp.where((lane_k >= 32) & (lane_k < 64), value, 0.0)
        ).astype(bf16)
        return 0

    lax.fori_loop(0, (total + 767) // 512, project_keys, 0)
    extra = pl.ds(PACK_ROWS, SPAN - PACK_ROWS)
    saves = [
        pltpu.make_async_copy(source, target, save_sem.at[n])
        for n, (source, target) in enumerate(
            ((qw, qw_hbm), (ka, ka_hbm), (va, va_hbm), (qa.at[:, extra], qa_hbm.at[:, extra]))
        )
    ]
    for copy in saves:
        copy.start()

    def per_segment(safe, s, _):
        q_start, q_end = bounds[s], bounds[s + 1]
        k_start, k_end = bounds[8 + s], bounds[9 + s]
        q_first = (q_start // 16) * 16
        k_first = (k_start // 16) * 16

        def per_query(size, base, i, _):
            q_row = pl.multiple_of(base + i * size, 16)
            q_rows = pl.ds(q_row, size)
            head = pl.ds(q_row, 16)
            kept = iota((16, 128), 0) + q_row < q_start
            olds = [raw[h, head, :] for h in range(2)]
            for h in range(2):
                raw[h, q_rows, :] = jnp.zeros((size, 128), f32)

            def per_key(tops, span, first_key, j, _):
                k_rows = pl.ds(pl.multiple_of(first_key + j * span, 16), span)
                for h in range(2):
                    score = mm(qa[h, q_rows, :], ka[h, k_rows, :], NT)
                    if tops is not None:
                        score = score - tops[h]
                    weight = jnp.exp2(score).astype(bf16)
                    raw[h, q_rows, :] += mm(weight, va[h, k_rows, :])
                return 0

            def peak(j, tops):
                k_rows = pl.ds(pl.multiple_of(k_first + j * 256, 16), 256)
                out = []
                for h in range(2):
                    score = mm(qa[h, q_rows, :], ka[h, k_rows, :], NT)
                    out.append(jnp.maximum(tops[h], jnp.max(score, axis=1, keepdims=True)))
                return tuple(out)

            if safe:
                steps = (k_end - k_first + 255) // 256
                low = jnp.full((size, 1), -3.0e38, f32)
                tops = lax.fori_loop(0, steps, peak, (low, low))
                lane = iota((size, 128), 1)
                raw[0, q_rows, :] = jnp.where(
                    lane == 64, tops[0], jnp.where(lane == 65, tops[1], 0.0)
                )
                lax.fori_loop(0, steps, functools.partial(per_key, tops, 256, k_first), 0)
            else:
                for span, offset, count in plan(k_end - k_first, FORWARD_KEY):
                    lax.fori_loop(
                        0, count, functools.partial(per_key, None, span, k_first + offset), 0
                    )
            for h in range(2):
                raw[h, head, :] = jnp.where(kept, olds[h], raw[h, head, :])
            return 0

        for size, offset, count in plan(q_end - q_first, FORWARD_QUERY):
            lax.fori_loop(0, count, functools.partial(per_query, size, q_first + offset), 0)
        return 0

    lax.fori_loop(0, IMAGES, functools.partial(per_segment, False), 0)

    def extremes(i, carry):
        rows = pl.ds(pl.multiple_of(i * 512, 512), 512)
        lane = iota((512, 128), 1)
        both = jnp.where(lane == 32, raw[0, rows, :], jnp.where(lane == 0, raw[1, rows, :], 1.0))
        return (
            jnp.maximum(carry[0], jnp.max(both, axis=0, keepdims=True)),
            jnp.minimum(carry[1], jnp.min(both, axis=0, keepdims=True)),
        )

    one_row = jnp.ones((1, 128), f32)
    most, least = lax.fori_loop(0, 8, extremes, (one_row, one_row))
    fine = (jnp.max(most) < LARGE) & (jnp.min(least) > SMALL)

    @pl.when(jnp.logical_not(fine))
    def _():
        lax.fori_loop(0, IMAGES, functools.partial(per_segment, True), 0)

    def close(b, _):
        rows = pl.ds(pl.multiple_of(b * 256, 256), 256)
        pair_rows = pl.ds(pl.multiple_of(b * 128, 128), 128)
        lane = iota((256, 128), 1)
        zero, one = raw[0, rows, :], raw[1, rows, :]
        l_zero = jnp.broadcast_to(zero[:, 32:33], (256, 128))
        l_one = jnp.broadcast_to(one[:, 0:1], (256, 128))
        lower = lane < 32
        joined = jnp.where(lower, zero, one) / jnp.where(lower, l_zero, l_one)
        early = lane < 73
        shift = jnp.where(
            early,
            jnp.broadcast_to(zero[:, 64:65], (256, 128)),
            jnp.broadcast_to(zero[:, 65:66], (256, 128)),
        )
        parts = pieces_of(-(shift + jnp.log2(jnp.where(early, l_zero, l_one))))
        for h in range(2):
            at = 70 + 3 * h
            value = qa[h, rows, :].astype(f32)
            for n in range(3):
                value = jnp.where(lane == at + n, parts[n], value)
            qa[h, rows, :] = value.astype(bf16)
        pair = jnp.where(
            iota((128, 128), 1) < 64, joined[0:128], pltpu.roll(joined[128:256], 64, 1)
        )
        ctx_pair[pair_rows, :] = pair
        packed[pair_rows, :] = pair.astype(bf16)
        return 0

    def stores(i):
        rows = pl.ds(pl.multiple_of(i * 512, 512), 512)
        pairs = pl.ds(pl.multiple_of(i * 256, 256), 256)
        return (
            pltpu.make_async_copy(qa.at[:, rows], qa_hbm.at[:, rows], close_sem.at[0, i]),
            pltpu.make_async_copy(ctx_pair.at[pairs], ctx_hbm.at[pairs], close_sem.at[1, i]),
            pltpu.make_async_copy(packed.at[pairs], packed_hbm.at[pairs], close_sem.at[2, i]),
        )

    def close_two(i, _):
        twice(close)(i, 0)
        for copy in stores(i):
            copy.start()
        return 0

    def settle(i, _):
        for copy in stores(i):
            copy.wait()
        return 0

    lax.fori_loop(0, 8, close_two, 0)
    for copy in saves:
        copy.wait()
    lax.fori_loop(0, 8, settle, 0)


VMEM_SPEC = pl.BlockSpec(memory_space=pltpu.VMEM)
SMEM_SPEC = pl.BlockSpec(memory_space=pltpu.SMEM)
ANY_SPEC = pl.BlockSpec(memory_space=pl.ANY)


def attend_forward(tokens, positions, w3, off, segment, padding):
    return pl.pallas_call(
        attend_forward_kernel,
        out_shape=(
            jax.ShapeDtypeStruct((2048, 128), bf16),
            jax.ShapeDtypeStruct((2048, 128), f32),
            jax.ShapeDtypeStruct((2, SPAN, 128), bf16),
            jax.ShapeDtypeStruct((SPAN, 128), bf16),
            jax.ShapeDtypeStruct((2, SPAN, 128), bf16),
            jax.ShapeDtypeStruct((2, SPAN, 128), bf16),
            jax.ShapeDtypeStruct((32, 1, 128), jnp.int32),
            jax.ShapeDtypeStruct((32,), jnp.int32),
        ),
        in_specs=[ANY_SPEC] * 2 + [VMEM_SPEC] * 4,
        out_specs=[ANY_SPEC] * 6 + [VMEM_SPEC, SMEM_SPEC],
        scratch_shapes=[
            pltpu.VMEM((PACK_ROWS, 256), bf16),
            pltpu.VMEM((PACK_ROWS, 256), bf16),
            pltpu.VMEM((2, SPAN, 128), f32),
            pltpu.VMEM((2048, 128), f32),
            pltpu.VMEM((2, SPAN, 128), bf16),
            pltpu.VMEM((SPAN, 128), bf16),
            pltpu.VMEM((2, SPAN, 128), bf16),
            pltpu.VMEM((2, SPAN, 128), bf16),
            pltpu.VMEM((256, 256), bf16),
            pltpu.VMEM((256, 256), bf16),
            pltpu.VMEM((SPAN, 512), bf16),
            pltpu.SMEM((16,), jnp.int32),
            pltpu.VMEM((2048, 128), bf16),
            pltpu.SemaphoreType.DMA((8,)),
            pltpu.SemaphoreType.DMA((4,)),
            pltpu.SemaphoreType.DMA((3, 8)),
        ],
        compiler_params=pltpu.CompilerParams(vmem_limit_bytes=LIMIT_FORWARD),
        cost_estimate=pl.CostEstimate(
            flops=20 * 10**9, bytes_accessed=20 * 10**6, transcendentals=10**7
        ),
    )(tokens, positions, w3, off, segment.reshape(32, 128), padding.reshape(32, 128))


def attend_backward_kernel(
    packed, ctx_hbm, qa_hbm, qw_hbm, ka_hbm, va_hbm, rank, bounds,
    gq_hbm, gkv_hbm,
    ctx, qa, qw, ka, va, do, kw, dq, dkv, turned_sum, gq, gkv, load_sem, store_sem,
):
    loads = [
        pltpu.make_async_copy(source, target, load_sem.at[n])
        for n, (source, target) in enumerate(
            ((ctx_hbm, ctx), (qa_hbm, qa), (ka_hbm, ka), (va_hbm, va), (qw_hbm, qw))
        )
    ]
    for copy in loads:
        copy.start()
    for i in range(SPAN // 512):
        rows = pl.ds(512 * i, 512)
        dq[rows, :] = jnp.zeros((512, 128), f32)
        dkv[rows, :] = jnp.zeros((512, 128), f32)
    do[:, pl.ds(PACK_ROWS, SPAN - PACK_ROWS), :] = jnp.zeros((2, SPAN - PACK_ROWS, 128), bf16)
    loads[0].wait()
    lane = iota((128, 128), 1)
    for b in range(16):
        pair = packed[pl.ds(128 * b, 128), :].astype(f32)
        product = pair * ctx[pl.ds(128 * b, 128), :]
        for half in range(2):
            rows = pl.ds(256 * b + 128 * half, 128)
            grad = pair if half == 0 else pltpu.roll(pair, 64, 1)
            at = 64 * half
            tails = []
            for h in range(2):
                inside = (lane >= at + 32 * h) & (lane < at + 32 * h + 32)
                delta = jnp.sum(jnp.where(inside, product, 0.0), axis=1, keepdims=True)
                one, two, three = pieces_of(-jnp.broadcast_to(delta, (128, 128)))
                spot = 32 - 32 * h
                tails.append(jnp.where(lane == spot, one, jnp.where(lane == spot + 1, two, three)))
            do[0, rows, :] = jnp.where(
                lane < 32, grad, jnp.where(lane < 35, tails[0], 0.0)
            ).astype(bf16)
            do[1, rows, :] = jnp.where(
                lane < 3, tails[1], jnp.where((lane >= 32) & (lane < 64), grad, 0.0)
            ).astype(bf16)
    for copy in loads[1:]:
        copy.wait()

    def per_segment(s, _):
        q_start, q_end = bounds[s], bounds[s + 1]
        k_start, k_end = bounds[8 + s], bounds[9 + s]
        q_first = (q_start // 16) * 16
        k_first = (k_start // 16) * 16
        q_plan = plan(q_end - q_first, BACK_QUERY)

        def per_key(span, first_key, j, _):
            k_row = pl.multiple_of(first_key + j * span, 16)
            k_rows = pl.ds(k_row, span)
            lane = iota((span, 128), 1)
            at = iota((span, 128), 0) + k_row
            mine = (at >= k_start) & (at < k_end)
            here = pl.ds(0, span)
            for h in range(2):
                mask = mine & (lane >= 32 * h) & (lane < 32 * h + 32)
                kw[h, here, :] = jnp.where(mask, ka[h, k_rows, :].astype(f32), 0.0).astype(bf16)

            turned_sum[:, here] = jnp.zeros((128, span), f32)

            def per_query(size, first_row, i, _):
                q_rows = pl.ds(pl.multiple_of(first_row + i * size, 16), size)
                for h in range(2):
                    score = mm(qa[h, q_rows, :], ka[h, k_rows, :], NT)
                    prob = jnp.exp2(score)
                    prob_grad = mm(do[h, q_rows, :], va[h, k_rows, :], NT)
                    score_grad = (prob * prob_grad).astype(bf16)
                    dq[q_rows, :] += mm(score_grad, kw[h, here, :])
                    cols = slice(32 * h, 32 * h + 32)
                    turned_sum[32 * h : 32 * h + 32, here] += mm(qw[q_rows, cols], score_grad, TN)
                    turned_sum[64 + 32 * h : 96 + 32 * h, here] += mm(
                        do[h, q_rows, cols], prob.astype(bf16), TN
                    )
                return 0

            for size, offset, count in q_plan:
                lax.fori_loop(0, count, functools.partial(per_query, size, q_first + offset), 0)
            fresh = turned_sum[:, here].T
            dkv[k_rows, :] = dkv[k_rows, :] + jnp.where(mine, fresh, 0.0)
            return 0

        for span, offset, count in plan(k_end - k_first, BACK_KEY):
            lax.fori_loop(0, count, functools.partial(per_key, span, k_first + offset), 0)
        return 0

    lax.fori_loop(0, IMAGES, per_segment, 0)

    def emit(i, _):
        rows = pl.ds(pl.multiple_of(i * 256, 256), 256)
        gq[rows, :] = (dq[rows, :] * HEAD_DIM**-0.5).astype(bf16)
        start = bounds[16 + i]
        aligned = pl.multiple_of((start // 16) * 16, 16)
        places = jnp.concatenate([rank[2 * i], rank[2 * i + 1]], axis=1)
        hot = jnp.where(iota((272, 256), 0) + aligned == places, 1.0, 0.0).astype(bf16)
        piece = dkv[pl.ds(aligned, 272), :]
        scale = jnp.where(iota((272, 128), 1) < 64, HEAD_DIM**-0.5, 1.0)
        gkv[rows, :] = mm(hot, (piece * scale).astype(bf16), TN).astype(bf16)
        return 0

    def stores(i):
        rows = pl.ds(pl.multiple_of(i * 512, 512), 512)
        return (
            pltpu.make_async_copy(gq.at[rows], gq_hbm.at[rows], store_sem.at[0, i]),
            pltpu.make_async_copy(gkv.at[rows], gkv_hbm.at[rows], store_sem.at[1, i]),
        )

    def emit_two(i, _):
        twice(emit)(i, 0)
        for copy in stores(i):
            copy.start()
        return 0

    def settle(i, _):
        for copy in stores(i):
            copy.wait()
        return 0

    lax.fori_loop(0, 8, emit_two, 0)
    lax.fori_loop(0, 8, settle, 0)


def attend_backward(packed, ctx, qa, qw, ka, va, rank, bounds):
    return pl.pallas_call(
        attend_backward_kernel,
        out_shape=(
            jax.ShapeDtypeStruct((PACK_ROWS, 128), bf16),
            jax.ShapeDtypeStruct((PACK_ROWS, 128), bf16),
        ),
        in_specs=[VMEM_SPEC] + [ANY_SPEC] * 5 + [VMEM_SPEC, SMEM_SPEC],
        out_specs=[ANY_SPEC] * 2,
        scratch_shapes=[
            pltpu.VMEM((2048, 128), f32),
            pltpu.VMEM((2, SPAN, 128), bf16),
            pltpu.VMEM((SPAN, 128), bf16),
            pltpu.VMEM((2, SPAN, 128), bf16),
            pltpu.VMEM((2, SPAN, 128), bf16),
            pltpu.VMEM((2, SPAN, 128), bf16),
            pltpu.VMEM((2, BACK_KEY[0], 128), bf16),
            pltpu.VMEM((SPAN, 128), f32),
            pltpu.VMEM((SPAN, 128), f32),
            pltpu.VMEM((128, BACK_KEY[0]), f32),
            pltpu.VMEM((PACK_ROWS, 128), bf16),
            pltpu.VMEM((PACK_ROWS, 128), bf16),
            pltpu.SemaphoreType.DMA((5,)),
            pltpu.SemaphoreType.DMA((2, 8)),
        ],
        compiler_params=pltpu.CompilerParams(vmem_limit_bytes=LIMIT_BACKWARD),
        cost_estimate=pl.CostEstimate(
            flops=50 * 10**9, bytes_accessed=20 * 10**6, transcendentals=10**7
        ),
    )(packed, ctx, qa, qw, ka, va, rank, bounds)


STEP = 10


neg_fill = -1e30
norm_eps = 1e-05
beta_one = 0.5
beta_two = 0.5
adam_eps = 1e-08
decay_rate = 0.0001
step_rates = (0.06, 0.15, 0.06, 0.03, 0.1, 0.1, 0.1)


def product(left_side, right_side):
    return jnp.dot(left_side, right_side, preferred_element_type=jnp.float32)


def product_left(left_side, right_side):
    return lax.dot_general(
        left_side, right_side, (((0,), (0,)), ((), ())), preferred_element_type=jnp.float32
    )


def product_right(left_side, right_side):
    return lax.dot_general(
        left_side, right_side, (((1,), (1,)), ((), ())), preferred_element_type=jnp.float32
    )


def smooth_unit(values):
    return jax.nn.gelu(values, approximate=False)


def norm_forward(values, gain_row, shift_row):
    center = values - jnp.mean(values, axis=-1, keepdims=True)
    inverse = lax.rsqrt(jnp.mean(center * center, axis=-1, keepdims=True) + norm_eps)
    scaled = center * inverse
    return (scaled * gain_row + shift_row, scaled, inverse)


def norm_backward(upstream, scaled, inverse, gain_row):
    spread = upstream * gain_row
    centred = (
        spread
        - jnp.mean(spread, axis=-1, keepdims=True)
        - scaled * jnp.mean(spread * scaled, axis=-1, keepdims=True)
    )
    return (inverse * centred, jnp.sum(upstream * scaled, axis=0), jnp.sum(upstream, axis=0))


def summed(partial_value):
    return lax.psum(partial_value, "tensor")


def adamw(master, gradient, old_first, old_second, step_rate):
    momentum = beta_one * old_first + (1.0 - beta_one) * gradient
    variance = beta_two * old_second + (1.0 - beta_two) * gradient * gradient
    normal_step = (
        momentum / (1.0 - beta_one**STEP) / (jnp.sqrt(variance / (1.0 - beta_two**STEP)) + adam_eps)
    )
    return (master - step_rate * (normal_step + decay_rate * master), momentum, variance)


MESH = pl.DeviceIdType.MESH
SHARD_ROWS = 304
GROUPS = 16
CHUNK = 256
CHUNKS = 4
STEPS = 2
BLOCK = 1024 // STEPS
PAIRS = BLOCK // 2
OWN_ROWS = CHUNK * CHUNKS


def greet(peers):
    barrier = pltpu.get_barrier_semaphore()
    for peer in peers:
        pl.semaphore_signal(barrier, inc=1, device_id=peer, device_id_type=MESH)
    return lambda: pl.semaphore_wait(barrier, len(peers))


def remote(source, target, send_sem, recv_sem, peer):
    return pltpu.make_async_remote_copy(
        src_ref=source,
        dst_ref=target,
        send_sem=send_sem,
        recv_sem=recv_sem,
        device_id=peer,
        device_id_type=MESH,
    )


def gather_kernel(
    up_hbm, down_hbm, outer, vec, shift, inward, off,
    pack, w3, offs,
    up, down, local_sem, small, one, send_buf, recv_buf, send_sem, recv_sem,
):
    me = lax.axis_index("dp")
    peers = [lax.rem(me + k, 8) for k in range(1, 8)]
    ready = greet([{"dp": p} for p in peers])
    loads = [
        pltpu.make_async_copy(up_hbm, up, local_sem.at[16]),
        pltpu.make_async_copy(down_hbm, down, local_sem.at[17]),
    ]
    for copy in loads:
        copy.start()
    send_buf[...] = jnp.zeros((112, 128), bf16)
    for which in range(3):
        send_buf[32 * which : 32 * which + 32, 0:64] = inward[which].astype(bf16)
    small[...] = jnp.zeros((3, 16, 128), f32)
    small[0, 0:2, 0:8] = off[...]
    small[1, 0:6, 0:32] = vec[...]
    small[2, 6:7, 0:64] = shift[...]
    send_buf[96:112, :] = pltpu.roll(small[0], me * 8, 1).astype(bf16)
    recv_buf[me] = send_buf[...]
    ready()
    copies = []
    for k, peer in enumerate(peers):
        copy = remote(
            send_buf, recv_buf.at[me], send_sem.at[k], recv_sem.at[me], {"dp": peer}
        )
        copy.start()
        copies.append(copy)
    for copy in loads:
        copy.wait()
    for b in range(4):
        one[32 * b : 32 * b + 32, :] = up[:, 128 * b : 128 * b + 128].astype(bf16)
        one[128 + 32 * b : 160 + 32 * b, :] = down[:, 128 * b : 128 * b + 128].astype(bf16)
    one[256:304, :] = jnp.zeros((48, 128), bf16)
    one[256:288, 0:64] = outer[...].astype(bf16)
    placed = pltpu.roll(small[1], lax.rem(me, 4) * 32, 1)
    placed = placed + pltpu.roll(small[2], lax.rem(me, 2) * 64, 1)
    one[288:304, :] = placed.astype(bf16)
    spreads = [
        pltpu.make_async_copy(one, pack.at[j], local_sem.at[j]) for j in range(GROUPS)
    ]
    for copy in spreads:
        copy.start()
    for peer in peers:
        remote(
            send_buf, recv_buf.at[peer], send_sem.at[0], recv_sem.at[peer], {"dp": peer}
        ).wait_recv()
    total = jnp.zeros((16, 128), f32)
    for d in range(8):
        for which in range(3):
            w3[which, 32 * d : 32 * d + 32, :] = recv_buf[d, 32 * which : 32 * which + 32, :]
        total = total + recv_buf[d, 96:112, :].astype(f32)
    offs[...] = total[0:8]
    for copy in copies:
        copy.wait_send()
    for copy in spreads:
        copy.wait()


def gather_weights(upward, down_t, out_t, vectors, shifts, inward, offsets):
    return pl.pallas_call(
        gather_kernel,
        out_shape=(
            jax.ShapeDtypeStruct((GROUPS, SHARD_ROWS, 128), bf16),
            jax.ShapeDtypeStruct((3, 256, 128), bf16),
            jax.ShapeDtypeStruct((8, 128), f32),
        ),
        in_specs=[ANY_SPEC] * 2 + [VMEM_SPEC] * 5,
        out_specs=[ANY_SPEC] + [VMEM_SPEC] * 2,
        scratch_shapes=[
            pltpu.VMEM((32, 512), f32),
            pltpu.VMEM((32, 512), f32),
            pltpu.SemaphoreType.DMA((18,)),
            pltpu.VMEM((3, 16, 128), f32),
            pltpu.VMEM((SHARD_ROWS, 128), bf16),
            pltpu.VMEM((112, 128), bf16),
            pltpu.VMEM((8, 112, 128), bf16),
            pltpu.SemaphoreType.DMA((7,)),
            pltpu.SemaphoreType.DMA((8,)),
        ],
        compiler_params=pltpu.CompilerParams(
            collective_id=0, has_side_effects=True, vmem_limit_bytes=LIMIT_GATHER
        ),
    )(upward, down_t, out_t, vectors, shifts, inward, offsets)


def norm_rows(values):
    center = values - jnp.mean(values, axis=1, keepdims=True)
    inverse = lax.rsqrt(jnp.mean(center * center, axis=1, keepdims=True) + norm_eps)
    return center * inverse, inverse


def norm_rows_back(spread, scaled, inverse):
    return inverse * (
        spread
        - jnp.mean(spread, axis=1, keepdims=True)
        - scaled * jnp.mean(spread * scaled, axis=1, keepdims=True)
    )


def dense_kernel(
    ctxp_hbm, half_hbm, tok_hbm, cot_hbm,
    encoded, dctx, first_hbm, gout,
    ctxp, half, first, enc, stage, other, ctxs, up, down, out_a, out_b, vec, shift,
    tok, cot, grads_ctx, normed_low, second_low, first_a, first_b,
    active, hgrad, slope, sums, give, take, keep,
    w_sem, load_sem, ctx_send, ctx_recv, dctx_send, dctx_recv,
    local_sem, enc_sem, first_sem, g_sem,
):
    me = lax.axis_index("tensor")
    core = lax.rem(me, 2)
    sibling = me + 1 - 2 * core
    across = lax.rem(me + 2, 4)
    diagonal = lax.rem(sibling + 2, 4)
    order = (sibling, across, diagonal)
    ready = greet([{"tensor": p} for p in order])
    own = pl.multiple_of(me * OWN_ROWS, OWN_ROWS)
    load_tok = pltpu.make_async_copy(tok_hbm.at[pl.ds(own, OWN_ROWS)], tok, load_sem.at[0])
    load_cot = pltpu.make_async_copy(cot_hbm.at[pl.ds(own, OWN_ROWS)], cot, load_sem.at[1])
    load_half = pltpu.make_async_copy(half_hbm, half, load_sem.at[2])
    load_ctxp = pltpu.make_async_copy(ctxp_hbm, ctxp, load_sem.at[3])
    load_ctxp.start()
    load_half.start()
    load_tok.start()
    load_cot.start()
    load_ctxp.wait()
    ctxs[me] = ctxp[pl.ds(pl.multiple_of(me * 512, 512), 512), :]
    sums[...] = jnp.zeros((8, 256), f32)
    ready()
    weights = [
        remote(
            half.at[:, pl.ds(256, 48)], other.at[:, pl.ds(256, 48)],
            w_sem.at[0], w_sem.at[1], {"tensor": sibling},
        ),
        remote(
            half.at[:, pl.ds(0, 256)], other.at[:, pl.ds(0, 256)],
            w_sem.at[2], w_sem.at[3], {"tensor": sibling},
        ),
    ]

    def ctx_copy(peer, c):
        rows = pl.ds(pl.multiple_of(peer * 512 + c * PAIRS, PAIRS), PAIRS)
        return remote(
            ctxp.at[rows], ctxs.at[me, pl.ds(pl.multiple_of(c * PAIRS, PAIRS), PAIRS)],
            ctx_send.at[peer, c], ctx_recv.at[me, c], {"tensor": peer},
        )

    def ctx_arrival(peer, c):
        rows = pl.ds(pl.multiple_of(c * PAIRS, PAIRS), PAIRS)
        return remote(
            ctxp.at[rows], ctxs.at[peer, rows],
            ctx_send.at[peer, c], ctx_recv.at[peer, c], {"tensor": peer},
        )

    for peer in (across, diagonal, sibling):
        ctx_copy(peer, 0).start()
    load_half.wait()
    weights[0].start()
    weights[1].start()
    for c in range(1, STEPS):
        for peer in (across, diagonal, sibling):
            ctx_copy(peer, c).start()

    out_a[...] = jnp.zeros((256, 512), bf16)
    out_b[...] = jnp.zeros((256, 512), bf16)

    def unpack_small(source, t_of):
        for ty in range(2):
            t = t_of(ty)
            lanes = pl.ds(pl.multiple_of(t * 128, 128), 128)
            for d in range(8):
                piece = source[8 * ty + d, 256:288, :].astype(f32)
                out_a[32 * d : 32 * d + 32, lanes] = piece.astype(bf16)
                out_b[32 * d : 32 * d + 32, lanes] = pltpu.roll(piece, 64, 1).astype(bf16)
            for b in range(4):
                both = source[8 * ty + 2 * b, 288:304, :] + source[8 * ty + 2 * b + 1, 288:304, :]
                shift[:, pl.ds(pl.multiple_of(t * 512 + 128 * b, 128), 128)] = (
                    both.astype(f32)[6:7]
                )

    def unpack_large(source, t_of):
        for ty in range(2):
            t = t_of(ty)

            def one_row(d, _):
                rows = pl.ds(pl.multiple_of(d * 32, 32), 32)
                for b in range(4):
                    lanes = pl.ds(pl.multiple_of(t * 512 + 128 * b, 128), 128)
                    up[rows, lanes] = source[8 * ty + d, 32 * b : 32 * b + 32, :]
                    down[rows, lanes] = source[8 * ty + d, 128 + 32 * b : 160 + 32 * b, :]
                return 0

            lax.fori_loop(0, 8, one_row, 0)

    mine_t = lambda ty: 2 * ty + core
    other_t = lambda ty: 2 * ty + 1 - core
    for b in range(2):
        total = jnp.zeros((16, 128), f32)
        for d in range(4 * b, 4 * b + 4):
            total = total + half[d, 288:304, :].astype(f32)
        vec[:, 128 * b : 128 * b + 128] = total[0:8]
    unpack_small(half, mine_t)
    unpack_large(half, mine_t)
    weights[0].wait_recv()
    unpack_small(other, other_t)
    weights[1].wait_recv()
    unpack_large(other, other_t)
    load_tok.wait()
    load_cot.wait()

    def enc_store(c):
        rows = pl.ds(pl.multiple_of(c * BLOCK, BLOCK), BLOCK)
        return pltpu.make_async_copy(enc.at[rows], encoded.at[rows], enc_sem.at[c])

    def first_store(c):
        rows = pl.ds(pl.multiple_of(c * BLOCK, BLOCK), BLOCK)
        return pltpu.make_async_copy(first.at[rows], first_hbm.at[rows], first_sem.at[c])

    def dctx_copy(peer, c):
        rows = pl.ds(pl.multiple_of(c * PAIRS, PAIRS), PAIRS)
        return remote(
            grads_ctx.at[peer, rows],
            dctx.at[pl.ds(pl.multiple_of(me * 512 + c * PAIRS, PAIRS), PAIRS)],
            dctx_send.at[peer, c], dctx_recv.at[me, c], {"tensor": peer},
        )

    def dctx_arrival(peer, c):
        rows = pl.ds(pl.multiple_of(c * PAIRS, PAIRS), PAIRS)
        return remote(
            grads_ctx.at[peer, rows],
            dctx.at[pl.ds(pl.multiple_of(peer * 512 + c * PAIRS, PAIRS), PAIRS)],
            dctx_send.at[peer, c], dctx_recv.at[peer, c], {"tensor": peer},
        )

    def dctx_local(c):
        rows = pl.ds(pl.multiple_of(c * PAIRS, PAIRS), PAIRS)
        return pltpu.make_async_copy(
            grads_ctx.at[me, rows],
            dctx.at[pl.ds(pl.multiple_of(me * 512 + c * PAIRS, PAIRS), PAIRS)],
            local_sem.at[c],
        )

    def chunk_step(c, _):
        for peer in order:
            ctx_arrival(peer, c).wait_recv()
        rows = pl.ds(pl.multiple_of(c * BLOCK, BLOCK), BLOCK)
        pair_rows = pl.ds(pl.multiple_of(c * PAIRS, PAIRS), PAIRS)
        context = jnp.concatenate([ctxs[t, pair_rows, :] for t in range(4)], axis=1)
        upper, lower = mm(context, out_a[...], NT), mm(context, out_b[...], NT)
        attended = jnp.concatenate(
            [half_of[g : g + 128] for g in range(0, PAIRS, 128) for half_of in (upper, lower)],
            axis=0,
        )
        first_sum = tok[rows, :].astype(f32) + attended + vec[4:5]
        scaled_one, inverse_one = norm_rows(first_sum)
        normed = scaled_one * vec[0:1] + vec[1:2]
        low = normed.astype(bf16)
        normed_low[rows, :] = low
        for n in range(4):
            span = slice(512 * n, 512 * n + 512)
            hidden = mm(low, up[:, span]) + shift[:, span]
            cumulative = 0.5 * (1.0 + lax.erf(hidden * 0.7071067811865476))
            active[rows, span] = (hidden * cumulative).astype(bf16)
            slope[:, span] = cumulative + hidden * (
                0.3989422804014327 * jnp.exp(-0.5 * hidden * hidden)
            )
        second_sum = normed + mm(active[rows, :], down[...], NT) + vec[5:6]
        scaled_two, inverse_two = norm_rows(second_sum)
        enc[rows, :] = (scaled_two * vec[2:3] + vec[3:4]).astype(bf16)
        enc_store(c).start()
        upstream = cot[rows, :].astype(f32)
        second_grad = norm_rows_back(upstream * vec[2:3], scaled_two, inverse_two)
        low_two = second_grad.astype(bf16)
        second_low[rows, :] = low_two
        for n in range(4):
            span = slice(512 * n, 512 * n + 512)
            hgrad[rows, span] = (mm(low_two, down[:, span]) * slope[:, span]).astype(bf16)
        normed_grad = second_grad + mm(hgrad[rows, :], up[...], NT)
        first_grad = norm_rows_back(normed_grad * vec[0:1], scaled_one, inverse_one)
        first[rows, :] = first_grad
        first_store(c).start()
        low_one = first_grad.astype(bf16)
        parts = [
            jnp.concatenate([low_one[g + at : g + at + 128] for g in range(0, BLOCK, 256)], axis=0)
            for at in (0, 128)
        ]
        first_a[pair_rows, :] = parts[0]
        first_b[pair_rows, :] = parts[1]
        back = (mm(parts[0], out_a[...]) + mm(parts[1], out_b[...])).astype(bf16)
        for t in range(4):
            grads_ctx[t, pair_rows, :] = back[:, 128 * t : 128 * t + 128]
        for peer in (across, diagonal, sibling):
            dctx_copy(peer, c).start()
        dctx_local(c).start()
        fold = lambda value: jnp.sum(value, axis=0, keepdims=True)
        sums[0:1] += fold(normed_grad * scaled_one)
        sums[1:2] += fold(normed_grad)
        sums[2:3] += fold(upstream * scaled_two)
        sums[3:4] += fold(upstream)
        sums[4:5] += fold(first_grad)
        sums[5:6] += fold(second_grad)
        return 0

    lax.fori_loop(0, STEPS, chunk_step, 0)

    ones = jnp.ones((8, OWN_ROWS), bf16)

    def weight_grads(t, ty, target, kind):
        lanes = pl.ds(pl.multiple_of(t * 512, 512), 512)
        grad_up = mm(normed_low[...], hgrad[:, lanes], TN).astype(kind)
        grad_down = mm(second_low[...], active[:, lanes], TN).astype(kind)
        part_a = mm(first_a[...], ctxs[t], TN)
        part_b = pltpu.roll(mm(first_b[...], ctxs[t], TN), 64, 1)
        grad_out = jnp.where(iota((256, 128), 1) < 64, part_a + part_b, 0.0).astype(kind)
        shift_sum = mm(ones, hgrad[:, lanes])
        for d in range(8):
            j = 8 * ty + d
            block = slice(32 * d, 32 * d + 32)
            for b in range(4):
                cols = slice(128 * b, 128 * b + 128)
                target[j, 32 * b : 32 * b + 32, :] = grad_up[block, cols]
                target[j, 128 + 32 * b : 160 + 32 * b, :] = grad_down[block, cols]
            target[j, 256:288, :] = grad_out[block]
            vector = sums[:, 128 * (d // 4) : 128 * (d // 4) + 128]
            cols = slice(128 * (d // 2), 128 * (d // 2) + 128)
            last = jnp.where(iota((8, 128), 0) == 6, shift_sum[:, cols], vector)
            target[j, 288:304, :] = jnp.concatenate(
                [last, jnp.zeros((8, 128), f32)], axis=0
            ).astype(kind)

    def trade(ty):
        slots = pl.ds(8 * ty, 8)
        return remote(give.at[slots], take.at[slots], g_sem.at[ty], g_sem.at[2 + ty],
                      {"tensor": sibling})

    def weight_store(ty):
        slots = pl.ds(8 * ty, 8)
        return pltpu.make_async_copy(stage.at[slots], gout.at[slots], g_sem.at[4 + ty])

    for ty in range(2):
        weight_grads(other_t(ty), ty, give, bf16)
        trade(ty).start()
    for ty in range(2):
        weight_grads(mine_t(ty), ty, keep, f32)
    for ty in range(2):
        trade(ty).wait_recv()
        slots = slice(8 * ty, 8 * ty + 8)
        stage[slots] = (keep[slots] + take[slots].astype(f32)).astype(bf16)
        weight_store(ty).start()

    for copy in weights:
        copy.wait_send()
    for c in range(STEPS):
        for peer in order:
            ctx_copy(peer, c).wait_send()
            dctx_copy(peer, c).wait_send()
            dctx_arrival(peer, c).wait_recv()
        dctx_local(c).wait()
        enc_store(c).wait()
        first_store(c).wait()
    for ty in range(2):
        trade(ty).wait_send()
        weight_store(ty).wait()


def dense(ctxp, half, tokens, cotangent):
    dma = pltpu.SemaphoreType.DMA
    return pl.pallas_call(
        dense_kernel,
        out_shape=(
            jax.ShapeDtypeStruct((OWN_ROWS, 256), bf16),
            jax.ShapeDtypeStruct((PACK_ROWS // 2, 128), bf16),
            jax.ShapeDtypeStruct((OWN_ROWS, 256), f32),
            jax.ShapeDtypeStruct((GROUPS, SHARD_ROWS, 128), bf16),
        ),
        in_specs=[ANY_SPEC] * 4,
        out_specs=[ANY_SPEC] * 4,
        scratch_shapes=[
            pltpu.VMEM((PACK_ROWS // 2, 128), bf16),
            pltpu.VMEM((GROUPS, SHARD_ROWS, 128), bf16),
            pltpu.VMEM((OWN_ROWS, 256), f32),
            pltpu.VMEM((OWN_ROWS, 256), bf16),
            pltpu.VMEM((GROUPS, SHARD_ROWS, 128), bf16),
            pltpu.VMEM((GROUPS, SHARD_ROWS, 128), bf16),
            pltpu.VMEM((4, 512, 128), bf16),
            pltpu.VMEM((256, 2048), bf16),
            pltpu.VMEM((256, 2048), bf16),
            pltpu.VMEM((256, 512), bf16),
            pltpu.VMEM((256, 512), bf16),
            pltpu.VMEM((8, 256), f32),
            pltpu.VMEM((1, 2048), f32),
            pltpu.VMEM((OWN_ROWS, 256), bf16),
            pltpu.VMEM((OWN_ROWS, 256), bf16),
            pltpu.VMEM((4, 512, 128), bf16),
            pltpu.VMEM((OWN_ROWS, 256), bf16),
            pltpu.VMEM((OWN_ROWS, 256), bf16),
            pltpu.VMEM((512, 256), bf16),
            pltpu.VMEM((512, 256), bf16),
            pltpu.VMEM((OWN_ROWS, 2048), bf16),
            pltpu.VMEM((OWN_ROWS, 2048), bf16),
            pltpu.VMEM((BLOCK, 2048), f32),
            pltpu.VMEM((8, 256), f32),
            pltpu.VMEM((GROUPS, SHARD_ROWS, 128), bf16),
            pltpu.VMEM((GROUPS, SHARD_ROWS, 128), bf16),
            pltpu.VMEM((GROUPS, SHARD_ROWS, 128), f32),
            dma((4,)),
            dma((4,)),
            dma((4, STEPS)),
            dma((4, STEPS)),
            dma((4, STEPS)),
            dma((4, STEPS)),
            dma((STEPS,)),
            dma((STEPS,)),
            dma((STEPS,)),
            dma((6,)),
        ],
        compiler_params=pltpu.CompilerParams(
            collective_id=1, has_side_effects=True, vmem_limit_bytes=LIMIT_DENSE
        ),
        cost_estimate=pl.CostEstimate(
            flops=7 * 10**9, bytes_accessed=8 * 10**6, transcendentals=4 * 10**6
        ),
    )(ctxp, half, tokens, cotangent)


def tail_kernel(
    gq_hbm, gkv_hbm, tok_hbm, pos_hbm, w3, first_hbm,
    tg, gin,
    gq, gkv, tok, pos, first, load_sem,
    wall, near_send, near_recv, far_send, far_recv, mine, in_send, in_recv,
    n_send, n_recv, f_send, f_recv, t_send, t_recv, i_send, i_recv, local_sem,
):
    me = lax.axis_index("tensor")
    rank = lax.axis_index("dp")
    core = lax.rem(me, 2)
    sibling = me + 1 - 2 * core
    across = lax.rem(me + 2, 4)
    diagonal = lax.rem(sibling + 2, 4)
    peers = [lax.rem(rank + k, 8) for k in range(1, 8)]
    ready = greet(
        [{"tensor": sibling}, {"tensor": across}] + [{"dp": peer} for peer in peers]
    )
    loads = [
        pltpu.make_async_copy(source, target, load_sem.at[n])
        for n, (source, target) in enumerate(
            ((gq_hbm, gq), (gkv_hbm, gkv), (first_hbm, first), (tok_hbm, tok), (pos_hbm, pos))
        )
    ]
    for copy in loads:
        copy.start()
    lane = iota((256, 128), 1)
    wall[:, 0:128] = w3[0]
    wall[:, 128:256] = jnp.where(
        lane < 64, w3[1].astype(f32), pltpu.roll(w3[2].astype(f32), 64, 1)
    ).astype(bf16)

    def rows_of(even, odd, i):
        owner = jnp.where(lax.rem(i, 2) == 0, even, odd)
        return pl.ds(pl.multiple_of(owner * OWN_ROWS + (i // 2) * CHUNK, CHUNK), CHUNK)

    def slot(i):
        return pl.ds(pl.multiple_of(i * CHUNK, CHUNK), CHUNK)

    def partial(rows):
        return mm(jnp.concatenate([gq[rows, :], gkv[rows, :]], axis=1), wall[...], NT)

    def near_copy(i):
        return remote(near_send.at[slot(i)], near_recv.at[slot(i)],
                      n_send.at[i], n_recv.at[i], {"tensor": sibling})

    def far_copy(i):
        theirs = i + 1 - 2 * lax.rem(i, 2)
        return remote(far_send.at[slot(i)], far_recv.at[slot(theirs)],
                      f_send.at[i], f_recv.at[theirs], {"tensor": across})

    def far_arrival(i):
        return remote(far_send.at[slot(i)], far_recv.at[slot(i)],
                      f_send.at[i], f_recv.at[i], {"tensor": across})

    def share_copy(i):
        return remote(mine.at[slot(i)], tg.at[rows_of(across, me, i)],
                      t_send.at[i], t_recv.at[i], {"tensor": sibling})

    def share_arrival(i):
        return remote(mine.at[slot(i)], tg.at[rows_of(diagonal, sibling, i)],
                      t_send.at[i], t_recv.at[i], {"tensor": sibling})

    def keep_copy(i):
        return pltpu.make_async_copy(
            mine.at[slot(i)], tg.at[rows_of(across, me, i)], local_sem.at[i]
        )

    def first_stage(i, _):
        near_send[slot(i), :] = partial(rows_of(diagonal, sibling, i)).astype(bf16)
        near_copy(i).start()
        return 0

    def second_stage(i, _):
        value = partial(rows_of(across, me, i))
        odd = lax.rem(i, 2).astype(f32)
        half = pl.ds(pl.multiple_of((i // 2) * CHUNK, CHUNK), CHUNK)
        value = value + first[half, :] * odd
        near_copy(i).wait_recv()
        far_send[slot(i), :] = (value + near_recv[slot(i), :].astype(f32)).astype(bf16)
        far_copy(i).start()
        return 0

    loads[0].wait()
    loads[1].wait()
    ready()
    lax.fori_loop(0, 2, first_stage, 0)
    loads[2].wait()

    def both_stages(i, _):
        first_stage(i + 2, 0)
        second_stage(i, 0)
        return 0

    lax.fori_loop(0, 6, both_stages, 0)
    lax.fori_loop(6, 8, second_stage, 0)

    loads[3].wait()
    loads[4].wait()

    def inward_step(i, carry):
        left, right, total = carry
        rows = pl.ds(pl.multiple_of(i * 1024, 1024), 1024)
        token = tok[rows, :]
        query_in = (token.astype(f32) + pos[rows, :].astype(f32)).astype(bf16)
        both = jnp.concatenate([gq[rows, :], gkv[rows, :]], axis=1)
        left = left + mm(query_in, both, TN)
        right = right + mm(token, gkv[rows, :], TN)
        total = total + mm(jnp.ones((8, 1024), bf16), both)
        return left, right, total

    left, right, total = lax.fori_loop(
        0, 4, inward_step,
        (jnp.zeros((256, 256), f32), jnp.zeros((256, 128), f32), jnp.zeros((8, 256), f32)),
    )
    joined = jnp.concatenate([jnp.where(lane < 64, left[:, 0:128], right), left[:, 128:256]], 1)
    for d in range(8):
        in_send[d, 0:32, :] = joined[32 * d : 32 * d + 32]
        in_send[d, 32:40, :] = total
    in_copies = []
    for k, peer in enumerate(peers):
        copy = remote(
            in_send.at[peer], in_recv.at[rank], i_send.at[k], i_recv.at[rank], {"dp": peer}
        )
        copy.start()
        in_copies.append(copy)

    def third_stage(i, _):
        far_arrival(i).wait_recv()
        mine[slot(i), :] = (
            far_send[slot(i), :].astype(f32) + far_recv[slot(i), :].astype(f32)
        ).astype(bf16)
        share_copy(i).start()
        keep_copy(i).start()
        return 0

    def third_pair(i, _):
        third_stage(2 * i + 1, 0)
        third_stage(2 * i, 0)
        return 0

    lax.fori_loop(0, 4, third_pair, 0)

    gathered = in_send[rank]
    for peer in peers:
        remote(
            in_send.at[peer], in_recv.at[peer], i_send.at[0], i_recv.at[peer], {"dp": peer}
        ).wait_recv()
        gathered = gathered + in_recv[peer]
    gin[...] = gathered

    for copy in in_copies:
        copy.wait_send()

    def finish(i, _):
        near_copy(i).wait_send()
        far_copy(i).wait_send()
        share_copy(i).wait_send()
        keep_copy(i).wait()
        share_arrival(i).wait_recv()
        return 0

    lax.fori_loop(0, 8, finish, 0)


def tail(gq, gkv, tokens, positions, w3, first):
    dma = pltpu.SemaphoreType.DMA
    return pl.pallas_call(
        tail_kernel,
        out_shape=(
            jax.ShapeDtypeStruct((PACK_ROWS, 256), bf16),
            jax.ShapeDtypeStruct((40, 256), f32),
        ),
        in_specs=[ANY_SPEC] * 4 + [VMEM_SPEC, ANY_SPEC],
        out_specs=[ANY_SPEC, VMEM_SPEC],
        scratch_shapes=[
            pltpu.VMEM((PACK_ROWS, 128), bf16),
            pltpu.VMEM((PACK_ROWS, 128), bf16),
            pltpu.VMEM((PACK_ROWS, 256), bf16),
            pltpu.VMEM((PACK_ROWS, 256), bf16),
            pltpu.VMEM((OWN_ROWS, 256), f32),
            dma((5,)),
            pltpu.VMEM((256, 256), bf16),
        ]
        + [pltpu.VMEM((8 * CHUNK, 256), bf16)] * 5
        + [
            pltpu.VMEM((8, 40, 256), f32),
            pltpu.VMEM((8, 40, 256), f32),
            dma((8,)),
            dma((8,)),
            dma((8,)),
            dma((8,)),
            dma((8,)),
            dma((8,)),
            dma((7,)),
            dma((8,)),
            dma((8,)),
        ],
        compiler_params=pltpu.CompilerParams(
            collective_id=2, has_side_effects=True, vmem_limit_bytes=LIMIT_TAIL
        ),
        cost_estimate=pl.CostEstimate(
            flops=3 * 10**9, bytes_accessed=16 * 10**6, transcendentals=0
        ),
    )(gq, gkv, tokens, positions, w3, first)


def update_kernel(pieces, gin, narrow, *refs):
    blocks, refs = refs[0:4], refs[4:]
    masters, firsts, seconds = refs[0:7], refs[7:14], refs[14:21]
    wide_out, encoded = refs[21:23]
    grads, news, lows, moms, varis = (
        refs[23:30], refs[30:37], refs[37:41], refs[41:48], refs[48:55],
    )
    stage, sem = refs[55:57]
    me = lax.axis_index("dp")
    copies = []
    col = lax.axis_index("tensor")
    low, high = lax.rem(col, 2), col // 2
    owners = (col, 2 * high + 1 - low, 2 * (1 - high) + low, 2 * (1 - high) + 1 - low)
    for i in range(4):
        rows = pl.ds(pl.multiple_of(owners[i] * OWN_ROWS, OWN_ROWS), OWN_ROWS)
        copy = pltpu.make_async_copy(blocks[i], encoded.at[rows], sem.at[8 + i])
        copy.start()
        copies.append(copy)
    for i in range(8):
        rows = pl.ds(512 * i, 512)
        stage[rows, :] = narrow[rows, :].astype(f32)
        copy = pltpu.make_async_copy(stage.at[rows], wide_out.at[rows], sem.at[i])
        copy.start()
        copies.append(copy)

    def add(j, total):
        return total + pieces[j].astype(f32)

    total = lax.fori_loop(0, GROUPS, add, jnp.zeros((SHARD_ROWS, 128), f32))
    wide = gin[...]
    small = total[288:296]
    vec_grad = pltpu.roll(small, lax.rem(128 - lax.rem(me, 4) * 32, 128), 1)[0:6, 0:32]
    shift_grad = pltpu.roll(small, lax.rem(128 - lax.rem(me, 2) * 64, 128), 1)[6:7, 0:64]
    off_q = pltpu.roll(wide[32:40, 0:128], lax.rem(128 - me * 8, 128), 1)
    off_v = pltpu.roll(wide[32:40, 128:256], 64 - me * 8, 1)
    off_grad = jnp.where(iota((8, 128), 0) == 0, off_q, off_v)[0:2, 0:8]
    left, right = wide[0:32, 0:128], wide[0:32, 128:256]
    inward_grads = (left[:, 0:64], right[:, 0:64], pltpu.roll(left, 64, 1)[:, 0:64])
    joined = lambda base: jnp.concatenate(
        [total[base + 32 * b : base + 32 * b + 32] for b in range(4)], axis=1
    )
    plain = (None, total[256:288, 0:64], joined(0), joined(128), vec_grad, off_grad, shift_grad)

    def apply(index, at, gradient):
        new, momentum, variance = adamw(
            masters[index][at], gradient, firsts[index][at], seconds[index][at],
            step_rates[index],
        )
        grads[index][at] = gradient
        news[index][at] = new
        moms[index][at] = momentum
        varis[index][at] = variance
        if index < 4:
            lows[index][at] = new.astype(bf16)

    for which in range(3):
        apply(0, which, inward_grads[which])
    for index in range(1, 7):
        apply(index, Ellipsis, plain[index])
    for copy in copies:
        copy.wait()


def update(pieces, gin, narrow, blocks, masters, firsts, seconds):
    shapes = [m.shape for m in masters]
    of = lambda kind, count: [jax.ShapeDtypeStruct(s, kind) for s in shapes[:count]]
    out = [
        jax.ShapeDtypeStruct((PACK_ROWS, 256), f32),
        jax.ShapeDtypeStruct((PACK_ROWS, 256), bf16),
    ]
    out = out + of(f32, 7) + of(f32, 7) + of(bf16, 4) + of(f32, 7) + of(f32, 7)
    return pl.pallas_call(
        update_kernel,
        out_shape=out,
        in_specs=[VMEM_SPEC] * 28,
        out_specs=[ANY_SPEC] * 2 + [VMEM_SPEC] * (len(out) - 2),
        scratch_shapes=[pltpu.VMEM((PACK_ROWS, 256), f32), pltpu.SemaphoreType.DMA((12,))],
        compiler_params=pltpu.CompilerParams(vmem_limit_bytes=LIMIT_UPDATE),
    )(pieces, gin, narrow, *blocks, *masters, *firsts, *seconds)


def exchange(pieces):
    groups = [[4 * d + 2 * y + c for y in range(2) for d in range(8)] for c in range(2)]
    return lax.all_to_all(
        pieces, ("dp", "tensor"), 0, 0, axis_index_groups=groups, tiled=True
    )


def turned(group):
    inward, outward, upward, downward, vectors, offsets, shifts = group
    return [inward, outward.T, upward, downward.T, vectors, offsets, shifts.reshape(1, -1)]


def returned(group):
    if len(group) == 4:
        return [group[0], group[1].T, group[2], group[3].T]
    inward, outward, upward, downward, vectors, offsets, shifts = group
    return [inward, outward.T, upward, downward.T, vectors, offsets, shifts.reshape(-1)]


def body_pods(tokens, positions, segment_ids, pad_flags, cotangent, *state):
    masters, firsts, seconds = (turned(state[7 * i : 7 * i + 7]) for i in range(3))
    inward, out_t, upward, down_t, vectors, offsets, shifts = masters
    pack, w3, off = gather_weights(upward, down_t, out_t, vectors, shifts, inward, offsets)
    half = exchange(pack)
    ctxp, *saved = attend_forward(tokens, positions, w3, off, segment_ids, pad_flags)
    own, dctx, first, gout = dense(ctxp, half, tokens, cotangent)
    blocks = [own] + [
        lax.ppermute(own, "tensor", [(t, t ^ flip) for t in range(4)]) for flip in (1, 2, 3)
    ]
    pieces = exchange(gout)
    gq, gkv = attend_backward(dctx, *saved)
    narrow, gin = tail(gq, gkv, tokens, positions, w3, first)
    token_grad, encoded, *outs = update(pieces, gin, narrow, blocks, masters, firsts, seconds)
    grads, news, lows, moms, varis = outs[:7], outs[7:14], outs[14:18], outs[18:25], outs[25:]
    return (
        encoded,
        token_grad,
        *returned(grads),
        *returned(news),
        *returned(lows),
        *returned(moms),
        *returned(varis),
    )


def body(
    tokens,
    positions,
    segment_ids,
    pad_flags,
    cotangent,
    inward,
    outward,
    upward,
    downward,
    vectors,
    offsets,
    shifts,
    first_inward,
    first_outward,
    first_upward,
    first_downward,
    first_vectors,
    first_offsets,
    first_shifts,
    second_inward,
    second_outward,
    second_upward,
    second_downward,
    second_vectors,
    second_offsets,
    second_shifts,
):
    w_inward, w_outward, w_upward, w_downward, vector_low, offset_low, shift_low = (
        lax.all_gather(inward.astype(jnp.bfloat16), "dp", axis=1, tiled=True),
        lax.all_gather(outward.astype(jnp.bfloat16), "dp", axis=1, tiled=True),
        lax.all_gather(upward.astype(jnp.bfloat16), "dp", axis=0, tiled=True),
        lax.all_gather(downward.astype(jnp.bfloat16), "dp", axis=1, tiled=True),
        lax.all_gather(vectors.astype(jnp.bfloat16), "dp", axis=1, tiled=True),
        lax.all_gather(offsets.astype(jnp.bfloat16), "dp", axis=1, tiled=True),
        lax.all_gather(shifts.astype(jnp.bfloat16), "dp", axis=0, tiled=True),
    )
    vector_wide = vector_low.astype(jnp.float32)
    offset_wide = offset_low.astype(jnp.float32)
    shift_wide = shift_low.astype(jnp.float32)
    input_wide = tokens.astype(jnp.float32)
    query_in = (input_wide + positions.astype(jnp.float32)).astype(jnp.bfloat16)
    w_lanes = jnp.pad(w_inward, ((0, 0), (0, 0), (0, 64)))
    off_lanes = jnp.pad(offset_wide, ((0, 6), (0, 64)))
    packed, *saved = attend_forward(
        tokens, positions, w_lanes, off_lanes, segment_ids, pad_flags
    )
    pairs = packed.reshape(16, 128, 2, 64)
    context_low = pairs.transpose(0, 2, 1, 3).reshape(PACK_ROWS, 64)
    first_sum = input_wide + summed(product(context_low, w_outward)) + vector_wide[4]
    normed, scaled_one, inverse_one = norm_forward(first_sum, vector_wide[0], vector_wide[1])
    normed_low = normed.astype(jnp.bfloat16)
    hidden = product(normed_low, w_upward) + shift_wide
    unit_value, unit_back = jax.vjp(smooth_unit, hidden)
    active = unit_value.astype(jnp.bfloat16)
    second_sum = normed + summed(product(active, w_downward)) + vector_wide[5]
    result, scaled_two, inverse_two = norm_forward(second_sum, vector_wide[2], vector_wide[3])
    encoded = result.astype(jnp.bfloat16)
    upstream = cotangent.astype(jnp.float32)
    second_grad, gain_two, shift_two = norm_backward(
        upstream, scaled_two, inverse_two, vector_wide[2]
    )
    down_low = second_grad.astype(jnp.bfloat16)
    grad_downward = product_left(active, down_low)
    hidden_low = unit_back(product_right(down_low, w_downward))[0].astype(jnp.bfloat16)
    grad_upward = product_left(normed_low, hidden_low)
    grad_shifts = jnp.sum(hidden_low.astype(jnp.float32), axis=0)
    normed_grad = second_grad + summed(product_right(hidden_low, w_upward))
    first_grad, gain_one, shift_one = norm_backward(
        normed_grad, scaled_one, inverse_one, vector_wide[0]
    )
    first_low = first_grad.astype(jnp.bfloat16)
    grad_outward = product_left(context_low, first_low)
    context_grad = product_right(first_low, w_outward).astype(jnp.bfloat16)
    halves = context_grad.reshape(16, 2, 128, 64)
    gq, gkv = attend_backward(
        halves.transpose(0, 2, 1, 3).reshape(2048, 128), *saved
    )
    query_grad, key_grad, value_grad = gq[:, :64], gkv[:, :64], gkv[:, 64:]
    grad_inward = jnp.stack(
        [
            product_left(query_in, query_grad),
            product_left(query_in, key_grad),
            product_left(tokens, value_grad),
        ]
    )
    grad_offsets = jnp.stack(
        [
            jnp.sum(query_grad.astype(jnp.float32), axis=0),
            jnp.sum(value_grad.astype(jnp.float32), axis=0),
        ]
    )
    input_part = (
        product_right(query_grad, w_inward[0])
        + product_right(key_grad, w_inward[1])
        + product_right(value_grad, w_inward[2])
    )
    input_grad = first_grad + summed(input_part)
    grad_vectors = jnp.stack(
        [
            gain_one,
            shift_one,
            gain_two,
            shift_two,
            jnp.sum(first_grad, axis=0),
            jnp.sum(second_grad, axis=0),
        ]
    )
    reduced = (
        lax.psum_scatter(grad_inward, "dp", scatter_dimension=1, tiled=True),
        lax.psum_scatter(grad_outward, "dp", scatter_dimension=1, tiled=True),
        lax.psum_scatter(grad_upward, "dp", scatter_dimension=0, tiled=True),
        lax.psum_scatter(grad_downward, "dp", scatter_dimension=1, tiled=True),
        lax.psum_scatter(grad_vectors, "dp", scatter_dimension=1, tiled=True),
        lax.psum_scatter(grad_offsets, "dp", scatter_dimension=1, tiled=True),
        lax.psum_scatter(grad_shifts, "dp", scatter_dimension=0, tiled=True),
    )
    masters = (inward, outward, upward, downward, vectors, offsets, shifts)
    firsts = (
        first_inward,
        first_outward,
        first_upward,
        first_downward,
        first_vectors,
        first_offsets,
        first_shifts,
    )
    seconds = (
        second_inward,
        second_outward,
        second_upward,
        second_downward,
        second_vectors,
        second_offsets,
        second_shifts,
    )
    updated = []
    momenta = []
    variances = []
    for master, gradient, old_first, old_second, step_rate in zip(
        masters, reduced, firsts, seconds, step_rates
    ):
        new_master, momentum, variance = adamw(master, gradient, old_first, old_second, step_rate)
        updated.append(new_master)
        momenta.append(momentum)
        variances.append(variance)
    return (
        encoded,
        input_grad,
        reduced[0],
        reduced[1],
        reduced[2],
        reduced[3],
        reduced[4],
        reduced[5],
        reduced[6],
        updated[0],
        updated[1],
        updated[2],
        updated[3],
        updated[4],
        updated[5],
        updated[6],
        updated[0].astype(jnp.bfloat16),
        updated[1].astype(jnp.bfloat16),
        updated[2].astype(jnp.bfloat16),
        updated[3].astype(jnp.bfloat16),
        momenta[0],
        momenta[1],
        momenta[2],
        momenta[3],
        momenta[4],
        momenta[5],
        momenta[6],
        variances[0],
        variances[1],
        variances[2],
        variances[3],
        variances[4],
        variances[5],
        variances[6],
    )


def solution(mesh):
    in_specs = (
        P("dp", None),
        P("dp", None),
        P("dp", None),
        P("dp", None),
        P("dp", None),
        P(None, "dp", "tensor"),
        P("tensor", "dp"),
        P("dp", "tensor"),
        P("tensor", "dp"),
        P(None, "dp"),
        P(None, ("tensor", "dp")),
        P(("tensor", "dp")),
        P(None, "dp", "tensor"),
        P("tensor", "dp"),
        P("dp", "tensor"),
        P("tensor", "dp"),
        P(None, "dp"),
        P(None, ("tensor", "dp")),
        P(("tensor", "dp")),
        P(None, "dp", "tensor"),
        P("tensor", "dp"),
        P("dp", "tensor"),
        P("tensor", "dp"),
        P(None, "dp"),
        P(None, ("tensor", "dp")),
        P(("tensor", "dp")),
    )
    out_specs = (
        P("dp", None),
        P("dp", None),
        P(None, "dp", "tensor"),
        P("tensor", "dp"),
        P("dp", "tensor"),
        P("tensor", "dp"),
        P(None, "dp"),
        P(None, ("tensor", "dp")),
        P(("tensor", "dp")),
        P(None, "dp", "tensor"),
        P("tensor", "dp"),
        P("dp", "tensor"),
        P("tensor", "dp"),
        P(None, "dp"),
        P(None, ("tensor", "dp")),
        P(("tensor", "dp")),
        P(None, "dp", "tensor"),
        P("tensor", "dp"),
        P("dp", "tensor"),
        P("tensor", "dp"),
        P(None, "dp", "tensor"),
        P("tensor", "dp"),
        P("dp", "tensor"),
        P("tensor", "dp"),
        P(None, "dp"),
        P(None, ("tensor", "dp")),
        P(("tensor", "dp")),
        P(None, "dp", "tensor"),
        P("tensor", "dp"),
        P("dp", "tensor"),
        P("tensor", "dp"),
        P(None, "dp"),
        P(None, ("tensor", "dp")),
        P(("tensor", "dp")),
    )
    pods = mesh.shape["dp"] == 8 and mesh.shape["tensor"] == 4
    chosen = body_pods if pods else body
    return jax.shard_map(chosen, mesh=mesh, in_specs=in_specs, out_specs=out_specs, check_vma=False)
```
